128 devices in a mesh: wide: 8 (over x, core), narrow: 16 (over z, y).
Axes of the slice: x: 4, y: 4, z: 4, core: 2. Of those that a mesh axis runs over, the one named last changes fastest.
Arguments:
- coarse_state: float32 [1024, 5, 16, 256], P(('wide', 'narrow')), as said below
- fine_state: float32 [1024, 5, 16, 256], P(('wide', 'narrow')), as said below
- fine_parent: int32 [128], replicated, may hold values from -1 to 1023, as said below
Outputs:
- coarse_next: float32 [1024, 5, 16, 256], P(('wide', 'narrow'))
- fine_next: float32 [1024, 5, 16, 256], P(('wide', 'narrow'))
The draws below stay inside these ranges and needn't reach their ends.
Inputs may be any that keep to these rules, and one draw needn't show every extreme that they name: `coarse_state`: coarse and fine states hold density 1 to 2, velocity components within -0.25 to 0.25 and pressure 1 to 2, stored as density, momenta and total energy with ratio of specific heats 1.4. `fine_state`: same law as coarse_state; rows of devices without children are ignored. `fine_parent`: exactly 96 entries are not -1; they are distinct coarse blocks.
All inputs are finite; a program needn't handle non-finite values.
Results may differ from the reference program's by a relative error of at most 0.0003.
Values sent between devices are 32-bit elements; how exact they have to be, the bound alone decides.
No kernel may reach another device: no remote copies, remote signals or barrier semaphores. Data moves between devices by JAX's collectives and lax.ppermute only.
A program may use at most 128 MiB of HBM per device.

```python
import jax
import jax.numpy as jnp
import numpy as np
from jax import lax

CELLS = 16
CB_DEV = 8
COARSE = 1024
FAMILIES = 96
FSLOTS = 1024


GAMMA = 1.4


def euler_cells(key, leading):
    subkeys = jax.random.split(key, 6)
    dims_out = (leading, CELLS, CELLS * CELLS)
    density = jnp.exp(jax.random.uniform(subkeys[0], dims_out, minval=0.0, maxval=0.6931))
    velocity_x = jax.random.uniform(subkeys[1], dims_out, minval=-0.25, maxval=0.25)
    velocity_y = jax.random.uniform(subkeys[2], dims_out, minval=-0.25, maxval=0.25)
    velocity_z = jax.random.uniform(subkeys[3], dims_out, minval=-0.25, maxval=0.25)
    pressure = jnp.exp(jax.random.uniform(subkeys[4], dims_out, minval=0.0, maxval=0.6931))
    kinetic = 0.5 * density * (velocity_x * velocity_x + velocity_y * velocity_y + velocity_z * velocity_z)
    energy = pressure / (GAMMA - 1.0) + kinetic
    return jnp.stack([density, density * velocity_x, density * velocity_y, density * velocity_z, energy], axis=1).astype(jnp.float32)


def draw_coarse_state(key, part):
    return euler_cells(jax.random.fold_in(key, 11), COARSE)


def draw_fine_state(key, part):
    return euler_cells(jax.random.fold_in(key, 23), FSLOTS)


def draw_fine_parent(key, part):
    subkeys = jax.random.split(jax.random.fold_in(key, 37), 4)
    device_total = FSLOTS // 8
    half_devices = device_total // 2
    first_device = jax.random.randint(subkeys[0], (), 0, half_devices).astype(jnp.int32)
    paired_device = first_device + half_devices
    first_block = (paired_device * CB_DEV + jax.random.randint(subkeys[1], (), 0, CB_DEV)).astype(jnp.int32)
    paired_block = jnp.bitwise_xor(first_block, 1)
    device_order = jax.random.permutation(subkeys[2], device_total).astype(jnp.int32)
    device_forced = ((device_order == first_device) | (device_order == paired_device)).astype(jnp.int32)
    device_order = device_order[jnp.argsort(device_forced, stable=True)]
    block_order = jax.random.permutation(subkeys[3], COARSE).astype(jnp.int32)
    block_forced = ((block_order == first_block) | (block_order == paired_block)).astype(jnp.int32)
    block_order = block_order[jnp.argsort(block_forced, stable=True)]
    result = jnp.full((device_total,), -1, jnp.int32)
    result = result.at[device_order[:FAMILIES - 2]].set(block_order[:FAMILIES - 2])
    result = result.at[first_device].set(first_block).at[paired_device].set(paired_block)
    return result


def setup_inputs(seed: int = 0) -> dict:
    key_of = jax.random.split(jax.random.key(seed), 4)
    return {
        "coarse_state": draw_coarse_state(jax.random.fold_in(key_of[3], 71), 0),
        "fine_state": draw_fine_state(jax.random.fold_in(key_of[3], 71), 0),
        "fine_parent": draw_fine_parent(jax.random.fold_in(key_of[3], 71), 0),
    }


GAMMA = 1.4
LAMBDA_STEP = 0.08


def morton_table(total_blocks):
    bit_count = total_blocks.bit_length() - 1
    numbers = np.arange(total_blocks, dtype=jnp.int32)
    coded = np.zeros((total_blocks, 3), dtype=jnp.int32)
    extent = [1, 1, 1]
    for bit_level in range(bit_count):
        axis_id = bit_level % 3
        coded[:, axis_id] |= ((numbers >> bit_level) & 1) << (bit_level // 3)
        extent[axis_id] *= 2
    coords = coded.copy()
    moving = coded >> 1
    for bit_level in range(bit_count):
        coords = coords ^ moving
        moving = moving >> 1
    lookup = np.zeros(extent, dtype=jnp.int32)
    lookup[coords[:, 0], coords[:, 1], coords[:, 2]] = numbers
    neighbor_ids = np.zeros((total_blocks, 6), dtype=jnp.int32)
    for facing in range(6):
        moved_coords = coords.copy()
        axis_id = facing // 2
        step_size = 1 if facing % 2 else -1
        moved_coords[:, axis_id] = (moved_coords[:, axis_id] + step_size) % extent[axis_id]
        neighbor_ids[:, facing] = lookup[moved_coords[:, 0], moved_coords[:, 1], moved_coords[:, 2]]
    return neighbor_ids


def flux_along(values, axis_id):
    density = values[0]
    momenta = values[1:4]
    energy = values[4]
    velocity = momenta[axis_id] / density
    squares = momenta[0] * momenta[0] + momenta[1] * momenta[1] + momenta[2] * momenta[2]
    pressure = (GAMMA - 1.0) * (energy - 0.5 * squares / density)
    components = [momenta[axis_id]]
    for component in range(3):
        momentum_flux = momenta[component] * velocity
        if component == axis_id:
            momentum_flux = momentum_flux + pressure
        components.append(momentum_flux)
    components.append((energy + pressure) * velocity)
    return jnp.stack(components)


def face_layer(block_values, facing, edge_cells):
    axis_id = facing // 2
    position = edge_cells - 1 if facing % 2 else 0
    leading = block_values.shape[0]
    if axis_id == 0:
        return block_values[:, position, :]
    cube_view = block_values.reshape(leading, edge_cells, edge_cells, edge_cells)
    if axis_id == 1:
        return cube_view[:, :, position, :].reshape(leading, edge_cells * edge_cells)
    return cube_view[:, :, :, position].reshape(leading, edge_cells * edge_cells)


def block_layers(block_values, edge_cells):
    return jnp.stack([face_layer(block_values, facing, edge_cells) for facing in range(6)])


def shifted(block_values, axis_id, ghost_layer, upward, edge_cells):
    leading = block_values.shape[0]
    if axis_id == 0:
        layer_view = ghost_layer[:, None, :]
        if upward:
            return jnp.concatenate([block_values[:, 1:], layer_view], axis=1)
        return jnp.concatenate([layer_view, block_values[:, :-1]], axis=1)
    sheet_view = ghost_layer.reshape(leading, edge_cells, edge_cells)
    if axis_id == 1:
        if upward:
            return jnp.concatenate([block_values[:, :, edge_cells:], sheet_view], axis=2)
        return jnp.concatenate([sheet_view, block_values[:, :, :-edge_cells]], axis=2)
    spread = jnp.repeat(sheet_view, edge_cells, axis=2)
    within = jnp.arange(edge_cells * edge_cells) % edge_cells
    if upward:
        return jnp.where(within == edge_cells - 1, spread, jnp.roll(block_values, -1, axis=2))
    return jnp.where(within == 0, spread, jnp.roll(block_values, 1, axis=2))


def advance_block(block_values, ghosts, edge_cells):
    total_change = jnp.zeros_like(block_values)
    for axis_id in range(3):
        low_ghost = ghosts[2 * axis_id]
        high_ghost = ghosts[2 * axis_id + 1]
        flux_here = flux_along(block_values, axis_id)
        above_cells = shifted(block_values, axis_id, high_ghost, True, edge_cells)
        flux_above = shifted(flux_here, axis_id, flux_along(high_ghost, axis_id), True, edge_cells)
        middle = 0.5 * (block_values + above_cells) - 0.5 * LAMBDA_STEP * (flux_above - flux_here)
        face_flux = flux_along(middle, axis_id)
        first_layer = face_layer(block_values, 2 * axis_id, edge_cells)
        first_flux = face_layer(flux_here, 2 * axis_id, edge_cells)
        low_middle = 0.5 * (low_ghost + first_layer) - 0.5 * LAMBDA_STEP * (first_flux - flux_along(low_ghost, axis_id))
        face_below = shifted(face_flux, axis_id, flux_along(low_middle, axis_id), False, edge_cells)
        total_change = total_change + (face_flux - face_below)
    return block_values - LAMBDA_STEP * total_change


def side_members(facing):
    axis_id = facing // 2
    wanted = facing % 2
    return [child_id for child_id in range(8) if (child_id >> axis_id) & 1 == wanted]


def pack_side(family_layers, facing):
    return jnp.stack([family_layers[child_id, facing] for child_id in side_members(facing)])


def injected(rim_face, child_id, axis_id, edge_cells):
    half_cells = edge_cells // 2
    leading = rim_face.shape[0]
    across = [other for other in range(3) if other != axis_id]
    first_bit = (child_id >> across[0]) & 1
    second_bit = (child_id >> across[1]) & 1
    sheet_view = rim_face.reshape(leading, edge_cells, edge_cells)
    sheet_view = sheet_view[:, first_bit * half_cells:(first_bit + 1) * half_cells, second_bit * half_cells:(second_bit + 1) * half_cells]
    widened = jnp.repeat(jnp.repeat(sheet_view, 2, axis=1), 2, axis=2)
    return widened.reshape(leading, edge_cells * edge_cells)


def family_ghosts(family_layers, far_sides, has_far, rim_faces, edge_cells):
    child_rows = []
    for child_id in range(8):
        ghost_list = []
        for facing in range(6):
            axis_id = facing // 2
            wanted = facing % 2
            bit_value = (child_id >> axis_id) & 1
            if bit_value != wanted:
                ghost_list.append(family_layers[child_id ^ (1 << axis_id), facing ^ 1])
            else:
                order_rank = side_members(facing).index(child_id)
                coarse_part = injected(rim_faces[facing], child_id, axis_id, edge_cells)
                ghost_list.append(jnp.where(has_far[facing], far_sides[facing, order_rank], coarse_part))
        child_rows.append(jnp.stack(ghost_list))
    return jnp.stack(child_rows)


def restricted(family, edge_cells):
    half_cells = edge_cells // 2
    leading = family.shape[1]
    parent = jnp.zeros((leading, edge_cells, edge_cells, edge_cells), family.dtype)
    for child_id in range(8):
        cube_view = family[child_id].reshape(leading, half_cells, 2, half_cells, 2, half_cells, 2)
        mean_cells = jnp.sum(cube_view, axis=(2, 4, 6)) * 0.125
        bit_x = child_id & 1
        bit_y = (child_id >> 1) & 1
        bit_z = (child_id >> 2) & 1
        parent = parent.at[:, bit_x * half_cells:(bit_x + 1) * half_cells, bit_y * half_cells:(bit_y + 1) * half_cells, bit_z * half_cells:(bit_z + 1) * half_cells].set(mean_cells)
    return parent.reshape(leading, edge_cells, edge_cells * edge_cells)


def reference(coarse_state, fine_state, fine_parent):
    total_blocks = coarse_state.shape[0]
    variables = coarse_state.shape[1]
    edge_cells = coarse_state.shape[2]
    devices = fine_parent.shape[0]
    neighbor_ids = jnp.asarray(morton_table(total_blocks))
    opposite = jnp.asarray(np.array([[1, 0, 3, 2, 5, 4]], dtype=jnp.int32))

    def ghosts_of(states):
        layers = jax.vmap(lambda one_block: block_layers(one_block, edge_cells))(states)
        return layers[neighbor_ids, opposite]

    ghosts_old = ghosts_of(coarse_state)
    coarse_new = lax.map(lambda paired: advance_block(paired[0], paired[1], edge_cells), (coarse_state, ghosts_old))
    ghosts_new = ghosts_of(coarse_new)
    family_live = fine_parent >= 0
    parent_safe = jnp.maximum(fine_parent, 0)
    device_ids = jnp.arange(devices, dtype=jnp.int32)
    family_of = jnp.full((total_blocks,), -1, jnp.int32).at[parent_safe].max(jnp.where(family_live, device_ids, -1))
    near_family = jnp.where(family_live[:, None], family_of[neighbor_ids[parent_safe]], -1)
    rim_old = ghosts_old[parent_safe]
    rim_mid = 0.5 * (rim_old + ghosts_new[parent_safe])
    families = fine_state.reshape(devices, 8, variables, edge_cells, edge_cells * edge_cells)

    def substep(current, rims):
        all_layers = jax.vmap(jax.vmap(lambda one_block: block_layers(one_block, edge_cells)))(current)

        def one_family(packed):
            family, near_row, rim_row, device_index = packed
            far_sides = jnp.stack([pack_side(all_layers[jnp.maximum(near_row[facing], 0)], facing ^ 1) for facing in range(6)])
            ghosts = family_ghosts(all_layers[device_index], far_sides, near_row >= 0, rim_row, edge_cells)
            return jax.vmap(lambda one_block, one_ghost: advance_block(one_block, one_ghost, edge_cells))(family, ghosts)

        return lax.map(one_family, (current, near_family, rims, device_ids))

    middle_state = substep(families, rim_old)
    final_state = substep(middle_state, rim_mid)
    fine_next = jnp.where(family_live[:, None, None, None, None], final_state, 0.0).reshape(fine_state.shape)
    averages = jax.vmap(lambda family: restricted(family, edge_cells))(final_state)
    coarse_next = coarse_new.at[jnp.where(family_live, fine_parent, total_blocks)].set(averages, mode="drop")
    return coarse_next, fine_next
```

```python
import functools

import jax
import jax.numpy as jnp
import numpy as np
from jax import lax
from jax.experimental import pallas as pl
from jax.experimental.pallas import tpu as pltpu
from jax.sharding import PartitionSpec as P

GAMMA = 1.4
LAMBDA_STEP = 0.08
AXES = ("wide", "narrow")
VARS = 5
SLOTS = 20
VMEM_BYTES = 56 * 1024 * 1024


def lanes_of(shape=(8, 128)):
    return lax.broadcasted_iota(jnp.int32, shape, 1)


def rows_of(shape=(8, 128)):
    return lax.broadcasted_iota(jnp.int32, shape, 0)


def others(axis_id):
    return [other for other in range(3) if other != axis_id]


def cube_block(axis_id, bit, t):
    first, second = others(axis_id)
    return (bit << axis_id) | ((t & 1) << first) | ((t >> 1) << second)


def rolled(values, shift, axis=1):
    shift %= values.shape[axis]
    return pltpu.roll(values, shift, axis) if shift else values


def pack_side(state, pack, pack_row, var, axis_id, high, bit):
    lanes = lanes_of()
    if axis_id == 0:
        row = 15 if high else 0
        for t in range(4):
            for half in range(2):
                tile = state[cube_block(0, bit, t) * 2 + half, var, row : row + 1, :]
                pack[pack_row, t * 2 + half : t * 2 + half + 1, :] = tile
        return
    total = jnp.zeros((8, 128), jnp.float32)
    if axis_id == 1:
        offset = 112 if high else 0
        for t in range(4):
            for part in range(2):
                group = t * 2 + part
                tile = state[cube_block(1, bit, t) * 2 + high, var, part * 8 : part * 8 + 8, :]
                total = jnp.where(lanes >> 4 == group, rolled(tile, group * 16 - offset), total)
    else:
        offset = 15 if high else 0
        for t in range(4):
            for part in range(2):
                for half in range(2):
                    place = t * 4 + part * 2 + half
                    tile = state[cube_block(2, bit, t) * 2 + half, var, part * 8 : part * 8 + 8, :]
                    total = jnp.where(lanes & 15 == place, rolled(tile, place - offset), total)
    pack[pack_row] = total


def unpack_side(tile, target, slot, var, axis_id, last):
    if axis_id == 0:
        row = 15 if last else 0
        for t in range(4):
            for half in range(2):
                target[slot + t * 2 + half, var, row : row + 1, :] = tile[t * 2 + half : t * 2 + half + 1, :]
    elif axis_id == 1:
        offset = 112 if last else 0
        for t in range(4):
            for part in range(2):
                target[slot + t, var, part * 8 : part * 8 + 8, :] = rolled(tile, offset - (t * 2 + part) * 16)
    else:
        offset = 15 if last else 0
        for t in range(4):
            for part in range(2):
                for half in range(2):
                    place = t * 4 + part * 2 + half
                    target[slot + t * 2 + half, var, part * 8 : part * 8 + 8, :] = rolled(tile, offset - place)


def take(tile, index, axis):
    return jnp.take_along_axis(tile, index, axis=axis, mode="promise_in_bounds")


def inject(tile, axis_id, t):
    lanes, rows = lanes_of(), rows_of()
    if axis_id == 0:
        row_index = 2 * t + (rows >> 1 & 1)
        lane_index = (4 * (rows & 1) + (lanes >> 5)) * 16 + 8 * (rows >> 2 & 1) + (lanes >> 1 & 7)
        return take(take(tile, row_index, 0), lane_index, 1)
    if axis_id == 1:
        part = lanes >> 4 & 1
        lane_index = (2 * t + (lanes >> 5 & 1)) * 16 + 8 * (lanes >> 6 & 1) + (lanes >> 1 & 7)
    else:
        part = lanes >> 1 & 1
        lane_index = (4 * (lanes & 1) + (lanes >> 5)) * 16 + 4 * t + 2 * (lanes >> 2 & 1) + (lanes >> 3 & 1)
    low = take(take(tile, rows >> 1, 0), lane_index, 1)
    high = take(take(tile, 4 + (rows >> 1), 0), lane_index, 1)
    return jnp.where(part == 1, high, low)


GHOST = (16, 24, 28)
STATE_TILES = 36
FLUX_TILES = 24


def primitives(values):
    inverse = 1.0 / values[0]
    squares = values[1] * values[1] + values[2] * values[2] + values[3] * values[3]
    pressure = (GAMMA - 1.0) * (values[4] - 0.5 * squares * inverse)
    return inverse, pressure


def flux_of(values, prims, axis_id):
    inverse, pressure = prims
    velocity = values[1 + axis_id] * inverse
    result = [values[1 + axis_id]]
    for component in range(3):
        term = values[1 + component] * velocity
        result.append(term + pressure if component == axis_id else term)
    result.append((values[4] + pressure) * velocity)
    return result


def face_flux(low, low_flux, high, axis_id):
    high_flux = flux_of(high, primitives(high), axis_id)
    middle = [
        0.5 * (low[v] + high[v]) - 0.5 * LAMBDA_STEP * (high_flux[v] - low_flux[v]) for v in range(VARS)
    ]
    return flux_of(middle, primitives(middle), axis_id)


def shift_up(tile, beyond, axis_id):
    lanes, rows = lanes_of((16, 128)), rows_of((16, 128))
    if axis_id == 0:
        return jnp.where(rows == 15, beyond[0:1, :], rolled(tile, -1, 0))
    if axis_id == 1:
        return jnp.where(lanes >= 112, rolled(beyond, -16), rolled(tile, -16))
    return jnp.where(lanes & 15 == 15, rolled(beyond, 15), rolled(tile, -1))


def shift_down(tile, before, axis_id):
    lanes, rows = lanes_of((16, 128)), rows_of((16, 128))
    if axis_id == 0:
        return jnp.where(rows == 0, before[15:16, :], rolled(tile, 1, 0))
    if axis_id == 1:
        return jnp.where(lanes < 16, rolled(before, 16), rolled(tile, 16))
    return jnp.where(lanes & 15 == 0, rolled(before, -15), rolled(tile, 1))


def advance_cube(state, fluxes, own_pack, ghost_pack, emit):
    for axis_id in range(3):
        for var in range(VARS):
            pack_side(state, own_pack, var, var, axis_id, 0, 0)
        inner = [own_pack[var] for var in range(VARS)]
        outer = [ghost_pack[2 * axis_id * VARS + var] for var in range(VARS)]
        low = face_flux(outer, flux_of(outer, primitives(outer), axis_id), inner, axis_id)
        for var in range(VARS):
            unpack_side(low[var], fluxes.at[axis_id], 16, var, axis_id, True)
            unpack_side(ghost_pack[(2 * axis_id + 1) * VARS + var], state, GHOST[axis_id], var, axis_id, False)

    def half_block(number, carry):
        block, half = number >> 1, number & 1
        bits = [block >> axis_id & 1 for axis_id in range(3)]
        pick = jnp.where
        following = [
            pick(bits[0] == 0, number + 2, GHOST[0] + (bits[1] + 2 * bits[2]) * 2 + half),
            pick(
                half == 0,
                number + 1,
                pick(bits[1] == 0, number + 3, GHOST[1] + bits[0] + 2 * bits[2]),
            ),
            pick(bits[2] == 0, number + 8, GHOST[2] + (bits[0] + 2 * bits[1]) * 2 + half),
        ]
        previous = [
            pick(bits[0] == 1, number - 2, 16 + (bits[1] + 2 * bits[2]) * 2 + half),
            pick(half == 1, number - 1, pick(bits[1] == 1, number - 3, 16 + bits[0] + 2 * bits[2])),
            pick(bits[2] == 1, number - 8, 16 + (bits[0] + 2 * bits[1]) * 2 + half),
        ]
        here = [state[number, var] for var in range(VARS)]
        prims = primitives(here)
        change = [None] * VARS
        for axis_id in range(3):
            above = [
                shift_up(here[var], state[following[axis_id], var], axis_id) for var in range(VARS)
            ]
            face = face_flux(here, flux_of(here, prims, axis_id), above, axis_id)
            for var in range(VARS):
                fluxes[axis_id, number, var] = face[var]
                below = shift_down(face[var], fluxes[axis_id, previous[axis_id], var], axis_id)
                term = face[var] - below
                change[var] = term if axis_id == 0 else change[var] + term
        emit(number, [here[var] - LAMBDA_STEP * change[var] for var in range(VARS)])
        return carry

    lax.fori_loop(0, 16, half_block, 0)


def load_state(source, state, flip):
    def one(block, carry):
        for var in range(VARS):
            for half in range(2):
                state[block * 2 + half, var] = source[block ^ flip, var, :, half * 128 : half * 128 + 128]
        return carry

    lax.fori_loop(0, 8, one, 0)


def pack_all(state, pack, base, inner):
    def one(var, carry):
        for facing in range(6):
            high = facing % 2
            pack_side(state, pack, base + facing * VARS + var, var, facing // 2, high, high ^ inner)
        return carry

    lax.fori_loop(0, VARS, one, 0)


def spread_packs(pack, base, out, stride, kind):
    def one(number, carry):
        for pair in range(4):
            out[(number * 4 + pair) * stride + kind] = pack[base + number, pair * 2 : pair * 2 + 2, :]
        return carry

    lax.fori_loop(0, 30, one, 0)


def collect_packs(incoming, stride, kind, pack):
    def one(var, carry):
        for facing in range(6):
            for pair in range(4):
                chunk = ((facing ^ 1) * SLOTS + var * 4 + pair) * stride + kind
                pack[facing * VARS + var, pair * 2 : pair * 2 + 2, :] = incoming[chunk]
        return carry

    lax.fori_loop(0, VARS, one, 0)


def first_kernel(scalars, coarse, fine, out, state, pack):
    load_state(fine, state, 0)
    pack_all(state, pack, 0, 0)
    load_state(coarse, state, scalars[0])
    pack_all(state, pack, 30, 0)
    pack_all(state, pack, 60, 1)
    for kind in range(3):
        spread_packs(pack, kind * 30, out, 3, kind)


def select_kernel(index, incoming, out, *, count):
    def one(step, carry):
        for lane in range(8):
            number = step * 8 + lane
            out[number] = incoming[index[number]]
        return carry

    lax.fori_loop(0, count // 8, one, 0)


def place_kernel(parent, incoming, out):
    def one(number, carry):
        @pl.when(parent[number] >= 0)
        def _():
            out[parent[number]] = incoming[number]

        return carry

    lax.fori_loop(0, parent.shape[0], one, 0)


def choose_ghosts(scalars, pack, ghost):
    for facing in range(6):

        @pl.when(scalars[1 + facing] > 0)
        def _():
            for var in range(VARS):
                ghost[facing * VARS + var] = pack[facing * VARS + var]

        @pl.when(scalars[1 + facing] == 0)
        def _():
            for var in range(VARS):
                tile = pack[facing * VARS + var]
                ghost[facing * VARS + var] = inject(tile, facing // 2, scalars[7 + facing])


def middle_kernel(
    scalars, coarse, fine, incoming, coarse_new, fine_mid, rim, out, state, fluxes, pack, ghost, own
):
    flip = scalars[0]

    def run(source, flipped, target):
        load_state(source, state, flipped)
        new = fluxes.at[3]

        def emit(number, values):
            for var in range(VARS):
                new[number, var] = values[var]

        advance_cube(state, fluxes, own, ghost, emit)

        def store(block, carry):
            for var in range(VARS):
                for half in range(2):
                    target[block ^ flipped, var, :, half * 128 : half * 128 + 128] = new[block * 2 + half, var]
            return carry

        lax.fori_loop(0, 8, store, 0)

    collect_packs(incoming, 2, 1, ghost)
    run(coarse, flip, coarse_new)
    pack_all(fluxes.at[3], pack, 30, 0)
    pack_all(fluxes.at[3], pack, 60, 1)
    collect_packs(incoming, 2, 0, rim)
    choose_ghosts(scalars, rim, ghost)
    run(fine, 0, fine_mid)
    pack_all(fluxes.at[3], pack, 0, 0)
    for kind in range(3):
        spread_packs(pack, kind * 30, out, 3, kind)


def last_kernel(scalars, fine, rim, incoming, fine_next, out, state, fluxes, pack, ghost, own):
    lanes = lanes_of()
    collect_packs(incoming, 1, 0, pack)
    for facing in range(6):

        @pl.when(scalars[1 + facing] == 0)
        def _():
            for var in range(VARS):
                row = facing * VARS + var
                pack[row] = 0.5 * (rim[row] + pack[row])

    choose_ghosts(scalars, pack, ghost)
    load_state(fine, state, 0)
    new = fluxes.at[3]

    def emit(number, values):
        for var in range(VARS):
            new[number, var] = values[var]

    advance_cube(state, fluxes, own, ghost, emit)
    live = scalars[13] > 0

    def store(block, carry):
        for var in range(VARS):
            for half in range(2):
                tile = new[block * 2 + half, var]
                fine_next[block, var, :, half * 128 : half * 128 + 128] = jnp.where(live, tile, 0.0)
        return carry

    lax.fori_loop(0, 8, store, 0)

    source = (lanes >> 4 & 3) * 32 + (lanes & 7) * 2

    def means(var, carry):
        for part in range(2):
            for y_bit in range(2):
                total = jnp.zeros((8, 128), jnp.float32)
                for half in range(2):
                    for z_bit in range(2):
                        number = (part | y_bit << 1 | z_bit << 2) * 2 + half
                        tile = new[number, var, pl.ds(0, 8, 2), :] + new[number, var, pl.ds(1, 8, 2), :]
                        tile = tile + rolled(tile, -1)
                        tile = tile + rolled(tile, -16)
                        tile = take(tile, source, 1) * 0.125
                        wanted = (lanes >> 6 == half) & (lanes >> 3 & 1 == z_bit)
                        total = jnp.where(wanted, tile, total)
                pack[(var * 2 + part) * 2 + y_bit] = total
        return carry

    lax.fori_loop(0, VARS, means, 0)

    def one(number, carry):
        for pair in range(4):
            out[number * 4 + pair] = pack[number, pair * 2 : pair * 2 + 2, :]
        return carry

    lax.fori_loop(0, 20, one, 0)


def merge_kernel(home, coarse_new, incoming, out):
    out[...] = coarse_new[...]
    for block in range(8):

        @pl.when(home[block] >= 0)
        def _():
            def one(number, carry):
                for part in range(2):
                    for half in range(2):
                        for pair in range(4):
                            chunk = ((number * 2 + part) * 2 + half) * 4 + pair
                            row = part * 8 + pair * 2
                            out[block, number, row : row + 2, half * 128 : half * 128 + 128] = incoming[
                                chunk * 8 + block
                            ]
                return carry

            lax.fori_loop(0, VARS, one, 0)


def call(kernel, scalar_count, shapes, scratch, *operands):
    vmem = pl.BlockSpec(memory_space=pltpu.VMEM)
    smem = pl.BlockSpec(memory_space=pltpu.SMEM)
    outs = [jax.ShapeDtypeStruct(shape, jnp.float32) for shape in shapes]
    result = pl.pallas_call(
        kernel,
        out_shape=outs,
        in_specs=[smem] * scalar_count + [vmem] * (len(operands) - scalar_count),
        out_specs=[vmem] * len(outs),
        scratch_shapes=[pltpu.VMEM(shape, jnp.float32) for shape in scratch],
        compiler_params=pltpu.CompilerParams(vmem_limit_bytes=VMEM_BYTES),
    )(*operands)
    return result if len(outs) > 1 else result[0]


def decode(code, levels):
    coords = []
    for axis_id in range(3):
        gray = jnp.zeros_like(code)
        for level in range(axis_id, levels, 3):
            gray = gray | ((code >> level & 1) << level // 3)
        coord = gray
        for shift in range(1, levels):
            coord = coord ^ (gray >> shift)
        coords.append(coord)
    return coords


def encode(coords, levels):
    code = jnp.zeros_like(coords[0])
    for level in range(levels):
        coord = coords[level % 3]
        gray = coord ^ (coord >> 1)
        code = code | ((gray >> level // 3 & 1) << level)
    return code


def extents(levels):
    return [1 << len(range(axis_id, levels, 3)) for axis_id in range(3)]


def moved(coords, axis_id, step, levels):
    sizes = extents(levels)
    return [jnp.where(axis_id == k, (coords[k] + step) & (sizes[k] - 1), coords[k]) for k in range(3)]


def exchange(values):
    return lax.all_to_all(values, AXES, split_axis=0, concat_axis=0, tiled=True)


def shards(coarse_state, fine_state, fine_parent):
    devices = lax.axis_size(AXES)
    device_id = lax.axis_index(AXES).astype(jnp.int32)
    blocks_here = coarse_state.shape[0]
    levels = (blocks_here * devices).bit_length() - 1
    device_levels = levels - 3
    device_ids = jnp.arange(devices, dtype=jnp.int32)

    facing = jnp.minimum(device_id // SLOTS, 5)
    axis_id, high = facing // 2, facing % 2
    step = 1 - 2 * high
    parents = jnp.maximum(fine_parent, 0)
    beside = moved(decode(parents, levels), axis_id, step, levels)
    beside_id = encode(beside, levels)
    match = jnp.where(fine_parent[None, :] == beside_id[:, None], device_ids[None, :], -1)
    near = jnp.max(match, axis=1)
    along = jnp.where(axis_id == 0, beside[0], jnp.where(axis_id == 1, beside[1], beside[2]))
    inner = jnp.where((along & 1) == high, 0, 1)
    fine_index = jnp.where(near >= 0, near * 3, (beside_id >> 3) * 3 + 1 + inner)
    across = encode(moved(decode(device_ids, device_levels), axis_id, step, device_levels), device_levels)
    first_index = jnp.stack([fine_index, across * 3 + 1], axis=1).reshape(-1)

    own_parent = lax.dynamic_index_in_dim(fine_parent, device_id, keepdims=False)
    live = own_parent >= 0
    own_coords = decode(jnp.maximum(own_parent, 0), levels)
    sides = jnp.arange(6, dtype=jnp.int32)
    side_ids = encode(
        moved([jnp.broadcast_to(c, (6,)) for c in own_coords], sides // 2, 2 * (sides % 2) - 1, levels), levels
    )
    side_near = jnp.any(fine_parent[None, :] == side_ids[:, None], axis=1).astype(jnp.int32)
    low_bits = [c & 1 for c in own_coords]
    turns = jnp.stack(
        [
            low_bits[others(side // 2)[0]] + 2 * low_bits[others(side // 2)[1]]
            for side in range(6)
        ]
    )
    parities = [c & 1 for c in decode(device_id, device_levels)]
    flip = parities[0] | parities[1] << 1 | parities[2] << 2
    scalars = jnp.concatenate(
        [flip[None], side_near, turns, live.astype(jnp.int32)[None]]
    ).astype(jnp.int32)
    local_ids = device_id * blocks_here + jnp.arange(blocks_here, dtype=jnp.int32)
    home = jnp.max(
        jnp.where(fine_parent[None, :] == local_ids[:, None], device_ids[None, :], -1), axis=1
    )

    block_shape = coarse_state.shape
    state_tiles = (STATE_TILES, VARS, 16, 128)
    flux_tiles = (4, FLUX_TILES, VARS, 16, 128)
    packs = (30, 8, 128)

    outgoing = call(
        first_kernel, 1, [(devices * 3, 2, 128)], [state_tiles, (90, 8, 128)], scalars, coarse_state, fine_state
    )
    incoming = exchange(outgoing)
    selected = call(
        functools.partial(select_kernel, count=2 * devices), 1, [(devices * 2, 2, 128)], [], first_index, incoming
    )
    received = exchange(selected)
    coarse_new, fine_mid, rim, outgoing = call(
        middle_kernel,
        1,
        [block_shape, block_shape, packs, (devices * 3, 2, 128)],
        [state_tiles, flux_tiles, (90, 8, 128), packs, (VARS, 8, 128)],
        scalars,
        coarse_state,
        fine_state,
        received,
    )
    incoming = exchange(outgoing)
    selected = call(
        functools.partial(select_kernel, count=devices), 1, [(devices, 2, 128)], [], fine_index, incoming
    )
    received = exchange(selected)
    fine_next, outgoing = call(
        last_kernel,
        1,
        [block_shape, (devices, 2, 128)],
        [state_tiles, flux_tiles, packs, packs, (VARS, 8, 128)],
        scalars,
        fine_mid,
        rim,
        received,
    )
    incoming = exchange(outgoing)
    placed = call(place_kernel, 1, [(devices * blocks_here, 2, 128)], [], fine_parent, incoming)
    received = exchange(placed)
    coarse_next = call(merge_kernel, 1, [block_shape], [], home, coarse_new, received)
    return coarse_next, fine_next


def solution(mesh):
    in_specs = (P(AXES, None, None, None), P(AXES, None, None, None), P())
    out_specs = (P(AXES, None, None, None), P(AXES, None, None, None))
    return jax.shard_map(shards, mesh=mesh, in_specs=in_specs, out_specs=out_specs, check_vma=False)
```

```python
import functools

import jax
import jax.numpy as jnp
import numpy as np
from jax import lax
from jax.experimental import pallas as pl
from jax.experimental.pallas import tpu as pltpu
from jax.sharding import PartitionSpec as P

GAMMA = 1.4
LAMBDA_STEP = 0.08
AXES = ("wide", "narrow")
VARS = 5
SLOTS = 20
VMEM_BYTES = 56 * 1024 * 1024


def lanes_of(shape=(8, 128)):
    return lax.broadcasted_iota(jnp.int32, shape, 1)


def rows_of(shape=(8, 128)):
    return lax.broadcasted_iota(jnp.int32, shape, 0)


def others(axis_id):
    return [other for other in range(3) if other != axis_id]


def cube_block(axis_id, bit, t):
    first, second = others(axis_id)
    return (bit << axis_id) | ((t & 1) << first) | ((t >> 1) << second)


def rolled(values, shift, axis=1):
    shift %= values.shape[axis]
    return pltpu.roll(values, shift, axis) if shift else values


def pack_side(cells, pack, pack_row, var, axis_id, high, bit):
    lanes = lanes_of()
    if axis_id == 0:
        row = 15 if high else 0
        for t in range(4):
            for half in range(2):
                tile = cells(cube_block(0, bit, t), half, var, row, 1)
                pack[pack_row, t * 2 + half : t * 2 + half + 1, :] = tile
        return
    total = jnp.zeros((8, 128), jnp.float32)
    if axis_id == 1:
        offset = 112 if high else 0
        for t in range(4):
            for part in range(2):
                group = t * 2 + part
                tile = cells(cube_block(1, bit, t), high, var, part * 8, 8)
                total = jnp.where(lanes >> 4 == group, rolled(tile, group * 16 - offset), total)
    else:
        offset = 15 if high else 0
        for t in range(4):
            for part in range(2):
                for half in range(2):
                    place = t * 4 + part * 2 + half
                    tile = cells(cube_block(2, bit, t), half, var, part * 8, 8)
                    total = jnp.where(lanes & 15 == place, rolled(tile, place - offset), total)
    pack[pack_row] = total


def take(tile, index, axis):
    return jnp.take_along_axis(tile, index, axis=axis, mode="promise_in_bounds")


def inject(tile, axis_id, t):
    lanes, rows = lanes_of(), rows_of()
    if axis_id == 0:
        row_index = 2 * t + (rows >> 1 & 1)
        lane_index = (4 * (rows & 1) + (lanes >> 5)) * 16 + 8 * (rows >> 2 & 1) + (lanes >> 1 & 7)
        return take(take(tile, row_index, 0), lane_index, 1)
    if axis_id == 1:
        part = lanes >> 4 & 1
        lane_index = (2 * t + (lanes >> 5 & 1)) * 16 + 8 * (lanes >> 6 & 1) + (lanes >> 1 & 7)
    else:
        part = lanes >> 1 & 1
        lane_index = (4 * (lanes & 1) + (lanes >> 5)) * 16 + 4 * t + 2 * (lanes >> 2 & 1) + (lanes >> 3 & 1)
    low = take(take(tile, rows >> 1, 0), lane_index, 1)
    high = take(take(tile, 4 + (rows >> 1), 0), lane_index, 1)
    return jnp.where(part == 1, high, low)


ROWS = 48


def primitives(values):
    inverse = 1.0 / values[0]
    squares = values[1] * values[1] + values[2] * values[2] + values[3] * values[3]
    pressure = (GAMMA - 1.0) * (values[4] - 0.5 * squares * inverse)
    return inverse, pressure


def flux_of(values, prims, axis_id):
    inverse, pressure = prims
    velocity = values[1 + axis_id] * inverse
    result = [values[1 + axis_id]]
    for component in range(3):
        term = values[1 + component] * velocity
        result.append(term + pressure if component == axis_id else term)
    result.append((values[4] + pressure) * velocity)
    return result


def face_flux(low, low_flux, high, axis_id):
    high_flux = flux_of(high, primitives(high), axis_id)
    middle = [
        0.5 * (low[v] + high[v]) - 0.5 * LAMBDA_STEP * (high_flux[v] - low_flux[v]) for v in range(VARS)
    ]
    return flux_of(middle, primitives(middle), axis_id)


def column(block, half):
    return (block >> 1) * 2 + half


def cells_of(columns):
    def cells(block, half, var, start, size):
        row = 8 + (block & 1) * 16 + start
        return columns[column(block, half), var, row : row + size, :]

    return cells


def cells_in(blocks, flip):
    def cells(block, half, var, start, size):
        return blocks[block ^ flip, var, start : start + size, half * 128 : half * 128 + 128]

    return cells


def parts_of(tile, shifts):
    return jnp.concatenate([rolled(tile, shift) for shift in shifts], axis=0)


def advance_cube(source, flip, columns, fluxes, passed, own_pack, ghost_pack, emit):
    lanes = lanes_of((16, 128))
    cells = cells_in(source, flip)
    ghost = [[ghost_pack[side * VARS + var] for var in range(VARS)] for side in range(6)]
    for block in range(8):
        row = 8 + (block & 1) * 16
        for half in range(2):
            for var in range(VARS):
                columns[column(block, half), var, row : row + 16, :] = cells(block, half, var, 0, 16)
    lows = []
    for axis_id in range(3):
        for var in range(VARS):
            pack_side(cells, own_pack, axis_id * VARS + var, var, axis_id, 0, 0)
        inner = [own_pack[axis_id * VARS + var] for var in range(VARS)]
        outer = ghost[2 * axis_id]
        lows.append(face_flux(outer, flux_of(outer, primitives(outer), axis_id), inner, axis_id))
    for number in range(8):
        for var in range(VARS):
            columns[number, var, 40:41, :] = ghost[1][var][number : number + 1, :]
            fluxes[number, var, 7:8, :] = lows[0][var][number : number + 1, :]

    def tiles(block, half):
        row = 8 + (block & 1) * 16
        return [columns[column(block, half), var, row : row + 16, :] for var in range(VARS)]

    for z_bit in range(2):
        for x_bit in range(2):
            t_y = x_bit + 2 * z_bit
            here = tiles(x_bit | z_bit << 2, 0)
            turned = [rolled(tile, -16) for tile in here]
            before = [
                parts_of(lows[1][var], [-(t_y * 2 + part) * 16 for part in range(2)]) for var in range(VARS)
            ]
            for y_bit in range(2):
                block = x_bit | y_bit << 1 | z_bit << 2
                t_z = x_bit + 2 * y_bit
                row = 8 + x_bit * 16
                for half in range(2):
                    spot = column(block, half)
                    if y_bit and half:
                        ahead = None
                        turned_ahead = [
                            parts_of(ghost[3][var], [112 - (t_y * 2 + part) * 16 for part in range(2)])
                            for var in range(VARS)
                        ]
                    else:
                        ahead = tiles(block, 1) if half == 0 else tiles(block | 2, 0)
                        turned_ahead = [rolled(tile, -16) for tile in ahead]
                    places = [t_z * 4 + part * 2 + half for part in range(2)]
                    if z_bit:
                        beyond = [
                            parts_of(ghost[5][var], [15 - place for place in places]) for var in range(VARS)
                        ]
                        behind = [passed[(x_bit * 2 + y_bit) * 2 + half, var] for var in range(VARS)]
                    else:
                        beyond = [rolled(tile, 15) for tile in tiles(block | 4, half)]
                        behind = [parts_of(lows[2][var], [-place for place in places]) for var in range(VARS)]
                    prims = primitives(here)

                    above = [columns[spot, var, row + 1 : row + 17, :] for var in range(VARS)]
                    face = face_flux(here, flux_of(here, prims, 0), above, 0)
                    change = []
                    for var in range(VARS):
                        fluxes[spot, var, row : row + 16, :] = face[var]
                        change.append(face[var] - fluxes[spot, var, row - 1 : row + 15, :])

                    above = [jnp.where(lanes >= 112, turned_ahead[v], turned[v]) for v in range(VARS)]
                    face = face_flux(here, flux_of(here, prims, 1), above, 1)
                    after = [rolled(face[var], 16) for var in range(VARS)]
                    for var in range(VARS):
                        change[var] += face[var] - jnp.where(lanes < 16, before[var], after[var])
                    before = after

                    above = [
                        jnp.where(lanes & 15 == 15, beyond[v], rolled(here[v], -1)) for v in range(VARS)
                    ]
                    face = face_flux(here, flux_of(here, prims, 2), above, 2)
                    for var in range(VARS):
                        down = jnp.where(lanes & 15 == 0, behind[var], rolled(face[var], 1))
                        change[var] += face[var] - down
                        if z_bit == 0:
                            passed[(x_bit * 2 + y_bit) * 2 + half, var] = rolled(face[var], -15)

                    emit(block, half, [here[v] - LAMBDA_STEP * change[v] for v in range(VARS)])
                    here, turned = ahead, turned_ahead


def pack_all(cells, pack, base, inner):
    def one(var, carry):
        for facing in range(6):
            high = facing % 2
            pack_side(cells, pack, base + facing * VARS + var, var, facing // 2, high, high ^ inner)
        return carry

    lax.fori_loop(0, VARS, one, 0)


def spread_packs(pack, base, out, stride, kind):
    def one(number, carry):
        for pair in range(4):
            out[(number * 4 + pair) * stride + kind] = pack[base + number, pair * 2 : pair * 2 + 2, :]
        return carry

    lax.fori_loop(0, 30, one, 0)


def collect_packs(incoming, stride, kind, pack):
    def one(var, carry):
        for facing in range(6):
            for pair in range(4):
                chunk = ((facing ^ 1) * SLOTS + var * 4 + pair) * stride + kind
                pack[facing * VARS + var, pair * 2 : pair * 2 + 2, :] = incoming[chunk]
        return carry

    lax.fori_loop(0, VARS, one, 0)


def flip_of(device_id):
    flip = 0
    for level in range(7):
        flip = flip ^ ((device_id >> level & 1) << level % 3)
    return flip


def first_kernel(scalars, coarse, fine, out, pack):
    pack_all(cells_in(fine, 0), pack, 0, 0)
    flip = flip_of(scalars[0])
    pack_all(cells_in(coarse, flip), pack, 30, 0)
    pack_all(cells_in(coarse, flip), pack, 60, 1)
    for kind in range(3):
        spread_packs(pack, kind * 30, out, 3, kind)


def select_kernel(index, incoming, out, *, count):
    def one(step, carry):
        for lane in range(8):
            number = step * 8 + lane
            out[number] = incoming[index[number]]
        return carry

    lax.fori_loop(0, count // 8, one, 0)


def place_kernel(target, incoming, out):
    def one(step, carry):
        for lane in range(8):
            number = step * 8 + lane
            out[target[number]] = incoming[number]
        return carry

    lax.fori_loop(0, target.shape[0] // 8, one, 0)


def choose_ghosts(scalars, pack, ghost):
    for facing in range(6):

        @pl.when(scalars[1 + facing] > 0)
        def _():
            for var in range(VARS):
                ghost[facing * VARS + var] = pack[facing * VARS + var]

        @pl.when(scalars[1 + facing] == 0)
        def _():
            for var in range(VARS):
                tile = pack[facing * VARS + var]
                ghost[facing * VARS + var] = inject(tile, facing // 2, scalars[7 + facing])


def middle_kernel(
    scalars, coarse, fine, incoming, coarse_new, fine_mid, rim, out, columns, fluxes, passed, pack, ghost, own
):
    flip = scalars[0]

    def run(source, flipped, target):
        def emit(block, half, values):
            for var in range(VARS):
                target[block ^ flipped, var, :, half * 128 : half * 128 + 128] = values[var]

        advance_cube(source, flipped, columns, fluxes, passed, own, ghost, emit)

    collect_packs(incoming, 2, 1, ghost)
    run(coarse, flip, coarse_new)
    pack_all(cells_in(coarse_new, flip), pack, 30, 0)
    pack_all(cells_in(coarse_new, flip), pack, 60, 1)
    collect_packs(incoming, 2, 0, rim)
    choose_ghosts(scalars, rim, ghost)
    run(fine, 0, fine_mid)
    pack_all(cells_in(fine_mid, 0), pack, 0, 0)
    for kind in range(3):
        spread_packs(pack, kind * 30, out, 3, kind)


def last_kernel(
    scalars, fine, rim, incoming, fine_next, out, columns, fluxes, passed, new, pack, ghost, own
):
    lanes = lanes_of()
    collect_packs(incoming, 1, 0, pack)
    for facing in range(6):

        @pl.when(scalars[1 + facing] == 0)
        def _():
            for var in range(VARS):
                row = facing * VARS + var
                pack[row] = 0.5 * (rim[row] + pack[row])

    choose_ghosts(scalars, pack, ghost)
    live = scalars[13] > 0

    def emit(block, half, values):
        for var in range(VARS):
            new[block * 2 + half, var] = values[var]
            fine_next[block, var, :, half * 128 : half * 128 + 128] = jnp.where(live, values[var], 0.0)

    advance_cube(fine, 0, columns, fluxes, passed, own, ghost, emit)

    source = (lanes >> 4 & 3) * 32 + (lanes & 7) * 2

    def means(var, carry):
        for part in range(2):
            for y_bit in range(2):
                total = jnp.zeros((8, 128), jnp.float32)
                for half in range(2):
                    for z_bit in range(2):
                        number = (part | y_bit << 1 | z_bit << 2) * 2 + half
                        tile = new[number, var, pl.ds(0, 8, 2), :] + new[number, var, pl.ds(1, 8, 2), :]
                        tile = tile + rolled(tile, -1)
                        tile = tile + rolled(tile, -16)
                        tile = take(tile, source, 1) * 0.125
                        wanted = (lanes >> 6 == half) & (lanes >> 3 & 1 == z_bit)
                        total = jnp.where(wanted, tile, total)
                pack[(var * 2 + part) * 2 + y_bit] = total
        return carry

    lax.fori_loop(0, VARS, means, 0)

    def one(number, carry):
        for pair in range(4):
            out[number * 4 + pair] = pack[number, pair * 2 : pair * 2 + 2, :]
        return carry

    lax.fori_loop(0, 20, one, 0)


def merge_kernel(home, coarse_new, incoming, out):
    out[...] = coarse_new[...]
    for block in range(8):

        @pl.when(home[block] >= 0)
        def _():
            def one(number, carry):
                for part in range(2):
                    for half in range(2):
                        for pair in range(4):
                            chunk = ((number * 2 + part) * 2 + half) * 4 + pair
                            row = part * 8 + pair * 2
                            out[block, number, row : row + 2, half * 128 : half * 128 + 128] = incoming[
                                chunk * 8 + block
                            ]
                return carry

            lax.fori_loop(0, VARS, one, 0)


def call(kernel, scalar_count, shapes, scratch, *operands):
    vmem = pl.BlockSpec(memory_space=pltpu.VMEM)
    smem = pl.BlockSpec(memory_space=pltpu.SMEM)
    outs = [jax.ShapeDtypeStruct(shape, jnp.float32) for shape in shapes]
    result = pl.pallas_call(
        kernel,
        out_shape=outs,
        in_specs=[smem] * scalar_count + [vmem] * (len(operands) - scalar_count),
        out_specs=[vmem] * len(outs),
        scratch_shapes=[pltpu.VMEM(shape, jnp.float32) for shape in scratch],
        compiler_params=pltpu.CompilerParams(vmem_limit_bytes=VMEM_BYTES),
    )(*operands)
    return result if len(outs) > 1 else result[0]


def decode(code, levels):
    coords = []
    for axis_id in range(3):
        gray = jnp.zeros_like(code)
        for level in range(axis_id, levels, 3):
            gray = gray | ((code >> level & 1) << level // 3)
        coord = gray
        for shift in range(1, levels):
            coord = coord ^ (gray >> shift)
        coords.append(coord)
    return coords


def encode(coords, levels):
    code = jnp.zeros_like(coords[0])
    for level in range(levels):
        coord = coords[level % 3]
        gray = coord ^ (coord >> 1)
        code = code | ((gray >> level // 3 & 1) << level)
    return code


def extents(levels):
    return [1 << len(range(axis_id, levels, 3)) for axis_id in range(3)]


def moved(coords, axis_id, step, levels):
    sizes = extents(levels)
    return [jnp.where(axis_id == k, (coords[k] + step) & (sizes[k] - 1), coords[k]) for k in range(3)]


def exchange(values):
    return lax.all_to_all(values, AXES, split_axis=0, concat_axis=0, tiled=True)


def shards(coarse_state, fine_state, fine_parent):
    devices = lax.axis_size(AXES)
    device_id = lax.axis_index(AXES).astype(jnp.int32)
    blocks_here = coarse_state.shape[0]
    levels = (blocks_here * devices).bit_length() - 1
    device_levels = levels - 3
    device_ids = jnp.arange(devices, dtype=jnp.int32)

    facing = jnp.minimum(device_id // SLOTS, 5)
    axis_id, high = facing // 2, facing % 2
    step = 1 - 2 * high
    parents = jnp.maximum(fine_parent, 0)
    beside = moved(decode(parents, levels), axis_id, step, levels)
    beside_id = encode(beside, levels)
    match = jnp.where(fine_parent[None, :] == beside_id[:, None], device_ids[None, :], -1)
    near = jnp.max(match, axis=1)
    along = jnp.where(axis_id == 0, beside[0], jnp.where(axis_id == 1, beside[1], beside[2]))
    inner = jnp.where((along & 1) == high, 0, 1)
    fine_index = jnp.where(near >= 0, near * 3, (beside_id >> 3) * 3 + 1 + inner)
    across = encode(moved(decode(device_ids, device_levels), axis_id, step, device_levels), device_levels)
    first_index = jnp.stack([fine_index, across * 3 + 1], axis=1).reshape(-1)

    own_parent = lax.dynamic_index_in_dim(fine_parent, device_id, keepdims=False)
    live = own_parent >= 0
    own_coords = decode(jnp.maximum(own_parent, 0), levels)
    sides = jnp.arange(6, dtype=jnp.int32)
    side_ids = encode(
        moved([jnp.broadcast_to(c, (6,)) for c in own_coords], sides // 2, 2 * (sides % 2) - 1, levels), levels
    )
    side_near = jnp.any(fine_parent[None, :] == side_ids[:, None], axis=1).astype(jnp.int32)
    low_bits = [c & 1 for c in own_coords]
    turns = jnp.stack(
        [
            low_bits[others(side // 2)[0]] + 2 * low_bits[others(side // 2)[1]]
            for side in range(6)
        ]
    )
    flip = flip_of(device_id)
    scalars = jnp.concatenate(
        [flip[None], side_near, turns, live.astype(jnp.int32)[None]]
    ).astype(jnp.int32)
    local_ids = device_id * blocks_here + jnp.arange(blocks_here, dtype=jnp.int32)
    home = jnp.max(
        jnp.where(fine_parent[None, :] == local_ids[:, None], device_ids[None, :], -1), axis=1
    )

    candidates = jnp.arange(2 * devices, dtype=jnp.int32)
    refined = jnp.any(fine_parent[None, :] == candidates[:, None], axis=1)
    unused = jnp.max(jnp.where(refined, -1, candidates))
    targets = jnp.where(fine_parent >= 0, fine_parent, unused)

    block_shape = coarse_state.shape
    columns = (8, VARS, ROWS, 128)
    passed = (8, VARS, 16, 128)
    packs = (30, 8, 128)
    own = (3 * VARS, 8, 128)

    outgoing = call(
        first_kernel, 1, [(devices * 3, 2, 128)], [(90, 8, 128)], device_id[None], coarse_state, fine_state
    )
    incoming = exchange(outgoing)
    selected = call(
        functools.partial(select_kernel, count=2 * devices), 1, [(devices * 2, 2, 128)], [], first_index, incoming
    )
    received = exchange(selected)
    coarse_new, fine_mid, rim, outgoing = call(
        middle_kernel,
        1,
        [block_shape, block_shape, packs, (devices * 3, 2, 128)],
        [columns, columns, passed, (90, 8, 128), packs, own],
        scalars,
        coarse_state,
        fine_state,
        received,
    )
    incoming = exchange(outgoing)
    selected = call(
        functools.partial(select_kernel, count=devices), 1, [(devices, 2, 128)], [], fine_index, incoming
    )
    received = exchange(selected)
    fine_next, outgoing = call(
        last_kernel,
        1,
        [block_shape, (devices, 2, 128)],
        [columns, columns, passed, (16, VARS, 16, 128), packs, packs, own],
        scalars,
        fine_mid,
        rim,
        received,
    )
    incoming = exchange(outgoing)
    placed = call(place_kernel, 1, [(devices * blocks_here, 2, 128)], [], targets, incoming)
    received = exchange(placed)
    coarse_next = call(merge_kernel, 1, [block_shape], [], home, coarse_new, received)
    return coarse_next, fine_next


def solution(mesh):
    in_specs = (P(AXES, None, None, None), P(AXES, None, None, None), P())
    out_specs = (P(AXES, None, None, None), P(AXES, None, None, None))
    return jax.shard_map(shards, mesh=mesh, in_specs=in_specs, out_specs=out_specs, check_vma=False)
```

```python
import functools

import jax
import jax.numpy as jnp
import numpy as np
from jax import lax
from jax.experimental import pallas as pl
from jax.experimental.pallas import tpu as pltpu
from jax.sharding import PartitionSpec as P

GAMMA = 1.4
LAMBDA_STEP = 0.08
AXES = ("wide", "narrow")
VARS = 5
SLOTS = 20
CHUNKS = 7
VMEM_BYTES = 56 * 1024 * 1024


def lanes_of(shape=(8, 128)):
    return lax.broadcasted_iota(jnp.int32, shape, 1)


def rows_of(shape=(8, 128)):
    return lax.broadcasted_iota(jnp.int32, shape, 0)


def others(axis_id):
    return [other for other in range(3) if other != axis_id]


def cube_block(axis_id, bit, t):
    first, second = others(axis_id)
    return (bit << axis_id) | ((t & 1) << first) | ((t >> 1) << second)


def rolled(values, shift, axis=1):
    shift %= values.shape[axis]
    return pltpu.roll(values, shift, axis) if shift else values


def sheet_cells(axis_id):
    row, lane = np.meshgrid(np.arange(8), np.arange(128), indexing="ij")
    if axis_id == 0:
        t, half = row >> 1, row & 1
        return (t & 1) * 16 + half * 8 + (lane >> 4), (t >> 1) * 16 + (lane & 15)
    if axis_id == 1:
        t, part = lane >> 5, lane >> 4 & 1
        return (t & 1) * 16 + part * 8 + row, (t >> 1) * 16 + (lane & 15)
    t, part, half = lane >> 2 & 3, lane >> 1 & 1, lane & 1
    return (t & 1) * 16 + part * 8 + row, (t >> 1) * 16 + half * 8 + (lane >> 4)


def sheet_tables():
    tables = np.zeros((3, 2, 2, 3, 8, 128), np.int32)
    for axis_id in range(3):
        cells = sheet_cells(axis_id)
        place = np.zeros((32, 32, 2), np.int32)
        for row in range(8):
            for lane in range(128):
                place[cells[0][row, lane], cells[1][row, lane]] = (row, lane)
        for lateral in range(2):
            for up in range(2):
                wanted = list(cells)
                wanted[lateral] = (wanted[lateral] + (1 if up else -1)) % 32
                source = place[wanted[0], wanted[1]]
                rows, lanes = source[..., 0], source[..., 1]
                table = tables[axis_id, lateral, up]
                table[1] = rows
                for lane in range(128):
                    table[0][rows[:, lane], lane] = lanes[:, lane]
                table[2] = cells[lateral] == (0 if up else 31)
    return tables


def pack_side(cells, pack, pack_row, var, axis_id, high, bit, depth=0):
    lanes = lanes_of()
    if axis_id == 0:
        row = 15 - depth if high else depth
        for t in range(4):
            for half in range(2):
                tile = cells(cube_block(0, bit, t), half, var, row, 1)
                pack[pack_row, t * 2 + half : t * 2 + half + 1, :] = tile
        return
    total = jnp.zeros((8, 128), jnp.float32)
    if axis_id == 1:
        offset = 112 - 16 * depth if high else 16 * depth
        for t in range(4):
            for part in range(2):
                group = t * 2 + part
                tile = cells(cube_block(1, bit, t), high, var, part * 8, 8)
                total = jnp.where(lanes >> 4 == group, rolled(tile, group * 16 - offset), total)
    else:
        offset = 15 - depth if high else depth
        for t in range(4):
            for part in range(2):
                for half in range(2):
                    place = t * 4 + part * 2 + half
                    tile = cells(cube_block(2, bit, t), half, var, part * 8, 8)
                    total = jnp.where(lanes & 15 == place, rolled(tile, place - offset), total)
    pack[pack_row] = total


def take(tile, index, axis):
    return jnp.take_along_axis(tile, index, axis=axis, mode="promise_in_bounds")


def inject(tile, axis_id, t):
    lanes, rows = lanes_of(), rows_of()
    if axis_id == 0:
        row_index = 2 * t + (rows >> 1 & 1)
        lane_index = (4 * (rows & 1) + (lanes >> 5)) * 16 + 8 * (rows >> 2 & 1) + (lanes >> 1 & 7)
        return take(take(tile, row_index, 0), lane_index, 1)
    if axis_id == 1:
        part = lanes >> 4 & 1
        lane_index = (2 * t + (lanes >> 5 & 1)) * 16 + 8 * (lanes >> 6 & 1) + (lanes >> 1 & 7)
    else:
        part = lanes >> 1 & 1
        lane_index = (4 * (lanes & 1) + (lanes >> 5)) * 16 + 4 * t + 2 * (lanes >> 2 & 1) + (lanes >> 3 & 1)
    low = take(take(tile, rows >> 1, 0), lane_index, 1)
    high = take(take(tile, 4 + (rows >> 1), 0), lane_index, 1)
    return jnp.where(part == 1, high, low)


ROWS = 48


def primitives(values):
    inverse = 1.0 / values[0]
    squares = values[1] * values[1] + values[2] * values[2] + values[3] * values[3]
    pressure = (GAMMA - 1.0) * (values[4] - 0.5 * squares * inverse)
    return inverse, pressure


def flux_of(values, prims, axis_id):
    inverse, pressure = prims
    velocity = values[1 + axis_id] * inverse
    result = [values[1 + axis_id]]
    for component in range(3):
        term = values[1 + component] * velocity
        result.append(term + pressure if component == axis_id else term)
    result.append((values[4] + pressure) * velocity)
    return result


def face_flux(low, low_flux, high, axis_id):
    high_flux = flux_of(high, primitives(high), axis_id)
    middle = [
        0.5 * (low[v] + high[v]) - 0.5 * LAMBDA_STEP * (high_flux[v] - low_flux[v]) for v in range(VARS)
    ]
    return flux_of(middle, primitives(middle), axis_id)


def column(block, half):
    return (block >> 1) * 2 + half


def cells_of(columns):
    def cells(block, half, var, start, size):
        row = 8 + (block & 1) * 16 + start
        return columns[column(block, half), var, row : row + size, :]

    return cells


def cells_in(blocks, flip):
    def cells(block, half, var, start, size):
        return blocks[block ^ flip, var, start : start + size, half * 128 : half * 128 + 128]

    return cells


def parts_of(tile, shifts):
    return jnp.concatenate([rolled(tile, shift) for shift in shifts], axis=0)


def advance_cube(source, flip, columns, fluxes, passed, own_pack, ghost_pack, emit):
    lanes = lanes_of((16, 128))
    cells = cells_in(source, flip)
    ghost = [[ghost_pack[side * VARS + var] for var in range(VARS)] for side in range(6)]
    for block in range(8):
        row = 8 + (block & 1) * 16
        for half in range(2):
            for var in range(VARS):
                columns[column(block, half), var, row : row + 16, :] = cells(block, half, var, 0, 16)
    lows = []
    for axis_id in range(3):
        for var in range(VARS):
            pack_side(cells, own_pack, axis_id * VARS + var, var, axis_id, 0, 0)
        inner = [own_pack[axis_id * VARS + var] for var in range(VARS)]
        outer = ghost[2 * axis_id]
        lows.append(face_flux(outer, flux_of(outer, primitives(outer), axis_id), inner, axis_id))
    for number in range(8):
        for var in range(VARS):
            columns[number, var, 40:41, :] = ghost[1][var][number : number + 1, :]
            fluxes[number, var, 7:8, :] = lows[0][var][number : number + 1, :]

    def tiles(block, half):
        row = 8 + (block & 1) * 16
        return [columns[column(block, half), var, row : row + 16, :] for var in range(VARS)]

    for z_bit in range(2):
        for x_bit in range(2):
            t_y = x_bit + 2 * z_bit
            here = tiles(x_bit | z_bit << 2, 0)
            turned = [rolled(tile, -16) for tile in here]
            before = [
                parts_of(lows[1][var], [-(t_y * 2 + part) * 16 for part in range(2)]) for var in range(VARS)
            ]
            for y_bit in range(2):
                block = x_bit | y_bit << 1 | z_bit << 2
                t_z = x_bit + 2 * y_bit
                row = 8 + x_bit * 16
                for half in range(2):
                    spot = column(block, half)
                    if y_bit and half:
                        ahead = None
                        turned_ahead = [
                            parts_of(ghost[3][var], [112 - (t_y * 2 + part) * 16 for part in range(2)])
                            for var in range(VARS)
                        ]
                    else:
                        ahead = tiles(block, 1) if half == 0 else tiles(block | 2, 0)
                        turned_ahead = [rolled(tile, -16) for tile in ahead]
                    places = [t_z * 4 + part * 2 + half for part in range(2)]
                    if z_bit:
                        beyond = [
                            parts_of(ghost[5][var], [15 - place for place in places]) for var in range(VARS)
                        ]
                        behind = [passed[(x_bit * 2 + y_bit) * 2 + half, var] for var in range(VARS)]
                    else:
                        beyond = [rolled(tile, 15) for tile in tiles(block | 4, half)]
                        behind = [parts_of(lows[2][var], [-place for place in places]) for var in range(VARS)]
                    prims = primitives(here)

                    above = [columns[spot, var, row + 1 : row + 17, :] for var in range(VARS)]
                    face = face_flux(here, flux_of(here, prims, 0), above, 0)
                    change = []
                    for var in range(VARS):
                        fluxes[spot, var, row : row + 16, :] = face[var]
                        change.append(face[var] - fluxes[spot, var, row - 1 : row + 15, :])

                    above = [jnp.where(lanes >= 112, turned_ahead[v], turned[v]) for v in range(VARS)]
                    face = face_flux(here, flux_of(here, prims, 1), above, 1)
                    after = [rolled(face[var], 16) for var in range(VARS)]
                    for var in range(VARS):
                        change[var] += face[var] - jnp.where(lanes < 16, before[var], after[var])
                    before = after

                    above = [
                        jnp.where(lanes & 15 == 15, beyond[v], rolled(here[v], -1)) for v in range(VARS)
                    ]
                    face = face_flux(here, flux_of(here, prims, 2), above, 2)
                    for var in range(VARS):
                        down = jnp.where(lanes & 15 == 0, behind[var], rolled(face[var], 1))
                        change[var] += face[var] - down
                        if z_bit == 0:
                            passed[(x_bit * 2 + y_bit) * 2 + half, var] = rolled(face[var], -15)

                    emit(block, half, [here[v] - LAMBDA_STEP * change[v] for v in range(VARS)])
                    here, turned = ahead, turned_ahead


def pack_all(cells, pack, base, inner, depth=0):
    def one(var, carry):
        for facing in range(6):
            high = facing % 2
            pack_side(cells, pack, base + facing * VARS + var, var, facing // 2, high, high ^ inner, depth)
        return carry

    lax.fori_loop(0, VARS, one, 0)


def spread_packs(pack, base, out, stride, kind):
    def one(number, carry):
        for pair in range(4):
            out[(number * 4 + pair) * stride + kind] = pack[base + number, pair * 2 : pair * 2 + 2, :]
        return carry

    lax.fori_loop(0, 30, one, 0)


def collect_packs(incoming, stride, kind, pack, turned=1):
    def one(var, carry):
        for facing in range(6):
            for pair in range(4):
                chunk = ((facing ^ turned) * SLOTS + var * 4 + pair) * stride + kind
                pack[facing * VARS + var, pair * 2 : pair * 2 + 2, :] = incoming[chunk]
        return carry

    lax.fori_loop(0, VARS, one, 0)


def flip_of(device_id):
    flip = 0
    for level in range(7):
        flip = flip ^ ((device_id >> level & 1) << level % 3)
    return flip


def first_kernel(scalars, coarse, fine, out, pack):
    flip = flip_of(scalars[0])
    for depth in range(2):
        pack_all(cells_in(fine, 0), pack, depth * 30, 0, depth)
        for inner in range(2):
            pack_all(cells_in(coarse, flip), pack, (2 + 2 * inner + depth) * 30, inner, depth)
    for kind in range(6):
        spread_packs(pack, kind * 30, out, 6, kind)


def select_kernel(index, incoming, masks, out):
    up = [masks[lateral] > 0 for lateral in range(2)]

    def one(step, carry):
        results = []
        for lane in range(4):
            number = step * 4 + lane
            rows = [incoming[index[number * 9 + column]] for column in range(9)]
            strips = [jnp.where(up[j], rows[4 + 2 * j], rows[3 + 2 * j]) for j in range(2)]
            results.append(rows[:3] + strips + rows[7:])
        for lane in range(4):
            for kind in range(CHUNKS):
                out[(step * 4 + lane) * CHUNKS + kind] = results[lane][kind]
        return carry

    lax.fori_loop(0, out.shape[0] // (4 * CHUNKS), one, 0)


def place_kernel(target, incoming, out):
    def one(step, carry):
        for lane in range(8):
            number = step * 8 + lane
            out[target[number]] = incoming[number]
        return carry

    lax.fori_loop(0, target.shape[0] // 8, one, 0)


def coarse_kernel(scalars, coarse, incoming, coarse_new, columns, fluxes, passed, ghost, own):
    flip = scalars[0]

    def emit(block, half, values):
        for var in range(VARS):
            coarse_new[block ^ flip, var, :, half * 128 : half * 128 + 128] = values[var]

    collect_packs(incoming, CHUNKS, 5, ghost)
    advance_cube(coarse, flip, columns, fluxes, passed, own, ghost, emit)


def sheet_step(facing, here, below, deeper, laterals):
    axis_id = facing // 2
    prims = primitives(here)
    change = [None] * VARS
    pairs = {axis_id: (below, deeper) if facing % 2 else (deeper, below)}
    for lateral, other in enumerate(others(axis_id)):
        pairs[other] = laterals[lateral]
    for along in range(3):
        down, up = pairs[along]
        upper = face_flux(here, flux_of(here, prims, along), up, along)
        lower = face_flux(down, flux_of(down, primitives(down), along), here, along)
        for var in range(VARS):
            term = upper[var] - lower[var]
            change[var] = term if along == 0 else change[var] + term
    return [here[var] - LAMBDA_STEP * change[var] for var in range(VARS)]


def family_ghosts(scalars, fine, tables, packs, old, mid, own):
    coarse_layer, other_layer, second_layer, strip_a, strip_b, parent_layer = packs
    strips = (strip_a, strip_b)
    for facing in range(6):
        axis_id, high = facing // 2, facing % 2
        rows = [facing * VARS + var for var in range(VARS)]
        turn = scalars[7 + facing]

        def moved_sheet(tile, strip, lateral, up):
            tile = jnp.where(tables[axis_id, lateral, up, 2] > 0, strip, tile)
            tile = take(tile, tables[axis_id, lateral, up, 0], 1)
            return take(tile, tables[axis_id, lateral, up, 1], 0)

        @pl.when(scalars[1 + facing] > 0)
        def _():
            for var in range(VARS):
                pack_side(cells_in(fine, 0), own, var, var, axis_id, high, high)
            here = [other_layer[row] for row in rows]
            laterals = []
            for lateral in range(2):
                pair = []
                for up in range(2):
                    known = scalars[14 + facing * 4 + lateral * 2 + up] > 0
                    edge = (tables[axis_id, lateral, 1 - up, 2] > 0) & jnp.logical_not(known)
                    values = []
                    for row in rows:
                        strip = strips[lateral][row]
                        coarse = moved_sheet(coarse_layer[row], strip, lateral, up)
                        fine_value = moved_sheet(other_layer[row], strip, lateral, up)
                        values.append(jnp.where(edge, inject(coarse, axis_id, turn), fine_value))
                    pair.append(values)
                laterals.append(pair)
            deeper = [second_layer[row] for row in rows]
            below = [own[var] for var in range(VARS)]
            result = sheet_step(facing, here, below, deeper, laterals)
            for var in range(VARS):
                old[rows[var]] = here[var]
                mid[rows[var]] = result[var]

        @pl.when(scalars[1 + facing] == 0)
        def _():
            here = [coarse_layer[row] for row in rows]
            laterals = [
                [[moved_sheet(coarse_layer[row], strips[lateral][row], lateral, up) for row in rows] for up in range(2)]
                for lateral in range(2)
            ]
            deeper = [other_layer[row] for row in rows]
            below = [parent_layer[row] for row in rows]
            result = sheet_step(facing, here, below, deeper, laterals)
            for var in range(VARS):
                old[rows[var]] = inject(here[var], axis_id, turn)
                mid[rows[var]] = inject(0.5 * (here[var] + result[var]), axis_id, turn)


def fine_kernel(
    scalars, fine, incoming, tables, fine_next, out, columns, fluxes, passed, new, middle, packs, old, mid, pack, own
):
    lanes = lanes_of()
    for number, kind in enumerate((0, 1, 2, 3, 4, 6)):
        collect_packs(incoming, CHUNKS, kind, packs.at[number], 0 if kind == 6 else 1)
    family_ghosts(scalars, fine, tables, [packs.at[number] for number in range(6)], old, mid, own)
    live = scalars[13] > 0

    def emit_middle(block, half, values):
        for var in range(VARS):
            middle[block, var, :, half * 128 : half * 128 + 128] = values[var]

    def emit(block, half, values):
        for var in range(VARS):
            new[block * 2 + half, var] = values[var]
            fine_next[block, var, :, half * 128 : half * 128 + 128] = jnp.where(live, values[var], 0.0)

    advance_cube(fine, 0, columns, fluxes, passed, own, old, emit_middle)
    advance_cube(middle, 0, columns, fluxes, passed, own, mid, emit)

    source = (lanes >> 4 & 3) * 32 + (lanes & 7) * 2

    def means(var, carry):
        for part in range(2):
            for y_bit in range(2):
                total = jnp.zeros((8, 128), jnp.float32)
                for half in range(2):
                    for z_bit in range(2):
                        number = (part | y_bit << 1 | z_bit << 2) * 2 + half
                        tile = new[number, var, pl.ds(0, 8, 2), :] + new[number, var, pl.ds(1, 8, 2), :]
                        tile = tile + rolled(tile, -1)
                        tile = tile + rolled(tile, -16)
                        tile = take(tile, source, 1) * 0.125
                        wanted = (lanes >> 6 == half) & (lanes >> 3 & 1 == z_bit)
                        total = jnp.where(wanted, tile, total)
                pack[(var * 2 + part) * 2 + y_bit] = total
        return carry

    lax.fori_loop(0, VARS, means, 0)

    def one(number, carry):
        for pair in range(4):
            out[number * 4 + pair] = pack[number, pair * 2 : pair * 2 + 2, :]
        return carry

    lax.fori_loop(0, 20, one, 0)


def merge_kernel(home, coarse_new, incoming, out):
    out[...] = coarse_new[...]
    for block in range(8):

        @pl.when(home[block] >= 0)
        def _():
            def one(number, carry):
                for part in range(2):
                    for half in range(2):
                        for pair in range(4):
                            chunk = ((number * 2 + part) * 2 + half) * 4 + pair
                            row = part * 8 + pair * 2
                            out[block, number, row : row + 2, half * 128 : half * 128 + 128] = incoming[
                                chunk * 8 + block
                            ]
                return carry

            lax.fori_loop(0, VARS, one, 0)


def call(kernel, scalar_count, shapes, scratch, *operands):
    vmem = pl.BlockSpec(memory_space=pltpu.VMEM)
    smem = pl.BlockSpec(memory_space=pltpu.SMEM)
    outs = [jax.ShapeDtypeStruct(shape, jnp.float32) for shape in shapes]
    result = pl.pallas_call(
        kernel,
        out_shape=outs,
        in_specs=[smem] * scalar_count + [vmem] * (len(operands) - scalar_count),
        out_specs=[vmem] * len(outs),
        scratch_shapes=[pltpu.VMEM(shape, jnp.float32) for shape in scratch],
        compiler_params=pltpu.CompilerParams(vmem_limit_bytes=VMEM_BYTES),
    )(*operands)
    return result if len(outs) > 1 else result[0]


def decode(code, levels):
    coords = []
    for axis_id in range(3):
        gray = jnp.zeros_like(code)
        for level in range(axis_id, levels, 3):
            gray = gray | ((code >> level & 1) << level // 3)
        coord = gray
        for shift in range(1, levels):
            coord = coord ^ (gray >> shift)
        coords.append(coord)
    return coords


def encode(coords, levels):
    code = jnp.zeros_like(coords[0])
    for level in range(levels):
        coord = coords[level % 3]
        gray = coord ^ (coord >> 1)
        code = code | ((gray >> level // 3 & 1) << level)
    return code


def extents(levels):
    return [1 << len(range(axis_id, levels, 3)) for axis_id in range(3)]


def moved(coords, axis_id, step, levels):
    sizes = extents(levels)
    return [jnp.where(axis_id == k, (coords[k] + step) & (sizes[k] - 1), coords[k]) for k in range(3)]


def exchange(values):
    return lax.all_to_all(values, AXES, split_axis=0, concat_axis=0, tiled=True)


def shards(coarse_state, fine_state, fine_parent):
    devices = lax.axis_size(AXES)
    device_id = lax.axis_index(AXES).astype(jnp.int32)
    blocks_here = coarse_state.shape[0]
    levels = (blocks_here * devices).bit_length() - 1
    device_levels = levels - 3
    device_ids = jnp.arange(devices, dtype=jnp.int32)

    facing = jnp.minimum(device_id // SLOTS, 5)
    axis_id, high = facing // 2, facing % 2
    step = 1 - 2 * high
    parents = jnp.maximum(fine_parent, 0)
    parent_coords = decode(parents, levels)

    def family_at(blocks):
        match = fine_parent[None, :] == blocks.reshape(-1)[:, None]
        return jnp.max(jnp.where(match, device_ids[None, :], -1), axis=1).reshape(blocks.shape)

    def inner_of(coords):
        along = jnp.where(axis_id == 0, coords[0], jnp.where(axis_id == 1, coords[1], coords[2]))
        return jnp.where((along & 1) == high, 0, 1)

    beside = moved(parent_coords, axis_id, step, levels)
    beside_id = encode(beside, levels)
    near = family_at(beside_id)
    coarse_kind = 2 + 2 * inner_of(beside)
    coarse_index = (beside_id >> 3) * 6 + coarse_kind
    columns_of = [coarse_index, jnp.where(near >= 0, near * 6, coarse_index + 1), jnp.maximum(near, 0) * 6 + 1]
    for lateral in range(2):
        other = jnp.where(axis_id > lateral, lateral, lateral + 1)
        for direction in (-1, 1):
            third_id = encode(moved(beside, other, direction, levels), levels)
            third = family_at(third_id)
            columns_of.append(
                jnp.where((near >= 0) & (third >= 0), third * 6, (third_id >> 3) * 6 + coarse_kind)
            )
    across = encode(moved(decode(device_ids, device_levels), axis_id, step, device_levels), device_levels)
    columns_of += [across * 6 + 2, (parents >> 3) * 6 + 2 + 2 * inner_of(parent_coords)]
    first_index = jnp.stack(columns_of, axis=1).reshape(-1)
    tables = jnp.asarray(sheet_tables())
    pair = (device_id - facing * SLOTS) % 4
    edges = jnp.asarray(sheet_tables()[:, :, 1, 2].reshape(3, 2, 4, 2, 128))
    masks = lax.dynamic_slice(edges, (axis_id, 0, pair, 0, 0), (1, 2, 1, 2, 128)).reshape(2, 2, 128)

    own_parent = lax.dynamic_index_in_dim(fine_parent, device_id, keepdims=False)
    live = own_parent >= 0
    own_coords = decode(jnp.maximum(own_parent, 0), levels)
    sides = jnp.arange(6, dtype=jnp.int32)
    side_coords = moved([jnp.broadcast_to(c, (6,)) for c in own_coords], sides // 2, 2 * (sides % 2) - 1, levels)

    def has_family(coords):
        ids = encode(coords, levels)
        return jnp.any(fine_parent[None, :] == ids[:, None], axis=1).astype(jnp.int32)

    side_near = has_family(side_coords)
    spots = jnp.arange(24, dtype=jnp.int32)
    spot_axis, spot_lateral = spots // 8, spots // 2 % 2
    spot_coords = moved([jnp.broadcast_to(c, (24,)) for c in own_coords], spot_axis, 2 * (spots // 4 % 2) - 1, levels)
    spot_other = jnp.where(spot_axis > spot_lateral, spot_lateral, spot_lateral + 1)
    third_near = has_family(moved(spot_coords, spot_other, 2 * (spots % 2) - 1, levels))
    low_bits = [c & 1 for c in own_coords]
    turns = jnp.stack(
        [
            low_bits[others(side // 2)[0]] + 2 * low_bits[others(side // 2)[1]]
            for side in range(6)
        ]
    )
    flip = flip_of(device_id)
    scalars = jnp.concatenate(
        [flip[None], side_near, turns, live.astype(jnp.int32)[None], third_near]
    ).astype(jnp.int32)
    local_ids = device_id * blocks_here + jnp.arange(blocks_here, dtype=jnp.int32)
    home = family_at(local_ids)

    candidates = jnp.arange(2 * devices, dtype=jnp.int32)
    refined = jnp.any(fine_parent[None, :] == candidates[:, None], axis=1)
    unused = jnp.max(jnp.where(refined, -1, candidates))
    targets = jnp.where(fine_parent >= 0, fine_parent, unused)

    block_shape = coarse_state.shape
    columns = (8, VARS, ROWS, 128)
    passed = (8, VARS, 16, 128)
    packs = (30, 8, 128)
    own = (3 * VARS, 8, 128)

    outgoing = call(
        first_kernel, 1, [(devices * 6, 2, 128)], [(180, 8, 128)], device_id[None], coarse_state, fine_state
    )
    incoming = exchange(outgoing)
    selected = call(select_kernel, 1, [(devices * CHUNKS, 2, 128)], [], first_index, incoming, masks)
    received = exchange(selected)
    fine_next, outgoing = call(
        fine_kernel,
        1,
        [block_shape, (devices, 2, 128)],
        [columns, columns, passed, (16, VARS, 16, 128), block_shape, (6, 30, 8, 128), packs, packs, packs, own],
        scalars,
        fine_state,
        received,
        tables,
    )
    coarse_new = call(
        coarse_kernel, 1, [block_shape], [columns, columns, passed, packs, own], scalars, coarse_state, received
    )
    incoming = exchange(outgoing)
    placed = call(place_kernel, 1, [(devices * blocks_here, 2, 128)], [], targets, incoming)
    received = exchange(placed)
    coarse_next = call(merge_kernel, 1, [block_shape], [], home, coarse_new, received)
    return coarse_next, fine_next


def solution(mesh):
    in_specs = (P(AXES, None, None, None), P(AXES, None, None, None), P())
    out_specs = (P(AXES, None, None, None), P(AXES, None, None, None))
    return jax.shard_map(shards, mesh=mesh, in_specs=in_specs, out_specs=out_specs, check_vma=False)
```

```python
import functools

import jax
import jax.numpy as jnp
import numpy as np
from jax import lax
from jax.experimental import pallas as pl
from jax.experimental.pallas import tpu as pltpu
from jax.sharding import PartitionSpec as P

GAMMA = 1.4
LAMBDA_STEP = 0.08
AXES = ("wide", "narrow")
VARS = 5
SLOTS = 20
CHUNKS = 7
MIB = 1024 * 1024


def lanes_of(shape=(8, 128)):
    return lax.broadcasted_iota(jnp.int32, shape, 1)


def rows_of(shape=(8, 128)):
    return lax.broadcasted_iota(jnp.int32, shape, 0)


def others(axis_id):
    return [other for other in range(3) if other != axis_id]


def cube_block(axis_id, bit, t):
    first, second = others(axis_id)
    return (bit << axis_id) | ((t & 1) << first) | ((t >> 1) << second)


def rolled(values, shift, axis=1):
    shift %= values.shape[axis]
    return pltpu.roll(values, shift, axis) if shift else values


def sheet_cells(axis_id):
    row, lane = np.meshgrid(np.arange(8), np.arange(128), indexing="ij")
    if axis_id == 0:
        t, half = row >> 1, row & 1
        return (t & 1) * 16 + half * 8 + (lane >> 4), (t >> 1) * 16 + (lane & 15)
    if axis_id == 1:
        t, part = lane >> 5, lane >> 4 & 1
        return (t & 1) * 16 + part * 8 + row, (t >> 1) * 16 + (lane & 15)
    t, part, half = lane >> 2 & 3, lane >> 1 & 1, lane & 1
    return (t & 1) * 16 + part * 8 + row, (t >> 1) * 16 + half * 8 + (lane >> 4)


def sheet_tables():
    tables = np.zeros((3, 2, 2, 3, 8, 128), np.int32)
    for axis_id in range(3):
        cells = sheet_cells(axis_id)
        place = np.zeros((32, 32, 2), np.int32)
        for row in range(8):
            for lane in range(128):
                place[cells[0][row, lane], cells[1][row, lane]] = (row, lane)
        for lateral in range(2):
            for up in range(2):
                wanted = list(cells)
                wanted[lateral] = (wanted[lateral] + (1 if up else -1)) % 32
                source = place[wanted[0], wanted[1]]
                rows, lanes = source[..., 0], source[..., 1]
                table = tables[axis_id, lateral, up]
                table[1] = rows
                for lane in range(128):
                    table[0][rows[:, lane], lane] = lanes[:, lane]
                table[2] = cells[lateral] == (0 if up else 31)
    return tables


def pack_side(cells, pack, pack_row, var, axis_id, high, bit, depth=0):
    lanes = lanes_of()
    if axis_id == 0:
        row = 15 - depth if high else depth
        for t in range(4):
            for half in range(2):
                tile = cells(cube_block(0, bit, t), half, var, row, 1)
                pack[pack_row, t * 2 + half : t * 2 + half + 1, :] = tile
        return
    total = jnp.zeros((8, 128), jnp.float32)
    if axis_id == 1:
        offset = 112 - 16 * depth if high else 16 * depth
        for t in range(4):
            for part in range(2):
                group = t * 2 + part
                tile = cells(cube_block(1, bit, t), high, var, part * 8, 8)
                total = jnp.where(lanes >> 4 == group, rolled(tile, group * 16 - offset), total)
    else:
        offset = 15 - depth if high else depth
        for t in range(4):
            for part in range(2):
                for half in range(2):
                    place = t * 4 + part * 2 + half
                    tile = cells(cube_block(2, bit, t), half, var, part * 8, 8)
                    total = jnp.where(lanes & 15 == place, rolled(tile, place - offset), total)
    pack[pack_row] = total


def take(tile, index, axis):
    return jnp.take_along_axis(tile, index, axis=axis, mode="promise_in_bounds")


def inject(tile, axis_id, t):
    lanes, rows = lanes_of(), rows_of()
    if axis_id == 0:
        row_index = 2 * t + (rows >> 1 & 1)
        lane_index = (4 * (rows & 1) + (lanes >> 5)) * 16 + 8 * (rows >> 2 & 1) + (lanes >> 1 & 7)
        return take(take(tile, row_index, 0), lane_index, 1)
    if axis_id == 1:
        part = lanes >> 4 & 1
        lane_index = (2 * t + (lanes >> 5 & 1)) * 16 + 8 * (lanes >> 6 & 1) + (lanes >> 1 & 7)
    else:
        part = lanes >> 1 & 1
        lane_index = (4 * (lanes & 1) + (lanes >> 5)) * 16 + 4 * t + 2 * (lanes >> 2 & 1) + (lanes >> 3 & 1)
    low = take(take(tile, rows >> 1, 0), lane_index, 1)
    high = take(take(tile, 4 + (rows >> 1), 0), lane_index, 1)
    return jnp.where(part == 1, high, low)


ROWS = 48


def primitives(values):
    inverse = 1.0 / values[0]
    squares = values[1] * values[1] + values[2] * values[2] + values[3] * values[3]
    pressure = (GAMMA - 1.0) * (values[4] - 0.5 * squares * inverse)
    return inverse, pressure


def flux_of(values, prims, axis_id):
    inverse, pressure = prims
    velocity = values[1 + axis_id] * inverse
    result = [values[1 + axis_id]]
    for component in range(3):
        term = values[1 + component] * velocity
        result.append(term + pressure if component == axis_id else term)
    result.append((values[4] + pressure) * velocity)
    return result


def face_flux(low, low_flux, high, axis_id):
    high_flux = flux_of(high, primitives(high), axis_id)
    middle = [
        0.5 * (low[v] + high[v]) - 0.5 * LAMBDA_STEP * (high_flux[v] - low_flux[v]) for v in range(VARS)
    ]
    return flux_of(middle, primitives(middle), axis_id)


def column(block, half):
    return (block >> 1) * 2 + half


def cells_of(columns):
    def cells(block, half, var, start, size):
        row = 8 + (block & 1) * 16 + start
        return columns[column(block, half), var, row : row + size, :]

    return cells


def cells_in(blocks, flip):
    def cells(block, half, var, start, size):
        return blocks[block ^ flip, var, start : start + size, half * 128 : half * 128 + 128]

    return cells


def parts_of(tile, shifts):
    return jnp.concatenate([rolled(tile, shift) for shift in shifts], axis=0)


def advance_cube(source, flip, columns, fluxes, passed, own_pack, ghost_pack, emit):
    lanes = lanes_of((16, 128))
    cells = cells_in(source, flip)
    ghost = [[ghost_pack[side * VARS + var] for var in range(VARS)] for side in range(6)]
    for block in range(8):
        row = 8 + (block & 1) * 16
        for half in range(2):
            for var in range(VARS):
                columns[column(block, half), var, row : row + 16, :] = cells(block, half, var, 0, 16)
    lows = []
    for axis_id in range(3):
        for var in range(VARS):
            pack_side(cells, own_pack, axis_id * VARS + var, var, axis_id, 0, 0)
        inner = [own_pack[axis_id * VARS + var] for var in range(VARS)]
        outer = ghost[2 * axis_id]
        lows.append(face_flux(outer, flux_of(outer, primitives(outer), axis_id), inner, axis_id))
    for number in range(8):
        for var in range(VARS):
            columns[number, var, 40:41, :] = ghost[1][var][number : number + 1, :]
            fluxes[number, var, 7:8, :] = lows[0][var][number : number + 1, :]

    def tiles(block, half):
        row = 8 + (block & 1) * 16
        return [columns[column(block, half), var, row : row + 16, :] for var in range(VARS)]

    for z_bit in range(2):
        for x_bit in range(2):
            t_y = x_bit + 2 * z_bit
            here = tiles(x_bit | z_bit << 2, 0)
            turned = [rolled(tile, -16) for tile in here]
            before = [
                parts_of(lows[1][var], [-(t_y * 2 + part) * 16 for part in range(2)]) for var in range(VARS)
            ]
            for y_bit in range(2):
                block = x_bit | y_bit << 1 | z_bit << 2
                t_z = x_bit + 2 * y_bit
                row = 8 + x_bit * 16
                for half in range(2):
                    spot = column(block, half)
                    if y_bit and half:
                        ahead = None
                        turned_ahead = [
                            parts_of(ghost[3][var], [112 - (t_y * 2 + part) * 16 for part in range(2)])
                            for var in range(VARS)
                        ]
                    else:
                        ahead = tiles(block, 1) if half == 0 else tiles(block | 2, 0)
                        turned_ahead = [rolled(tile, -16) for tile in ahead]
                    places = [t_z * 4 + part * 2 + half for part in range(2)]
                    if z_bit:
                        beyond = [
                            parts_of(ghost[5][var], [15 - place for place in places]) for var in range(VARS)
                        ]
                        behind = [passed[(x_bit * 2 + y_bit) * 2 + half, var] for var in range(VARS)]
                    else:
                        beyond = [rolled(tile, 15) for tile in tiles(block | 4, half)]
                        behind = [parts_of(lows[2][var], [-place for place in places]) for var in range(VARS)]
                    prims = primitives(here)

                    above = [columns[spot, var, row + 1 : row + 17, :] for var in range(VARS)]
                    face = face_flux(here, flux_of(here, prims, 0), above, 0)
                    change = []
                    for var in range(VARS):
                        fluxes[spot, var, row : row + 16, :] = face[var]
                        change.append(face[var] - fluxes[spot, var, row - 1 : row + 15, :])

                    above = [jnp.where(lanes >= 112, turned_ahead[v], turned[v]) for v in range(VARS)]
                    face = face_flux(here, flux_of(here, prims, 1), above, 1)
                    after = [rolled(face[var], 16) for var in range(VARS)]
                    for var in range(VARS):
                        change[var] += face[var] - jnp.where(lanes < 16, before[var], after[var])
                    before = after

                    above = [
                        jnp.where(lanes & 15 == 15, beyond[v], rolled(here[v], -1)) for v in range(VARS)
                    ]
                    face = face_flux(here, flux_of(here, prims, 2), above, 2)
                    for var in range(VARS):
                        down = jnp.where(lanes & 15 == 0, behind[var], rolled(face[var], 1))
                        change[var] += face[var] - down
                        if z_bit == 0:
                            passed[(x_bit * 2 + y_bit) * 2 + half, var] = rolled(face[var], -15)

                    emit(block, half, [here[v] - LAMBDA_STEP * change[v] for v in range(VARS)])
                    here, turned = ahead, turned_ahead


def pack_all(cells, pack, base, inner, depth=0):
    def one(var, carry):
        for facing in range(6):
            high = facing % 2
            pack_side(cells, pack, base + facing * VARS + var, var, facing // 2, high, high ^ inner, depth)
        return carry

    lax.fori_loop(0, VARS, one, 0)


def spread_packs(pack, base, out, stride, kind):
    def one(number, carry):
        for pair in range(4):
            out[(number * 4 + pair) * stride + kind] = pack[base + number, pair * 2 : pair * 2 + 2, :]
        return carry

    lax.fori_loop(0, 30, one, 0)


def collect_packs(incoming, stride, kind, pack, turned=1):
    def one(var, carry):
        for facing in range(6):
            for pair in range(4):
                chunk = ((facing ^ turned) * SLOTS + var * 4 + pair) * stride + kind
                pack[facing * VARS + var, pair * 2 : pair * 2 + 2, :] = incoming[chunk]
        return carry

    lax.fori_loop(0, VARS, one, 0)


def flip_of(device_id):
    flip = 0
    for level in range(7):
        flip = flip ^ ((device_id >> level & 1) << level % 3)
    return flip


def first_kernel(scalars, coarse, fine, out, pack):
    flip = flip_of(scalars[0])
    for depth in range(2):
        pack_all(cells_in(fine, 0), pack, depth * 30, 0, depth)
        for inner in range(2):
            pack_all(cells_in(coarse, flip), pack, (2 + 2 * inner + depth) * 30, inner, depth)
    for kind in range(6):
        spread_packs(pack, kind * 30, out, 6, kind)


def select_kernel(index, incoming, masks, out):
    up = [masks[lateral] > 0 for lateral in range(2)]

    def one(step, carry):
        results = []
        for lane in range(4):
            number = step * 4 + lane
            rows = [incoming[index[number * 9 + column]] for column in range(9)]
            strips = [jnp.where(up[j], rows[4 + 2 * j], rows[3 + 2 * j]) for j in range(2)]
            results.append(rows[:3] + strips + rows[7:])
        for lane in range(4):
            for kind in range(CHUNKS):
                out[(step * 4 + lane) * CHUNKS + kind] = results[lane][kind]
        return carry

    lax.fori_loop(0, out.shape[0] // (4 * CHUNKS), one, 0)


def place_kernel(target, incoming, out):
    def one(step, carry):
        for lane in range(8):
            number = step * 8 + lane
            out[target[number]] = incoming[number]
        return carry

    lax.fori_loop(0, target.shape[0] // 8, one, 0)


def coarse_kernel(scalars, coarse, incoming, coarse_new, columns, fluxes, passed, ghost, own):
    flip = scalars[0]

    def emit(block, half, values):
        for var in range(VARS):
            coarse_new[block ^ flip, var, :, half * 128 : half * 128 + 128] = values[var]

    collect_packs(incoming, CHUNKS, 5, ghost)
    advance_cube(coarse, flip, columns, fluxes, passed, own, ghost, emit)


def sheet_step(facing, here, below, deeper, laterals):
    axis_id = facing // 2
    prims = primitives(here)
    change = [None] * VARS
    pairs = {axis_id: (below, deeper) if facing % 2 else (deeper, below)}
    for lateral, other in enumerate(others(axis_id)):
        pairs[other] = laterals[lateral]
    for along in range(3):
        down, up = pairs[along]
        upper = face_flux(here, flux_of(here, prims, along), up, along)
        lower = face_flux(down, flux_of(down, primitives(down), along), here, along)
        for var in range(VARS):
            term = upper[var] - lower[var]
            change[var] = term if along == 0 else change[var] + term
    return [here[var] - LAMBDA_STEP * change[var] for var in range(VARS)]


def family_ghosts(scalars, fine, tables, packs, old, mid, own):
    coarse_layer, other_layer, second_layer, strip_a, strip_b, parent_layer = packs
    strips = (strip_a, strip_b)
    for facing in range(6):
        axis_id, high = facing // 2, facing % 2
        rows = [facing * VARS + var for var in range(VARS)]
        turn = scalars[7 + facing]

        def moved_sheet(tile, strip, lateral, up):
            tile = jnp.where(tables[axis_id, lateral, up, 2] > 0, strip, tile)
            tile = take(tile, tables[axis_id, lateral, up, 0], 1)
            return take(tile, tables[axis_id, lateral, up, 1], 0)

        @pl.when(scalars[1 + facing] > 0)
        def _():
            for var in range(VARS):
                pack_side(cells_in(fine, 0), own, var, var, axis_id, high, high)
            here = [other_layer[row] for row in rows]
            laterals = []
            for lateral in range(2):
                pair = []
                for up in range(2):
                    known = scalars[14 + facing * 4 + lateral * 2 + up] > 0
                    edge = (tables[axis_id, lateral, 1 - up, 2] > 0) & jnp.logical_not(known)
                    values = []
                    for row in rows:
                        strip = strips[lateral][row]
                        coarse = moved_sheet(coarse_layer[row], strip, lateral, up)
                        fine_value = moved_sheet(other_layer[row], strip, lateral, up)
                        values.append(jnp.where(edge, inject(coarse, axis_id, turn), fine_value))
                    pair.append(values)
                laterals.append(pair)
            deeper = [second_layer[row] for row in rows]
            below = [own[var] for var in range(VARS)]
            result = sheet_step(facing, here, below, deeper, laterals)
            for var in range(VARS):
                old[rows[var]] = here[var]
                mid[rows[var]] = result[var]

        @pl.when(scalars[1 + facing] == 0)
        def _():
            here = [coarse_layer[row] for row in rows]
            laterals = [
                [[moved_sheet(coarse_layer[row], strips[lateral][row], lateral, up) for row in rows] for up in range(2)]
                for lateral in range(2)
            ]
            deeper = [other_layer[row] for row in rows]
            below = [parent_layer[row] for row in rows]
            result = sheet_step(facing, here, below, deeper, laterals)
            for var in range(VARS):
                old[rows[var]] = inject(here[var], axis_id, turn)
                mid[rows[var]] = inject(0.5 * (here[var] + result[var]), axis_id, turn)


def fine_kernel(
    scalars, fine, incoming, tables, fine_next, out, columns, fluxes, passed, new, middle, packs, old, mid, pack, own
):
    lanes = lanes_of()
    for number, kind in enumerate((0, 1, 2, 3, 4, 6)):
        collect_packs(incoming, CHUNKS, kind, packs.at[number], 0 if kind == 6 else 1)
    family_ghosts(scalars, fine, tables, [packs.at[number] for number in range(6)], old, mid, own)
    live = scalars[13] > 0

    def emit_middle(block, half, values):
        for var in range(VARS):
            middle[block, var, :, half * 128 : half * 128 + 128] = values[var]

    def emit(block, half, values):
        for var in range(VARS):
            new[block * 2 + half, var] = values[var]
            fine_next[block, var, :, half * 128 : half * 128 + 128] = jnp.where(live, values[var], 0.0)

    advance_cube(fine, 0, columns, fluxes, passed, own, old, emit_middle)
    advance_cube(middle, 0, columns, fluxes, passed, own, mid, emit)

    source = (lanes >> 4 & 3) * 32 + (lanes & 7) * 2

    def means(var, carry):
        for part in range(2):
            for y_bit in range(2):
                total = jnp.zeros((8, 128), jnp.float32)
                for half in range(2):
                    for z_bit in range(2):
                        number = (part | y_bit << 1 | z_bit << 2) * 2 + half
                        tile = new[number, var, pl.ds(0, 8, 2), :] + new[number, var, pl.ds(1, 8, 2), :]
                        tile = tile + rolled(tile, -1)
                        tile = tile + rolled(tile, -16)
                        tile = take(tile, source, 1) * 0.125
                        wanted = (lanes >> 6 == half) & (lanes >> 3 & 1 == z_bit)
                        total = jnp.where(wanted, tile, total)
                pack[(var * 2 + part) * 2 + y_bit] = total
        return carry

    lax.fori_loop(0, VARS, means, 0)

    def one(number, carry):
        for pair in range(4):
            out[number * 4 + pair] = pack[number, pair * 2 : pair * 2 + 2, :]
        return carry

    lax.fori_loop(0, 20, one, 0)


def merge_kernel(home, coarse_new, incoming, out):
    out[...] = coarse_new[...]
    for block in range(8):

        @pl.when(home[block] >= 0)
        def _():
            def one(number, carry):
                for part in range(2):
                    for half in range(2):
                        for pair in range(4):
                            chunk = ((number * 2 + part) * 2 + half) * 4 + pair
                            row = part * 8 + pair * 2
                            out[block, number, row : row + 2, half * 128 : half * 128 + 128] = incoming[
                                chunk * 8 + block
                            ]
                return carry

            lax.fori_loop(0, VARS, one, 0)


def call(kernel, mebibytes, scalar_count, shapes, scratch, *operands):
    vmem = pl.BlockSpec(memory_space=pltpu.VMEM)
    smem = pl.BlockSpec(memory_space=pltpu.SMEM)
    outs = [jax.ShapeDtypeStruct(shape, jnp.float32) for shape in shapes]
    result = pl.pallas_call(
        kernel,
        out_shape=outs,
        in_specs=[smem] * scalar_count + [vmem] * (len(operands) - scalar_count),
        out_specs=[vmem] * len(outs),
        scratch_shapes=[pltpu.VMEM(shape, jnp.float32) for shape in scratch],
        compiler_params=pltpu.CompilerParams(vmem_limit_bytes=mebibytes * MIB),
    )(*operands)
    return result if len(outs) > 1 else result[0]


def decode(code, levels):
    coords = []
    for axis_id in range(3):
        gray = jnp.zeros_like(code)
        for level in range(axis_id, levels, 3):
            gray = gray | ((code >> level & 1) << level // 3)
        coord = gray
        for shift in range(1, levels):
            coord = coord ^ (gray >> shift)
        coords.append(coord)
    return coords


def encode(coords, levels):
    code = jnp.zeros_like(coords[0])
    for level in range(levels):
        coord = coords[level % 3]
        gray = coord ^ (coord >> 1)
        code = code | ((gray >> level // 3 & 1) << level)
    return code


def extents(levels):
    return [1 << len(range(axis_id, levels, 3)) for axis_id in range(3)]


def moved(coords, axis_id, step, levels):
    sizes = extents(levels)
    return [jnp.where(axis_id == k, (coords[k] + step) & (sizes[k] - 1), coords[k]) for k in range(3)]


def exchange(values):
    return lax.all_to_all(values, AXES, split_axis=0, concat_axis=0, tiled=True)


def shards(coarse_state, fine_state, fine_parent):
    devices = lax.axis_size(AXES)
    device_id = lax.axis_index(AXES).astype(jnp.int32)
    blocks_here = coarse_state.shape[0]
    levels = (blocks_here * devices).bit_length() - 1
    device_levels = levels - 3
    device_ids = jnp.arange(devices, dtype=jnp.int32)

    facing = jnp.minimum(device_id // SLOTS, 5)
    axis_id, high = facing // 2, facing % 2
    step = 1 - 2 * high
    parents = jnp.maximum(fine_parent, 0)
    parent_coords = decode(parents, levels)

    def family_at(blocks):
        match = fine_parent[None, :] == blocks.reshape(-1)[:, None]
        return jnp.max(jnp.where(match, device_ids[None, :], -1), axis=1).reshape(blocks.shape)

    def inner_of(coords):
        along = jnp.where(axis_id == 0, coords[0], jnp.where(axis_id == 1, coords[1], coords[2]))
        return jnp.where((along & 1) == high, 0, 1)

    beside = moved(parent_coords, axis_id, step, levels)
    beside_id = encode(beside, levels)
    near = family_at(beside_id)
    coarse_kind = 2 + 2 * inner_of(beside)
    coarse_index = (beside_id >> 3) * 6 + coarse_kind
    columns_of = [coarse_index, jnp.where(near >= 0, near * 6, coarse_index + 1), jnp.maximum(near, 0) * 6 + 1]
    for lateral in range(2):
        other = jnp.where(axis_id > lateral, lateral, lateral + 1)
        for direction in (-1, 1):
            third_id = encode(moved(beside, other, direction, levels), levels)
            third = family_at(third_id)
            columns_of.append(
                jnp.where((near >= 0) & (third >= 0), third * 6, (third_id >> 3) * 6 + coarse_kind)
            )
    across = encode(moved(decode(device_ids, device_levels), axis_id, step, device_levels), device_levels)
    columns_of += [across * 6 + 2, (parents >> 3) * 6 + 2 + 2 * inner_of(parent_coords)]
    first_index = jnp.stack(columns_of, axis=1).reshape(-1)
    tables = jnp.asarray(sheet_tables())
    pair = (device_id - facing * SLOTS) % 4
    edges = jnp.asarray(sheet_tables()[:, :, 1, 2].reshape(3, 2, 4, 2, 128))
    masks = lax.dynamic_slice(edges, (axis_id, 0, pair, 0, 0), (1, 2, 1, 2, 128)).reshape(2, 2, 128)

    own_parent = lax.dynamic_index_in_dim(fine_parent, device_id, keepdims=False)
    live = own_parent >= 0
    own_coords = decode(jnp.maximum(own_parent, 0), levels)
    sides = jnp.arange(6, dtype=jnp.int32)
    side_coords = moved([jnp.broadcast_to(c, (6,)) for c in own_coords], sides // 2, 2 * (sides % 2) - 1, levels)

    def has_family(coords):
        ids = encode(coords, levels)
        return jnp.any(fine_parent[None, :] == ids[:, None], axis=1).astype(jnp.int32)

    side_near = has_family(side_coords)
    spots = jnp.arange(24, dtype=jnp.int32)
    spot_axis, spot_lateral = spots // 8, spots // 2 % 2
    spot_coords = moved([jnp.broadcast_to(c, (24,)) for c in own_coords], spot_axis, 2 * (spots // 4 % 2) - 1, levels)
    spot_other = jnp.where(spot_axis > spot_lateral, spot_lateral, spot_lateral + 1)
    third_near = has_family(moved(spot_coords, spot_other, 2 * (spots % 2) - 1, levels))
    low_bits = [c & 1 for c in own_coords]
    turns = jnp.stack(
        [
            low_bits[others(side // 2)[0]] + 2 * low_bits[others(side // 2)[1]]
            for side in range(6)
        ]
    )
    flip = flip_of(device_id)
    scalars = jnp.concatenate(
        [flip[None], side_near, turns, live.astype(jnp.int32)[None], third_near]
    ).astype(jnp.int32)
    local_ids = device_id * blocks_here + jnp.arange(blocks_here, dtype=jnp.int32)
    home = family_at(local_ids)

    candidates = jnp.arange(2 * devices, dtype=jnp.int32)
    refined = jnp.any(fine_parent[None, :] == candidates[:, None], axis=1)
    unused = jnp.max(jnp.where(refined, -1, candidates))
    targets = jnp.where(fine_parent >= 0, fine_parent, unused)

    block_shape = coarse_state.shape
    columns = (8, VARS, ROWS, 128)
    passed = (8, VARS, 16, 128)
    packs = (30, 8, 128)
    own = (3 * VARS, 8, 128)

    outgoing = call(
        first_kernel, 8, 1, [(devices * 6, 2, 128)], [(180, 8, 128)], device_id[None], coarse_state, fine_state
    )
    incoming = exchange(outgoing)
    selected = call(select_kernel, 6, 1, [(devices * CHUNKS, 2, 128)], [], first_index, incoming, masks)
    received = exchange(selected)
    fine_next, outgoing = call(
        fine_kernel,
        16,
        1,
        [block_shape, (devices, 2, 128)],
        [columns, columns, passed, (16, VARS, 16, 128), block_shape, (6, 30, 8, 128), packs, packs, packs, own],
        scalars,
        fine_state,
        received,
        tables,
    )
    coarse_new = call(
        coarse_kernel, 12, 1, [block_shape], [columns, columns, passed, packs, own], scalars, coarse_state, received
    )
    incoming = exchange(outgoing)
    placed = call(place_kernel, 4, 1, [(devices * blocks_here, 2, 128)], [], targets, incoming)
    received = exchange(placed)
    coarse_next = call(merge_kernel, 6, 1, [block_shape], [], home, coarse_new, received)
    return coarse_next, fine_next


def solution(mesh):
    in_specs = (P(AXES, None, None, None), P(AXES, None, None, None), P())
    out_specs = (P(AXES, None, None, None), P(AXES, None, None, None))
    return jax.shard_map(shards, mesh=mesh, in_specs=in_specs, out_specs=out_specs, check_vma=False)
```

```python
import functools

import jax
import jax.numpy as jnp
import numpy as np
from jax import lax
from jax.experimental import pallas as pl
from jax.experimental.pallas import tpu as pltpu
from jax.sharding import PartitionSpec as P

GAMMA = 1.4
LAMBDA_STEP = 0.08
AXES = ("wide", "narrow")
VARS = 5
SLOTS = 20
CHUNKS = 7
MIB = 1024 * 1024


def lanes_of(shape=(8, 128)):
    return lax.broadcasted_iota(jnp.int32, shape, 1)


def rows_of(shape=(8, 128)):
    return lax.broadcasted_iota(jnp.int32, shape, 0)


def others(axis_id):
    return [other for other in range(3) if other != axis_id]


def cube_block(axis_id, bit, t):
    first, second = others(axis_id)
    return (bit << axis_id) | ((t & 1) << first) | ((t >> 1) << second)


def rolled(values, shift, axis=1):
    shift %= values.shape[axis]
    return pltpu.roll(values, shift, axis) if shift else values


def sheet_cells(axis_id):
    row, lane = np.meshgrid(np.arange(8), np.arange(128), indexing="ij")
    if axis_id == 0:
        t, half = row >> 1, row & 1
        return (t & 1) * 16 + half * 8 + (lane >> 4), (t >> 1) * 16 + (lane & 15)
    if axis_id == 1:
        t, part = lane >> 5, lane >> 4 & 1
        return (t & 1) * 16 + part * 8 + row, (t >> 1) * 16 + (lane & 15)
    t, part, half = lane >> 2 & 3, lane >> 1 & 1, lane & 1
    return (t & 1) * 16 + part * 8 + row, (t >> 1) * 16 + half * 8 + (lane >> 4)


def sheet_tables():
    tables = np.zeros((3, 2, 2, 3, 8, 128), np.int32)
    for axis_id in range(3):
        cells = sheet_cells(axis_id)
        place = np.zeros((32, 32, 2), np.int32)
        for row in range(8):
            for lane in range(128):
                place[cells[0][row, lane], cells[1][row, lane]] = (row, lane)
        for lateral in range(2):
            for up in range(2):
                wanted = list(cells)
                wanted[lateral] = (wanted[lateral] + (1 if up else -1)) % 32
                source = place[wanted[0], wanted[1]]
                rows, lanes = source[..., 0], source[..., 1]
                table = tables[axis_id, lateral, up]
                table[1] = rows
                for lane in range(128):
                    table[0][rows[:, lane], lane] = lanes[:, lane]
                table[2] = cells[lateral] == (0 if up else 31)
    return tables


def pack_side(cells, pack, pack_row, var, axis_id, high, bit, depth=0):
    lanes = lanes_of()
    if axis_id == 0:
        row = 15 - depth if high else depth
        for t in range(4):
            for half in range(2):
                tile = cells(cube_block(0, bit, t), half, var, row, 1)
                pack[pack_row, t * 2 + half : t * 2 + half + 1, :] = tile
        return
    total = jnp.zeros((8, 128), jnp.float32)
    if axis_id == 1:
        offset = 112 - 16 * depth if high else 16 * depth
        for t in range(4):
            for part in range(2):
                group = t * 2 + part
                tile = cells(cube_block(1, bit, t), high, var, part * 8, 8)
                total = jnp.where(lanes >> 4 == group, rolled(tile, group * 16 - offset), total)
    else:
        offset = 15 - depth if high else depth
        for t in range(4):
            for part in range(2):
                for half in range(2):
                    place = t * 4 + part * 2 + half
                    tile = cells(cube_block(2, bit, t), half, var, part * 8, 8)
                    total = jnp.where(lanes & 15 == place, rolled(tile, place - offset), total)
    pack[pack_row] = total


def take(tile, index, axis):
    return jnp.take_along_axis(tile, index, axis=axis, mode="promise_in_bounds")


def inject(tile, axis_id, t):
    lanes, rows = lanes_of(), rows_of()
    if axis_id == 0:
        row_index = 2 * t + (rows >> 1 & 1)
        lane_index = (4 * (rows & 1) + (lanes >> 5)) * 16 + 8 * (rows >> 2 & 1) + (lanes >> 1 & 7)
        return take(take(tile, row_index, 0), lane_index, 1)
    if axis_id == 1:
        part = lanes >> 4 & 1
        lane_index = (2 * t + (lanes >> 5 & 1)) * 16 + 8 * (lanes >> 6 & 1) + (lanes >> 1 & 7)
    else:
        part = lanes >> 1 & 1
        lane_index = (4 * (lanes & 1) + (lanes >> 5)) * 16 + 4 * t + 2 * (lanes >> 2 & 1) + (lanes >> 3 & 1)
    low = take(take(tile, rows >> 1, 0), lane_index, 1)
    high = take(take(tile, 4 + (rows >> 1), 0), lane_index, 1)
    return jnp.where(part == 1, high, low)


ROWS = 48


def primitives(values):
    inverse = 1.0 / values[0]
    squares = values[1] * values[1] + values[2] * values[2] + values[3] * values[3]
    pressure = (GAMMA - 1.0) * (values[4] - 0.5 * squares * inverse)
    return inverse, pressure


def flux_of(values, prims, axis_id):
    inverse, pressure = prims
    velocity = values[1 + axis_id] * inverse
    result = [values[1 + axis_id]]
    for component in range(3):
        term = values[1 + component] * velocity
        result.append(term + pressure if component == axis_id else term)
    result.append((values[4] + pressure) * velocity)
    return result


def face_flux(low, low_flux, high, axis_id):
    high_flux = flux_of(high, primitives(high), axis_id)
    middle = [
        0.5 * (low[v] + high[v]) - 0.5 * LAMBDA_STEP * (high_flux[v] - low_flux[v]) for v in range(VARS)
    ]
    return flux_of(middle, primitives(middle), axis_id)


def column(block, half):
    return (block >> 1) * 2 + half


def cells_of(columns):
    def cells(block, half, var, start, size):
        row = 8 + (block & 1) * 16 + start
        return columns[column(block, half), var, row : row + size, :]

    return cells


def cells_in(blocks, flip):
    def cells(block, half, var, start, size):
        return blocks[block ^ flip, var, start : start + size, half * 128 : half * 128 + 128]

    return cells


def parts_of(tile, shifts):
    return jnp.concatenate([rolled(tile, shift) for shift in shifts], axis=0)


def advance_cube(source, flip, columns, fluxes, passed, own_pack, ghost_pack, emit):
    lanes = lanes_of((16, 128))
    cells = cells_in(source, flip)
    ghost = [[ghost_pack[side * VARS + var] for var in range(VARS)] for side in range(6)]
    for block in range(8):
        row = 8 + (block & 1) * 16
        for half in range(2):
            for var in range(VARS):
                columns[column(block, half), var, row : row + 16, :] = cells(block, half, var, 0, 16)
    lows = []
    for axis_id in range(3):
        for var in range(VARS):
            pack_side(cells, own_pack, axis_id * VARS + var, var, axis_id, 0, 0)
        inner = [own_pack[axis_id * VARS + var] for var in range(VARS)]
        outer = ghost[2 * axis_id]
        lows.append(face_flux(outer, flux_of(outer, primitives(outer), axis_id), inner, axis_id))
    for number in range(8):
        for var in range(VARS):
            columns[number, var, 40:41, :] = ghost[1][var][number : number + 1, :]
            fluxes[number, var, 7:8, :] = lows[0][var][number : number + 1, :]

    def tiles(block, half):
        row = 8 + (block & 1) * 16
        return [columns[column(block, half), var, row : row + 16, :] for var in range(VARS)]

    for z_bit in range(2):
        for x_bit in range(2):
            t_y = x_bit + 2 * z_bit
            here = tiles(x_bit | z_bit << 2, 0)
            turned = [rolled(tile, -16) for tile in here]
            before = [
                parts_of(lows[1][var], [-(t_y * 2 + part) * 16 for part in range(2)]) for var in range(VARS)
            ]
            for y_bit in range(2):
                block = x_bit | y_bit << 1 | z_bit << 2
                t_z = x_bit + 2 * y_bit
                row = 8 + x_bit * 16
                for half in range(2):
                    spot = column(block, half)
                    if y_bit and half:
                        ahead = None
                        turned_ahead = [
                            parts_of(ghost[3][var], [112 - (t_y * 2 + part) * 16 for part in range(2)])
                            for var in range(VARS)
                        ]
                    else:
                        ahead = tiles(block, 1) if half == 0 else tiles(block | 2, 0)
                        turned_ahead = [rolled(tile, -16) for tile in ahead]
                    places = [t_z * 4 + part * 2 + half for part in range(2)]
                    if z_bit:
                        beyond = [
                            parts_of(ghost[5][var], [15 - place for place in places]) for var in range(VARS)
                        ]
                        behind = [passed[(x_bit * 2 + y_bit) * 2 + half, var] for var in range(VARS)]
                    else:
                        beyond = [rolled(tile, 15) for tile in tiles(block | 4, half)]
                        behind = [parts_of(lows[2][var], [-place for place in places]) for var in range(VARS)]
                    prims = primitives(here)

                    above = [columns[spot, var, row + 1 : row + 17, :] for var in range(VARS)]
                    face = face_flux(here, flux_of(here, prims, 0), above, 0)
                    change = []
                    for var in range(VARS):
                        fluxes[spot, var, row : row + 16, :] = face[var]
                        change.append(face[var] - fluxes[spot, var, row - 1 : row + 15, :])

                    above = [jnp.where(lanes >= 112, turned_ahead[v], turned[v]) for v in range(VARS)]
                    face = face_flux(here, flux_of(here, prims, 1), above, 1)
                    after = [rolled(face[var], 16) for var in range(VARS)]
                    for var in range(VARS):
                        change[var] += face[var] - jnp.where(lanes < 16, before[var], after[var])
                    before = after

                    above = [
                        jnp.where(lanes & 15 == 15, beyond[v], rolled(here[v], -1)) for v in range(VARS)
                    ]
                    face = face_flux(here, flux_of(here, prims, 2), above, 2)
                    for var in range(VARS):
                        down = jnp.where(lanes & 15 == 0, behind[var], rolled(face[var], 1))
                        change[var] += face[var] - down
                        if z_bit == 0:
                            passed[(x_bit * 2 + y_bit) * 2 + half, var] = rolled(face[var], -15)

                    emit(block, half, [here[v] - LAMBDA_STEP * change[v] for v in range(VARS)])
                    here, turned = ahead, turned_ahead


def pack_all(cells, pack, base, inner, depth=0):
    def one(var, carry):
        for facing in range(6):
            high = facing % 2
            pack_side(cells, pack, base + facing * VARS + var, var, facing // 2, high, high ^ inner, depth)
        return carry

    lax.fori_loop(0, VARS, one, 0)


def spread_packs(pack, base, out, stride, kind):
    def one(number, carry):
        for pair in range(4):
            out[(number * 4 + pair) * stride + kind] = pack[base + number, pair * 2 : pair * 2 + 2, :]
        return carry

    lax.fori_loop(0, 30, one, 0)


def collect_packs(incoming, stride, kind, pack, turned=1):
    def one(var, carry):
        for facing in range(6):
            for pair in range(4):
                chunk = ((facing ^ turned) * SLOTS + var * 4 + pair) * stride + kind
                pack[facing * VARS + var, pair * 2 : pair * 2 + 2, :] = incoming[chunk]
        return carry

    lax.fori_loop(0, VARS, one, 0)


def flip_of(device_id):
    flip = 0
    for level in range(7):
        flip = flip ^ ((device_id >> level & 1) << level % 3)
    return flip


def first_kernel(scalars, coarse_hbm, fine_hbm, out, pack, coarse, fine, arrived):
    flip = flip_of(scalars[0])
    copies = [
        pltpu.make_async_copy(fine_hbm, fine, arrived.at[0]),
        pltpu.make_async_copy(coarse_hbm, coarse, arrived.at[1]),
    ]
    for copy in copies:
        copy.start()
    copies[0].wait()
    for depth in range(2):
        pack_all(cells_in(fine, 0), pack, depth * 30, 0, depth)
        spread_packs(pack, depth * 30, out, 6, depth)
    copies[1].wait()
    for inner in range(2):
        for depth in range(2):
            kind = 2 + 2 * inner + depth
            pack_all(cells_in(coarse, flip), pack, kind * 30, inner, depth)
            spread_packs(pack, kind * 30, out, 6, kind)


def select_kernel(index, incoming, masks, out):
    up = [masks[lateral] > 0 for lateral in range(2)]

    def one(step, carry):
        results = []
        for lane in range(8):
            number = step * 8 + lane
            rows = [incoming[index[number * 9 + column]] for column in range(9)]
            strips = [jnp.where(up[j], rows[4 + 2 * j], rows[3 + 2 * j]) for j in range(2)]
            results.append(rows[:3] + strips + rows[7:])
        for lane in range(8):
            for kind in range(CHUNKS):
                out[(step * 8 + lane) * CHUNKS + kind] = results[lane][kind]
        return carry

    lax.fori_loop(0, out.shape[0] // (8 * CHUNKS), one, 0)


def place_kernel(target, incoming, out):
    def one(step, carry):
        for lane in range(8):
            number = step * 8 + lane
            out[target[number]] = incoming[number]
        return carry

    lax.fori_loop(0, target.shape[0] // 8, one, 0)


def coarse_kernel(scalars, coarse, incoming, coarse_new, columns, fluxes, passed, ghost, own):
    flip = scalars[0]

    def emit(block, half, values):
        for var in range(VARS):
            coarse_new[block ^ flip, var, :, half * 128 : half * 128 + 128] = values[var]

    collect_packs(incoming, CHUNKS, 5, ghost)
    advance_cube(coarse, flip, columns, fluxes, passed, own, ghost, emit)


def sheet_step(facing, here, below, deeper, laterals):
    axis_id = facing // 2
    prims = primitives(here)
    change = [None] * VARS
    pairs = {axis_id: (below, deeper) if facing % 2 else (deeper, below)}
    for lateral, other in enumerate(others(axis_id)):
        pairs[other] = laterals[lateral]
    for along in range(3):
        down, up = pairs[along]
        upper = face_flux(here, flux_of(here, prims, along), up, along)
        lower = face_flux(down, flux_of(down, primitives(down), along), here, along)
        for var in range(VARS):
            term = upper[var] - lower[var]
            change[var] = term if along == 0 else change[var] + term
    return [here[var] - LAMBDA_STEP * change[var] for var in range(VARS)]


def family_ghosts(scalars, fine, tables, packs, old, mid, own):
    coarse_layer, other_layer, second_layer, strip_a, strip_b, parent_layer = packs
    strips = (strip_a, strip_b)
    for facing in range(6):
        axis_id, high = facing // 2, facing % 2
        rows = [facing * VARS + var for var in range(VARS)]
        turn = scalars[7 + facing]

        def moved_sheet(tile, strip, lateral, up):
            tile = jnp.where(tables[axis_id, lateral, up, 2] > 0, strip, tile)
            tile = take(tile, tables[axis_id, lateral, up, 0], 1)
            return take(tile, tables[axis_id, lateral, up, 1], 0)

        @pl.when(scalars[1 + facing] > 0)
        def _():
            for var in range(VARS):
                pack_side(cells_in(fine, 0), own, var, var, axis_id, high, high)
            here = [other_layer[row] for row in rows]
            laterals = []
            for lateral in range(2):
                pair = []
                for up in range(2):
                    known = scalars[14 + facing * 4 + lateral * 2 + up] > 0
                    edge = (tables[axis_id, lateral, 1 - up, 2] > 0) & jnp.logical_not(known)
                    values = []
                    for row in rows:
                        strip = strips[lateral][row]
                        coarse = moved_sheet(coarse_layer[row], strip, lateral, up)
                        fine_value = moved_sheet(other_layer[row], strip, lateral, up)
                        values.append(jnp.where(edge, inject(coarse, axis_id, turn), fine_value))
                    pair.append(values)
                laterals.append(pair)
            deeper = [second_layer[row] for row in rows]
            below = [own[var] for var in range(VARS)]
            result = sheet_step(facing, here, below, deeper, laterals)
            for var in range(VARS):
                old[rows[var]] = here[var]
                mid[rows[var]] = result[var]

        @pl.when(scalars[1 + facing] == 0)
        def _():
            here = [coarse_layer[row] for row in rows]
            laterals = [
                [[moved_sheet(coarse_layer[row], strips[lateral][row], lateral, up) for row in rows] for up in range(2)]
                for lateral in range(2)
            ]
            deeper = [other_layer[row] for row in rows]
            below = [parent_layer[row] for row in rows]
            result = sheet_step(facing, here, below, deeper, laterals)
            for var in range(VARS):
                old[rows[var]] = inject(here[var], axis_id, turn)
                mid[rows[var]] = inject(0.5 * (here[var] + result[var]), axis_id, turn)


def fine_kernel(
    scalars, fine, incoming, tables, fine_next, out, columns, fluxes, passed, new, middle, packs, old, mid, pack, own
):
    lanes = lanes_of()
    for number, kind in enumerate((0, 1, 2, 3, 4, 6)):
        collect_packs(incoming, CHUNKS, kind, packs.at[number], 0 if kind == 6 else 1)
    family_ghosts(scalars, fine, tables, [packs.at[number] for number in range(6)], old, mid, own)
    live = scalars[13] > 0

    def emit_middle(block, half, values):
        for var in range(VARS):
            middle[block, var, :, half * 128 : half * 128 + 128] = values[var]

    def emit(block, half, values):
        for var in range(VARS):
            new[block * 2 + half, var] = values[var]
            fine_next[block, var, :, half * 128 : half * 128 + 128] = jnp.where(live, values[var], 0.0)

    advance_cube(fine, 0, columns, fluxes, passed, own, old, emit_middle)
    advance_cube(middle, 0, columns, fluxes, passed, own, mid, emit)

    source = (lanes >> 4 & 3) * 32 + (lanes & 7) * 2

    def means(var, carry):
        for part in range(2):
            for y_bit in range(2):
                total = jnp.zeros((8, 128), jnp.float32)
                for half in range(2):
                    for z_bit in range(2):
                        number = (part | y_bit << 1 | z_bit << 2) * 2 + half
                        tile = new[number, var, pl.ds(0, 8, 2), :] + new[number, var, pl.ds(1, 8, 2), :]
                        tile = tile + rolled(tile, -1)
                        tile = tile + rolled(tile, -16)
                        tile = take(tile, source, 1) * 0.125
                        wanted = (lanes >> 6 == half) & (lanes >> 3 & 1 == z_bit)
                        total = jnp.where(wanted, tile, total)
                pack[(var * 2 + part) * 2 + y_bit] = total
        return carry

    lax.fori_loop(0, VARS, means, 0)

    def one(number, carry):
        for pair in range(4):
            out[number * 4 + pair] = pack[number, pair * 2 : pair * 2 + 2, :]
        return carry

    lax.fori_loop(0, 20, one, 0)


def merge_kernel(home_rank, coarse_new, incoming, out, *, places):
    out[...] = coarse_new[...]
    for block in range(8):

        @pl.when(home_rank[block] >= 0)
        def _():
            def one(number, carry):
                for part in range(2):
                    for half in range(2):
                        for pair in range(4):
                            chunk = ((number * 2 + part) * 2 + half) * 4 + pair
                            row = part * 8 + pair * 2
                            out[block, number, row : row + 2, half * 128 : half * 128 + 128] = incoming[
                                chunk * places + home_rank[block]
                            ]
                return carry

            lax.fori_loop(0, VARS, one, 0)


def call(kernel, mebibytes, scalar_count, shapes, scratch, *operands, space=pltpu.VMEM, semaphores=0):
    vmem = pl.BlockSpec(memory_space=pltpu.VMEM)
    smem = pl.BlockSpec(memory_space=pltpu.SMEM)
    outs = [jax.ShapeDtypeStruct(shape, jnp.float32) for shape in shapes]
    result = pl.pallas_call(
        kernel,
        out_shape=outs,
        in_specs=[smem] * scalar_count + [pl.BlockSpec(memory_space=space)] * (len(operands) - scalar_count),
        out_specs=[vmem] * len(outs),
        scratch_shapes=[pltpu.VMEM(shape, jnp.float32) for shape in scratch]
        + ([pltpu.SemaphoreType.DMA((semaphores,))] if semaphores else []),
        compiler_params=pltpu.CompilerParams(vmem_limit_bytes=mebibytes * MIB),
    )(*operands)
    return result if len(outs) > 1 else result[0]


def decode(code, levels):
    coords = []
    for axis_id in range(3):
        gray = jnp.zeros_like(code)
        for level in range(axis_id, levels, 3):
            gray = gray | ((code >> level & 1) << level // 3)
        coord = gray
        for shift in range(1, levels):
            coord = coord ^ (gray >> shift)
        coords.append(coord)
    return coords


def encode(coords, levels):
    code = jnp.zeros_like(coords[0])
    for level in range(levels):
        coord = coords[level % 3]
        gray = coord ^ (coord >> 1)
        code = code | ((gray >> level // 3 & 1) << level)
    return code


def extents(levels):
    return [1 << len(range(axis_id, levels, 3)) for axis_id in range(3)]


def moved(coords, axis_id, step, levels):
    sizes = extents(levels)
    return [jnp.where(axis_id == k, (coords[k] + step) & (sizes[k] - 1), coords[k]) for k in range(3)]


def exchange(values):
    return lax.all_to_all(values, AXES, split_axis=0, concat_axis=0, tiled=True)


def shards(coarse_state, fine_state, fine_parent):
    devices = lax.axis_size(AXES)
    device_id = lax.axis_index(AXES).astype(jnp.int32)
    blocks_here = coarse_state.shape[0]
    levels = (blocks_here * devices).bit_length() - 1
    device_levels = levels - 3
    device_ids = jnp.arange(devices, dtype=jnp.int32)

    facing = jnp.minimum(device_id // SLOTS, 5)
    axis_id, high = facing // 2, facing % 2
    step = 1 - 2 * high
    parents = jnp.maximum(fine_parent, 0)
    parent_coords = decode(parents, levels)

    def family_at(blocks):
        match = fine_parent[None, :] == blocks.reshape(-1)[:, None]
        return jnp.max(jnp.where(match, device_ids[None, :], -1), axis=1).reshape(blocks.shape)

    def inner_of(coords):
        along = jnp.where(axis_id == 0, coords[0], jnp.where(axis_id == 1, coords[1], coords[2]))
        return jnp.where((along & 1) == high, 0, 1)

    beside = moved(parent_coords, axis_id, step, levels)
    beside_id = encode(beside, levels)
    near = family_at(beside_id)
    coarse_kind = 2 + 2 * inner_of(beside)
    coarse_index = (beside_id >> 3) * 6 + coarse_kind
    columns_of = [coarse_index, jnp.where(near >= 0, near * 6, coarse_index + 1), jnp.maximum(near, 0) * 6 + 1]
    for lateral in range(2):
        other = jnp.where(axis_id > lateral, lateral, lateral + 1)
        for direction in (-1, 1):
            third_id = encode(moved(beside, other, direction, levels), levels)
            third = family_at(third_id)
            columns_of.append(
                jnp.where((near >= 0) & (third >= 0), third * 6, (third_id >> 3) * 6 + coarse_kind)
            )
    across = encode(moved(decode(device_ids, device_levels), axis_id, step, device_levels), device_levels)
    columns_of += [across * 6 + 2, (parents >> 3) * 6 + 2 + 2 * inner_of(parent_coords)]
    first_index = jnp.stack(columns_of, axis=1).reshape(-1)
    tables = jnp.asarray(sheet_tables())
    pair = (device_id - facing * SLOTS) % 4
    edges = jnp.asarray(sheet_tables()[:, :, 1, 2].reshape(3, 2, 4, 2, 128))
    masks = lax.dynamic_slice(edges, (axis_id, 0, pair, 0, 0), (1, 2, 1, 2, 128)).reshape(2, 2, 128)

    own_parent = lax.dynamic_index_in_dim(fine_parent, device_id, keepdims=False)
    live = own_parent >= 0
    own_coords = decode(jnp.maximum(own_parent, 0), levels)
    sides = jnp.arange(6, dtype=jnp.int32)
    side_coords = moved([jnp.broadcast_to(c, (6,)) for c in own_coords], sides // 2, 2 * (sides % 2) - 1, levels)

    def has_family(coords):
        ids = encode(coords, levels)
        return jnp.any(fine_parent[None, :] == ids[:, None], axis=1).astype(jnp.int32)

    side_near = has_family(side_coords)
    spots = jnp.arange(24, dtype=jnp.int32)
    spot_axis, spot_lateral = spots // 8, spots // 2 % 2
    spot_coords = moved([jnp.broadcast_to(c, (24,)) for c in own_coords], spot_axis, 2 * (spots // 4 % 2) - 1, levels)
    spot_other = jnp.where(spot_axis > spot_lateral, spot_lateral, spot_lateral + 1)
    third_near = has_family(moved(spot_coords, spot_other, 2 * (spots % 2) - 1, levels))
    low_bits = [c & 1 for c in own_coords]
    turns = jnp.stack(
        [
            low_bits[others(side // 2)[0]] + 2 * low_bits[others(side // 2)[1]]
            for side in range(6)
        ]
    )
    flip = flip_of(device_id)
    scalars = jnp.concatenate(
        [flip[None], side_near, turns, live.astype(jnp.int32)[None], third_near]
    ).astype(jnp.int32)
    local_ids = device_id * blocks_here + jnp.arange(blocks_here, dtype=jnp.int32)
    home = family_at(local_ids)

    has_children = fine_parent >= 0
    owner = jnp.where(has_children, fine_parent >> 3, -1)
    earlier = device_ids[None, :] < device_ids[:, None]
    rank = jnp.sum(((owner[None, :] == owner[:, None]) & earlier).astype(jnp.int32), axis=1)
    fullest = jnp.max(jnp.where(has_children, rank, 0)) + 1
    empty = jnp.max(jnp.where(jnp.any(owner[None, :] == device_ids[:, None], axis=1), -1, device_ids))
    target_owner = jnp.where(has_children, owner, empty)
    target_rank = jnp.where(has_children, rank, 0)
    before_home = (owner[None, :] == device_id) & (device_ids[None, :] < home[:, None])
    home_rank = jnp.where(home >= 0, jnp.sum(before_home.astype(jnp.int32), axis=1), -1)

    block_shape = coarse_state.shape
    columns = (8, VARS, ROWS, 128)
    passed = (8, VARS, 16, 128)
    packs = (30, 8, 128)
    own = (3 * VARS, 8, 128)

    outgoing = call(
        first_kernel,
        56,
        1,
        [(devices * 6, 2, 128)],
        [(180, 8, 128), block_shape, block_shape],
        device_id[None],
        coarse_state,
        fine_state,
        space=pl.ANY,
        semaphores=2,
    )
    incoming = exchange(outgoing)
    selected = call(select_kernel, 6, 1, [(devices * CHUNKS, 2, 128)], [], first_index, incoming, masks)
    received = exchange(selected)
    fine_next, outgoing = call(
        fine_kernel,
        16,
        1,
        [block_shape, (devices, 2, 128)],
        [columns, columns, passed, (16, VARS, 16, 128), block_shape, (6, 30, 8, 128), packs, packs, packs, own],
        scalars,
        fine_state,
        received,
        tables,
    )
    coarse_new = call(
        coarse_kernel, 12, 1, [block_shape], [columns, columns, passed, packs, own], scalars, coarse_state, received
    )
    incoming = exchange(outgoing)

    def finish(places):
        def branch(incoming, coarse_new, targets, home_rank):
            placed = call(place_kernel, 4, 1, [(devices * places, 2, 128)], [], targets, incoming)
            received = exchange(placed)
            merge = functools.partial(merge_kernel, places=places)
            return call(merge, 6, 1, [block_shape], [], home_rank, coarse_new, received)

        return branch

    sizes = (3, 4, 5, 8)
    choice = sum((fullest > size).astype(jnp.int32) for size in sizes[:-1])
    places_now = sum(jnp.where(choice == number, size, 0) for number, size in enumerate(sizes))
    targets, home_rank = lax.optimization_barrier((target_owner * places_now + target_rank, home_rank))
    coarse_next = lax.switch(
        choice, [finish(size) for size in sizes], incoming, coarse_new, targets, home_rank
    )
    return coarse_next, fine_next


def solution(mesh):
    in_specs = (P(AXES, None, None, None), P(AXES, None, None, None), P())
    out_specs = (P(AXES, None, None, None), P(AXES, None, None, None))
    return jax.shard_map(shards, mesh=mesh, in_specs=in_specs, out_specs=out_specs, check_vma=False)
```

```python
import functools

import jax
import jax.numpy as jnp
import numpy as np
from jax import lax
from jax.experimental import pallas as pl
from jax.experimental.pallas import tpu as pltpu
from jax.sharding import PartitionSpec as P

GAMMA = 1.4
LAMBDA_STEP = 0.08
AXES = ("wide", "narrow")
VARS = 5
SLOTS = 20
CHUNKS = 7
MIB = 1024 * 1024


def lanes_of(shape=(8, 128)):
    return lax.broadcasted_iota(jnp.int32, shape, 1)


def rows_of(shape=(8, 128)):
    return lax.broadcasted_iota(jnp.int32, shape, 0)


def others(axis_id):
    return [other for other in range(3) if other != axis_id]


def cube_block(axis_id, bit, t):
    first, second = others(axis_id)
    return (bit << axis_id) | ((t & 1) << first) | ((t >> 1) << second)


def rolled(values, shift, axis=1):
    shift %= values.shape[axis]
    return pltpu.roll(values, shift, axis) if shift else values


def sheet_cells(axis_id):
    row, lane = np.meshgrid(np.arange(8), np.arange(128), indexing="ij")
    if axis_id == 0:
        t, half = row >> 1, row & 1
        return (t & 1) * 16 + half * 8 + (lane >> 4), (t >> 1) * 16 + (lane & 15)
    if axis_id == 1:
        t, part = lane >> 5, lane >> 4 & 1
        return (t & 1) * 16 + part * 8 + row, (t >> 1) * 16 + (lane & 15)
    t, part, half = lane >> 2 & 3, lane >> 1 & 1, lane & 1
    return (t & 1) * 16 + part * 8 + row, (t >> 1) * 16 + half * 8 + (lane >> 4)


def sheet_tables():
    tables = np.zeros((3, 2, 2, 3, 8, 128), np.int32)
    for axis_id in range(3):
        cells = sheet_cells(axis_id)
        place = np.zeros((32, 32, 2), np.int32)
        for row in range(8):
            for lane in range(128):
                place[cells[0][row, lane], cells[1][row, lane]] = (row, lane)
        for lateral in range(2):
            for up in range(2):
                wanted = list(cells)
                wanted[lateral] = (wanted[lateral] + (1 if up else -1)) % 32
                source = place[wanted[0], wanted[1]]
                rows, lanes = source[..., 0], source[..., 1]
                table = tables[axis_id, lateral, up]
                table[1] = rows
                for lane in range(128):
                    table[0][rows[:, lane], lane] = lanes[:, lane]
                table[2] = cells[lateral] == (0 if up else 31)
    return tables


def pack_side(cells, pack, pack_row, var, axis_id, high, bit, depth=0):
    lanes = lanes_of()
    if axis_id == 0:
        row = 15 - depth if high else depth
        for t in range(4):
            for half in range(2):
                tile = cells(cube_block(0, bit, t), half, var, row, 1)
                pack[pack_row, t * 2 + half : t * 2 + half + 1, :] = tile
        return
    total = jnp.zeros((8, 128), jnp.float32)
    if axis_id == 1:
        offset = 112 - 16 * depth if high else 16 * depth
        for t in range(4):
            for part in range(2):
                group = t * 2 + part
                tile = cells(cube_block(1, bit, t), high, var, part * 8, 8)
                total = jnp.where(lanes >> 4 == group, rolled(tile, group * 16 - offset), total)
    else:
        offset = 15 - depth if high else depth
        for t in range(4):
            for part in range(2):
                for half in range(2):
                    place = t * 4 + part * 2 + half
                    tile = cells(cube_block(2, bit, t), half, var, part * 8, 8)
                    total = jnp.where(lanes & 15 == place, rolled(tile, place - offset), total)
    pack[pack_row] = total


def take(tile, index, axis):
    return jnp.take_along_axis(tile, index, axis=axis, mode="promise_in_bounds")


def inject(tile, axis_id, t):
    lanes, rows = lanes_of(), rows_of()
    if axis_id == 0:
        row_index = 2 * t + (rows >> 1 & 1)
        lane_index = (4 * (rows & 1) + (lanes >> 5)) * 16 + 8 * (rows >> 2 & 1) + (lanes >> 1 & 7)
        return take(take(tile, row_index, 0), lane_index, 1)
    if axis_id == 1:
        part = lanes >> 4 & 1
        lane_index = (2 * t + (lanes >> 5 & 1)) * 16 + 8 * (lanes >> 6 & 1) + (lanes >> 1 & 7)
    else:
        part = lanes >> 1 & 1
        lane_index = (4 * (lanes & 1) + (lanes >> 5)) * 16 + 4 * t + 2 * (lanes >> 2 & 1) + (lanes >> 3 & 1)
    low = take(take(tile, rows >> 1, 0), lane_index, 1)
    high = take(take(tile, 4 + (rows >> 1), 0), lane_index, 1)
    return jnp.where(part == 1, high, low)


ROWS = 48


def primitives(values):
    inverse = 1.0 / values[0]
    squares = values[1] * values[1] + values[2] * values[2] + values[3] * values[3]
    pressure = (GAMMA - 1.0) * (values[4] - 0.5 * squares * inverse)
    return inverse, pressure


def flux_of(values, prims, axis_id):
    inverse, pressure = prims
    velocity = values[1 + axis_id] * inverse
    result = [values[1 + axis_id]]
    for component in range(3):
        term = values[1 + component] * velocity
        result.append(term + pressure if component == axis_id else term)
    result.append((values[4] + pressure) * velocity)
    return result


def face_flux(low, low_flux, high, axis_id):
    high_flux = flux_of(high, primitives(high), axis_id)
    middle = [
        0.5 * (low[v] + high[v]) - 0.5 * LAMBDA_STEP * (high_flux[v] - low_flux[v]) for v in range(VARS)
    ]
    return flux_of(middle, primitives(middle), axis_id)


def column(block, half):
    return (block >> 1) * 2 + half


def cells_of(columns):
    def cells(block, half, var, start, size):
        row = 8 + (block & 1) * 16 + start
        return columns[column(block, half), var, row : row + size, :]

    return cells


def cells_in(blocks, flip):
    def cells(block, half, var, start, size):
        return blocks[block ^ flip, var, start : start + size, half * 128 : half * 128 + 128]

    return cells


def parts_of(tile, shifts):
    return jnp.concatenate([rolled(tile, shift) for shift in shifts], axis=0)


def advance_cube(source, flip, columns, fluxes, passed, own_pack, ghost_pack, emit):
    lanes = lanes_of((16, 128))
    cells = cells_in(source, flip)
    ghost = [[ghost_pack[side * VARS + var] for var in range(VARS)] for side in range(6)]
    for block in range(8):
        row = 8 + (block & 1) * 16
        for half in range(2):
            for var in range(VARS):
                columns[column(block, half), var, row : row + 16, :] = cells(block, half, var, 0, 16)
    lows = []
    for axis_id in range(3):
        for var in range(VARS):
            pack_side(cells, own_pack, axis_id * VARS + var, var, axis_id, 0, 0)
        inner = [own_pack[axis_id * VARS + var] for var in range(VARS)]
        outer = ghost[2 * axis_id]
        lows.append(face_flux(outer, flux_of(outer, primitives(outer), axis_id), inner, axis_id))
    for number in range(8):
        for var in range(VARS):
            columns[number, var, 40:41, :] = ghost[1][var][number : number + 1, :]
            fluxes[number, var, 7:8, :] = lows[0][var][number : number + 1, :]

    def tiles(block, half):
        row = 8 + (block & 1) * 16
        return [columns[column(block, half), var, row : row + 16, :] for var in range(VARS)]

    def places_of(t, half):
        return [t * 4 + part * 2 + half for part in range(2)]

    chains = [(x_bit, z_bit) for z_bit in range(2) for x_bit in range(2)]
    for x_bit, z_bit in chains:
        t = x_bit + 2 * z_bit
        line = [(x_bit | y_bit << 1 | z_bit << 2, half) for y_bit in range(2) for half in range(2)]
        for var in range(VARS):
            turned = [rolled(tiles(*spot)[var], -16) for spot in line]
            turned.append(parts_of(ghost[3][var], [112 - (t * 2 + part) * 16 for part in range(2)]))
            for number, (block, half) in enumerate(line):
                above = jnp.where(lanes >= 112, turned[number + 1], turned[number])
                passed[block * 2 + half, var] = above
                if z_bit:
                    places = places_of(block & 3, half)
                    beyond = parts_of(ghost[5][var], [15 - place for place in places])
                else:
                    beyond = rolled(tiles(block | 4, half)[var], 15)
                own_turned = rolled(tiles(block, half)[var], -1)
                passed[16 + block * 2 + half, var] = jnp.where(lanes & 15 == 15, beyond, own_turned)

    for block in range(8):
        row = 8 + (block & 1) * 16
        for half in range(2):
            here = tiles(block, half)
            prims = primitives(here)
            spot, number = column(block, half), block * 2 + half
            above = [
                [columns[spot, var, row + 1 : row + 17, :] for var in range(VARS)],
                [passed[number, var] for var in range(VARS)],
                [passed[16 + number, var] for var in range(VARS)],
            ]
            faces = [face_flux(here, flux_of(here, prims, k), above[k], k) for k in range(3)]
            for var in range(VARS):
                fluxes[spot, var, row : row + 16, :] = faces[0][var]
                passed[number, var] = faces[1][var]
                passed[16 + number, var] = faces[2][var]

    for x_bit, z_bit in chains:
        t = x_bit + 2 * z_bit
        row = 8 + x_bit * 16
        before = [parts_of(lows[1][var], [-(t * 2 + part) * 16 for part in range(2)]) for var in range(VARS)]
        for y_bit in range(2):
            block = x_bit | y_bit << 1 | z_bit << 2
            for half in range(2):
                spot, number = column(block, half), block * 2 + half
                places = places_of(block & 3, half)
                here = tiles(block, half)
                result = []
                for var in range(VARS):
                    faces = [fluxes[spot, var, row : row + 16, :], passed[number, var], passed[16 + number, var]]
                    change = faces[0] - fluxes[spot, var, row - 1 : row + 15, :]
                    after = rolled(faces[1], 16)
                    change += faces[1] - jnp.where(lanes < 16, before[var], after)
                    before[var] = after
                    if z_bit:
                        behind = rolled(passed[16 + number - 8, var], -15)
                    else:
                        behind = parts_of(lows[2][var], [-place for place in places])
                    change += faces[2] - jnp.where(lanes & 15 == 0, behind, rolled(faces[2], 1))
                    result.append(here[var] - LAMBDA_STEP * change)
                emit(block, half, result)


def pack_all(cells, pack, base, inner, depth=0):
    def one(var, carry):
        for facing in range(6):
            high = facing % 2
            pack_side(cells, pack, base + facing * VARS + var, var, facing // 2, high, high ^ inner, depth)
        return carry

    lax.fori_loop(0, VARS, one, 0)


def spread_packs(pack, base, out, stride, kind):
    def one(number, carry):
        for pair in range(4):
            out[(number * 4 + pair) * stride + kind] = pack[base + number, pair * 2 : pair * 2 + 2, :]
        return carry

    lax.fori_loop(0, 30, one, 0)


def collect_packs(incoming, stride, kind, pack, turned=1):
    def one(var, carry):
        for facing in range(6):
            for pair in range(4):
                chunk = ((facing ^ turned) * SLOTS + var * 4 + pair) * stride + kind
                pack[facing * VARS + var, pair * 2 : pair * 2 + 2, :] = incoming[chunk]
        return carry

    lax.fori_loop(0, VARS, one, 0)


def flip_of(device_id):
    flip = 0
    for level in range(7):
        flip = flip ^ ((device_id >> level & 1) << level % 3)
    return flip


def first_kernel(scalars, coarse_hbm, fine_hbm, out, pack, coarse, fine, arrived):
    flip = flip_of(scalars[0])
    copies = [
        pltpu.make_async_copy(fine_hbm, fine, arrived.at[0]),
        pltpu.make_async_copy(coarse_hbm, coarse, arrived.at[1]),
    ]
    for copy in copies:
        copy.start()
    copies[0].wait()
    for depth in range(2):
        pack_all(cells_in(fine, 0), pack, depth * 30, 0, depth)
        spread_packs(pack, depth * 30, out, 6, depth)
    copies[1].wait()
    for inner in range(2):
        for depth in range(2):
            kind = 2 + 2 * inner + depth
            pack_all(cells_in(coarse, flip), pack, kind * 30, inner, depth)
            spread_packs(pack, kind * 30, out, 6, kind)


def select_kernel(index, incoming, masks, out):
    up = [masks[lateral] > 0 for lateral in range(2)]

    def one(step, carry):
        results = []
        for lane in range(8):
            number = step * 8 + lane
            rows = [incoming[index[number * 9 + column]] for column in range(9)]
            strips = [jnp.where(up[j], rows[4 + 2 * j], rows[3 + 2 * j]) for j in range(2)]
            results.append(rows[:3] + strips + rows[7:])
        for lane in range(8):
            for kind in range(CHUNKS):
                out[(step * 8 + lane) * CHUNKS + kind] = results[lane][kind]
        return carry

    lax.fori_loop(0, out.shape[0] // (8 * CHUNKS), one, 0)


def place_kernel(target, incoming, out):
    def one(step, carry):
        for lane in range(8):
            number = step * 8 + lane
            out[target[number]] = incoming[number]
        return carry

    lax.fori_loop(0, target.shape[0] // 8, one, 0)


def coarse_kernel(scalars, coarse, incoming, coarse_new, columns, fluxes, passed, ghost, own):
    flip = scalars[0]

    def emit(block, half, values):
        for var in range(VARS):
            coarse_new[block ^ flip, var, :, half * 128 : half * 128 + 128] = values[var]

    collect_packs(incoming, CHUNKS, 5, ghost)
    advance_cube(coarse, flip, columns, fluxes, passed, own, ghost, emit)


def sheet_step(facing, here, below, deeper, laterals):
    axis_id = facing // 2
    prims = primitives(here)
    change = [None] * VARS
    pairs = {axis_id: (below, deeper) if facing % 2 else (deeper, below)}
    for lateral, other in enumerate(others(axis_id)):
        pairs[other] = laterals[lateral]
    for along in range(3):
        down, up = pairs[along]
        upper = face_flux(here, flux_of(here, prims, along), up, along)
        lower = face_flux(down, flux_of(down, primitives(down), along), here, along)
        for var in range(VARS):
            term = upper[var] - lower[var]
            change[var] = term if along == 0 else change[var] + term
    return [here[var] - LAMBDA_STEP * change[var] for var in range(VARS)]


def family_ghosts(scalars, fine, tables, packs, old, mid, own):
    coarse_layer, other_layer, second_layer, strip_a, strip_b, parent_layer = packs
    strips = (strip_a, strip_b)
    for facing in range(6):
        axis_id, high = facing // 2, facing % 2
        rows = [facing * VARS + var for var in range(VARS)]
        turn = scalars[7 + facing]

        def moved_sheet(tile, strip, lateral, up):
            tile = jnp.where(tables[axis_id, lateral, up, 2] > 0, strip, tile)
            tile = take(tile, tables[axis_id, lateral, up, 0], 1)
            return take(tile, tables[axis_id, lateral, up, 1], 0)

        @pl.when(scalars[1 + facing] > 0)
        def _():
            for var in range(VARS):
                pack_side(cells_in(fine, 0), own, var, var, axis_id, high, high)
            here = [other_layer[row] for row in rows]
            laterals = []
            for lateral in range(2):
                pair = []
                for up in range(2):
                    known = scalars[14 + facing * 4 + lateral * 2 + up] > 0
                    edge = (tables[axis_id, lateral, 1 - up, 2] > 0) & jnp.logical_not(known)
                    values = []
                    for row in rows:
                        strip = strips[lateral][row]
                        coarse = moved_sheet(coarse_layer[row], strip, lateral, up)
                        fine_value = moved_sheet(other_layer[row], strip, lateral, up)
                        values.append(jnp.where(edge, inject(coarse, axis_id, turn), fine_value))
                    pair.append(values)
                laterals.append(pair)
            deeper = [second_layer[row] for row in rows]
            below = [own[var] for var in range(VARS)]
            result = sheet_step(facing, here, below, deeper, laterals)
            for var in range(VARS):
                old[rows[var]] = here[var]
                mid[rows[var]] = result[var]

        @pl.when(scalars[1 + facing] == 0)
        def _():
            here = [coarse_layer[row] for row in rows]
            laterals = [
                [[moved_sheet(coarse_layer[row], strips[lateral][row], lateral, up) for row in rows] for up in range(2)]
                for lateral in range(2)
            ]
            deeper = [other_layer[row] for row in rows]
            below = [parent_layer[row] for row in rows]
            result = sheet_step(facing, here, below, deeper, laterals)
            for var in range(VARS):
                old[rows[var]] = inject(here[var], axis_id, turn)
                mid[rows[var]] = inject(0.5 * (here[var] + result[var]), axis_id, turn)


def fine_kernel(
    scalars, fine, incoming, tables, fine_next, out, columns, fluxes, passed, new, middle, packs, old, mid, pack, own
):
    lanes = lanes_of()
    for number, kind in enumerate((0, 1, 2, 3, 4, 6)):
        collect_packs(incoming, CHUNKS, kind, packs.at[number], 0 if kind == 6 else 1)
    family_ghosts(scalars, fine, tables, [packs.at[number] for number in range(6)], old, mid, own)
    live = scalars[13] > 0

    def emit_middle(block, half, values):
        for var in range(VARS):
            middle[block, var, :, half * 128 : half * 128 + 128] = values[var]

    def emit(block, half, values):
        for var in range(VARS):
            new[block * 2 + half, var] = values[var]
            fine_next[block, var, :, half * 128 : half * 128 + 128] = jnp.where(live, values[var], 0.0)

    advance_cube(fine, 0, columns, fluxes, passed, own, old, emit_middle)
    advance_cube(middle, 0, columns, fluxes, passed, own, mid, emit)

    source = (lanes >> 4 & 3) * 32 + (lanes & 7) * 2

    def means(var, carry):
        for part in range(2):
            for y_bit in range(2):
                total = jnp.zeros((8, 128), jnp.float32)
                for half in range(2):
                    for z_bit in range(2):
                        number = (part | y_bit << 1 | z_bit << 2) * 2 + half
                        tile = new[number, var, pl.ds(0, 8, 2), :] + new[number, var, pl.ds(1, 8, 2), :]
                        tile = tile + rolled(tile, -1)
                        tile = tile + rolled(tile, -16)
                        tile = take(tile, source, 1) * 0.125
                        wanted = (lanes >> 6 == half) & (lanes >> 3 & 1 == z_bit)
                        total = jnp.where(wanted, tile, total)
                pack[(var * 2 + part) * 2 + y_bit] = total
        return carry

    lax.fori_loop(0, VARS, means, 0)

    def one(number, carry):
        for pair in range(4):
            out[number * 4 + pair] = pack[number, pair * 2 : pair * 2 + 2, :]
        return carry

    lax.fori_loop(0, 20, one, 0)


def merge_kernel(home_rank, coarse_new, incoming, out, *, places):
    out[...] = coarse_new[...]
    for block in range(8):

        @pl.when(home_rank[block] >= 0)
        def _():
            def one(number, carry):
                for part in range(2):
                    for half in range(2):
                        for pair in range(4):
                            chunk = ((number * 2 + part) * 2 + half) * 4 + pair
                            row = part * 8 + pair * 2
                            out[block, number, row : row + 2, half * 128 : half * 128 + 128] = incoming[
                                chunk * places + home_rank[block]
                            ]
                return carry

            lax.fori_loop(0, VARS, one, 0)


def call(kernel, mebibytes, scalar_count, shapes, scratch, *operands, space=pltpu.VMEM, semaphores=0):
    vmem = pl.BlockSpec(memory_space=pltpu.VMEM)
    smem = pl.BlockSpec(memory_space=pltpu.SMEM)
    outs = [jax.ShapeDtypeStruct(shape, jnp.float32) for shape in shapes]
    result = pl.pallas_call(
        kernel,
        out_shape=outs,
        in_specs=[smem] * scalar_count + [pl.BlockSpec(memory_space=space)] * (len(operands) - scalar_count),
        out_specs=[vmem] * len(outs),
        scratch_shapes=[pltpu.VMEM(shape, jnp.float32) for shape in scratch]
        + ([pltpu.SemaphoreType.DMA((semaphores,))] if semaphores else []),
        compiler_params=pltpu.CompilerParams(vmem_limit_bytes=mebibytes * MIB),
    )(*operands)
    return result if len(outs) > 1 else result[0]


def decode(code, levels):
    coords = []
    for axis_id in range(3):
        gray = jnp.zeros_like(code)
        for level in range(axis_id, levels, 3):
            gray = gray | ((code >> level & 1) << level // 3)
        coord = gray
        for shift in range(1, levels):
            coord = coord ^ (gray >> shift)
        coords.append(coord)
    return coords


def encode(coords, levels):
    code = jnp.zeros_like(coords[0])
    for level in range(levels):
        coord = coords[level % 3]
        gray = coord ^ (coord >> 1)
        code = code | ((gray >> level // 3 & 1) << level)
    return code


def extents(levels):
    return [1 << len(range(axis_id, levels, 3)) for axis_id in range(3)]


def moved(coords, axis_id, step, levels):
    sizes = extents(levels)
    return [jnp.where(axis_id == k, (coords[k] + step) & (sizes[k] - 1), coords[k]) for k in range(3)]


def exchange(values):
    return lax.all_to_all(values, AXES, split_axis=0, concat_axis=0, tiled=True)


def shards(coarse_state, fine_state, fine_parent):
    devices = lax.axis_size(AXES)
    device_id = lax.axis_index(AXES).astype(jnp.int32)
    blocks_here = coarse_state.shape[0]
    levels = (blocks_here * devices).bit_length() - 1
    device_levels = levels - 3
    device_ids = jnp.arange(devices, dtype=jnp.int32)

    facing = jnp.minimum(device_id // SLOTS, 5)
    axis_id, high = facing // 2, facing % 2
    step = 1 - 2 * high
    parents = jnp.maximum(fine_parent, 0)
    parent_coords = decode(parents, levels)

    def family_at(blocks):
        match = fine_parent[None, :] == blocks.reshape(-1)[:, None]
        return jnp.max(jnp.where(match, device_ids[None, :], -1), axis=1).reshape(blocks.shape)

    def inner_of(coords):
        along = jnp.where(axis_id == 0, coords[0], jnp.where(axis_id == 1, coords[1], coords[2]))
        return jnp.where((along & 1) == high, 0, 1)

    beside = moved(parent_coords, axis_id, step, levels)
    beside_id = encode(beside, levels)
    near = family_at(beside_id)
    coarse_kind = 2 + 2 * inner_of(beside)
    coarse_index = (beside_id >> 3) * 6 + coarse_kind
    columns_of = [coarse_index, jnp.where(near >= 0, near * 6, coarse_index + 1), jnp.maximum(near, 0) * 6 + 1]
    for lateral in range(2):
        other = jnp.where(axis_id > lateral, lateral, lateral + 1)
        for direction in (-1, 1):
            third_id = encode(moved(beside, other, direction, levels), levels)
            third = family_at(third_id)
            columns_of.append(
                jnp.where((near >= 0) & (third >= 0), third * 6, (third_id >> 3) * 6 + coarse_kind)
            )
    across = encode(moved(decode(device_ids, device_levels), axis_id, step, device_levels), device_levels)
    columns_of += [across * 6 + 2, (parents >> 3) * 6 + 2 + 2 * inner_of(parent_coords)]
    first_index = jnp.stack(columns_of, axis=1).reshape(-1)
    tables = jnp.asarray(sheet_tables())
    pair = (device_id - facing * SLOTS) % 4
    edges = jnp.asarray(sheet_tables()[:, :, 1, 2].reshape(3, 2, 4, 2, 128))
    masks = lax.dynamic_slice(edges, (axis_id, 0, pair, 0, 0), (1, 2, 1, 2, 128)).reshape(2, 2, 128)

    own_parent = lax.dynamic_index_in_dim(fine_parent, device_id, keepdims=False)
    live = own_parent >= 0
    own_coords = decode(jnp.maximum(own_parent, 0), levels)
    sides = jnp.arange(6, dtype=jnp.int32)
    side_coords = moved([jnp.broadcast_to(c, (6,)) for c in own_coords], sides // 2, 2 * (sides % 2) - 1, levels)

    def has_family(coords):
        ids = encode(coords, levels)
        return jnp.any(fine_parent[None, :] == ids[:, None], axis=1).astype(jnp.int32)

    side_near = has_family(side_coords)
    spots = jnp.arange(24, dtype=jnp.int32)
    spot_axis, spot_lateral = spots // 8, spots // 2 % 2
    spot_coords = moved([jnp.broadcast_to(c, (24,)) for c in own_coords], spot_axis, 2 * (spots // 4 % 2) - 1, levels)
    spot_other = jnp.where(spot_axis > spot_lateral, spot_lateral, spot_lateral + 1)
    third_near = has_family(moved(spot_coords, spot_other, 2 * (spots % 2) - 1, levels))
    low_bits = [c & 1 for c in own_coords]
    turns = jnp.stack(
        [
            low_bits[others(side // 2)[0]] + 2 * low_bits[others(side // 2)[1]]
            for side in range(6)
        ]
    )
    flip = flip_of(device_id)
    scalars = jnp.concatenate(
        [flip[None], side_near, turns, live.astype(jnp.int32)[None], third_near]
    ).astype(jnp.int32)
    local_ids = device_id * blocks_here + jnp.arange(blocks_here, dtype=jnp.int32)
    home = family_at(local_ids)

    has_children = fine_parent >= 0
    owner = jnp.where(has_children, fine_parent >> 3, -1)
    earlier = device_ids[None, :] < device_ids[:, None]
    rank = jnp.sum(((owner[None, :] == owner[:, None]) & earlier).astype(jnp.int32), axis=1)
    fullest = jnp.max(jnp.where(has_children, rank, 0)) + 1
    empty = jnp.max(jnp.where(jnp.any(owner[None, :] == device_ids[:, None], axis=1), -1, device_ids))
    target_owner = jnp.where(has_children, owner, empty)
    target_rank = jnp.where(has_children, rank, 0)
    before_home = (owner[None, :] == device_id) & (device_ids[None, :] < home[:, None])
    home_rank = jnp.where(home >= 0, jnp.sum(before_home.astype(jnp.int32), axis=1), -1)

    block_shape = coarse_state.shape
    columns = (8, VARS, ROWS, 128)
    passed = (32, VARS, 16, 128)
    packs = (30, 8, 128)
    own = (3 * VARS, 8, 128)

    outgoing = call(
        first_kernel,
        56,
        1,
        [(devices * 6, 2, 128)],
        [(180, 8, 128), block_shape, block_shape],
        device_id[None],
        coarse_state,
        fine_state,
        space=pl.ANY,
        semaphores=2,
    )
    incoming = exchange(outgoing)
    selected = call(select_kernel, 6, 1, [(devices * CHUNKS, 2, 128)], [], first_index, incoming, masks)
    received = exchange(selected)
    fine_next, outgoing = call(
        fine_kernel,
        16,
        1,
        [block_shape, (devices, 2, 128)],
        [columns, columns, passed, (16, VARS, 16, 128), block_shape, (6, 30, 8, 128), packs, packs, packs, own],
        scalars,
        fine_state,
        received,
        tables,
    )
    coarse_new = call(
        coarse_kernel, 12, 1, [block_shape], [columns, columns, passed, packs, own], scalars, coarse_state, received
    )
    incoming = exchange(outgoing)

    def finish(places):
        def branch(incoming, coarse_new, targets, home_rank):
            placed = call(place_kernel, 4, 1, [(devices * places, 2, 128)], [], targets, incoming)
            received = exchange(placed)
            merge = functools.partial(merge_kernel, places=places)
            return call(merge, 6, 1, [block_shape], [], home_rank, coarse_new, received)

        return branch

    sizes = (3, 4, 5, 8)
    choice = sum((fullest > size).astype(jnp.int32) for size in sizes[:-1])
    places_now = sum(jnp.where(choice == number, size, 0) for number, size in enumerate(sizes))
    targets, home_rank = lax.optimization_barrier((target_owner * places_now + target_rank, home_rank))
    coarse_next = lax.switch(
        choice, [finish(size) for size in sizes], incoming, coarse_new, targets, home_rank
    )
    return coarse_next, fine_next


def solution(mesh):
    in_specs = (P(AXES, None, None, None), P(AXES, None, None, None), P())
    out_specs = (P(AXES, None, None, None), P(AXES, None, None, None))
    return jax.shard_map(shards, mesh=mesh, in_specs=in_specs, out_specs=out_specs, check_vma=False)
```

```python
import functools

import jax
import jax.numpy as jnp
import numpy as np
from jax import lax
from jax.experimental import pallas as pl
from jax.experimental.pallas import tpu as pltpu
from jax.sharding import PartitionSpec as P

GAMMA = 1.4
LAMBDA_STEP = 0.08
AXES = ("wide", "narrow")
VARS = 5
SLOTS = 20
CHUNKS = 7
MIB = 1024 * 1024


def lanes_of(shape=(8, 128)):
    return lax.broadcasted_iota(jnp.int32, shape, 1)


def rows_of(shape=(8, 128)):
    return lax.broadcasted_iota(jnp.int32, shape, 0)


def others(axis_id):
    return [other for other in range(3) if other != axis_id]


def cube_block(axis_id, bit, t):
    first, second = others(axis_id)
    return (bit << axis_id) | ((t & 1) << first) | ((t >> 1) << second)


def rolled(values, shift, axis=1):
    shift %= values.shape[axis]
    return pltpu.roll(values, shift, axis) if shift else values


def sheet_cells(axis_id):
    row, lane = np.meshgrid(np.arange(8), np.arange(128), indexing="ij")
    if axis_id == 0:
        t, half = row >> 1, row & 1
        return (t & 1) * 16 + half * 8 + (lane >> 4), (t >> 1) * 16 + (lane & 15)
    if axis_id == 1:
        t, part = lane >> 5, lane >> 4 & 1
        return (t & 1) * 16 + part * 8 + row, (t >> 1) * 16 + (lane & 15)
    t, part, half = lane >> 2 & 3, lane >> 1 & 1, lane & 1
    return (t & 1) * 16 + part * 8 + row, (t >> 1) * 16 + half * 8 + (lane >> 4)


def sheet_tables():
    tables = np.zeros((3, 2, 2, 3, 8, 128), np.int32)
    for axis_id in range(3):
        cells = sheet_cells(axis_id)
        place = np.zeros((32, 32, 2), np.int32)
        for row in range(8):
            for lane in range(128):
                place[cells[0][row, lane], cells[1][row, lane]] = (row, lane)
        for lateral in range(2):
            for up in range(2):
                wanted = list(cells)
                wanted[lateral] = (wanted[lateral] + (1 if up else -1)) % 32
                source = place[wanted[0], wanted[1]]
                rows, lanes = source[..., 0], source[..., 1]
                table = tables[axis_id, lateral, up]
                table[1] = rows
                for lane in range(128):
                    table[0][rows[:, lane], lane] = lanes[:, lane]
                table[2] = cells[lateral] == (0 if up else 31)
    return tables


def pack_side(cells, pack, pack_row, var, axis_id, high, bit, depth=0):
    lanes = lanes_of()
    if axis_id == 0:
        row = 15 - depth if high else depth
        for t in range(4):
            for half in range(2):
                tile = cells(cube_block(0, bit, t), half, var, row, 1)
                pack[pack_row, t * 2 + half : t * 2 + half + 1, :] = tile
        return
    total = jnp.zeros((8, 128), jnp.float32)
    if axis_id == 1:
        offset = 112 - 16 * depth if high else 16 * depth
        for t in range(4):
            for part in range(2):
                group = t * 2 + part
                tile = cells(cube_block(1, bit, t), high, var, part * 8, 8)
                total = jnp.where(lanes >> 4 == group, rolled(tile, group * 16 - offset), total)
    else:
        offset = 15 - depth if high else depth
        for t in range(4):
            for part in range(2):
                for half in range(2):
                    place = t * 4 + part * 2 + half
                    tile = cells(cube_block(2, bit, t), half, var, part * 8, 8)
                    total = jnp.where(lanes & 15 == place, rolled(tile, place - offset), total)
    pack[pack_row] = total


def take(tile, index, axis):
    return jnp.take_along_axis(tile, index, axis=axis, mode="promise_in_bounds")


def inject(tile, axis_id, t):
    lanes, rows = lanes_of(), rows_of()
    if axis_id == 0:
        row_index = 2 * t + (rows >> 1 & 1)
        lane_index = (4 * (rows & 1) + (lanes >> 5)) * 16 + 8 * (rows >> 2 & 1) + (lanes >> 1 & 7)
        return take(take(tile, row_index, 0), lane_index, 1)
    if axis_id == 1:
        part = lanes >> 4 & 1
        lane_index = (2 * t + (lanes >> 5 & 1)) * 16 + 8 * (lanes >> 6 & 1) + (lanes >> 1 & 7)
    else:
        part = lanes >> 1 & 1
        lane_index = (4 * (lanes & 1) + (lanes >> 5)) * 16 + 4 * t + 2 * (lanes >> 2 & 1) + (lanes >> 3 & 1)
    low = take(take(tile, rows >> 1, 0), lane_index, 1)
    high = take(take(tile, 4 + (rows >> 1), 0), lane_index, 1)
    return jnp.where(part == 1, high, low)


ROWS = 48


def primitives(values):
    inverse = 1.0 / values[0]
    squares = values[1] * values[1] + values[2] * values[2] + values[3] * values[3]
    pressure = (GAMMA - 1.0) * (values[4] - 0.5 * squares * inverse)
    return inverse, pressure


def flux_of(values, prims, axis_id):
    inverse, pressure = prims
    velocity = values[1 + axis_id] * inverse
    result = [values[1 + axis_id]]
    for component in range(3):
        term = values[1 + component] * velocity
        result.append(term + pressure if component == axis_id else term)
    result.append((values[4] + pressure) * velocity)
    return result


def face_flux(low, low_flux, high, axis_id):
    high_flux = flux_of(high, primitives(high), axis_id)
    middle = [
        0.5 * (low[v] + high[v]) - 0.5 * LAMBDA_STEP * (high_flux[v] - low_flux[v]) for v in range(VARS)
    ]
    return flux_of(middle, primitives(middle), axis_id)


def column(block, half):
    return (block >> 1) * 2 + half


def cells_of(columns):
    def cells(block, half, var, start, size):
        row = 8 + (block & 1) * 16 + start
        return columns[column(block, half), var, row : row + size, :]

    return cells


def cells_in(blocks, flip):
    def cells(block, half, var, start, size):
        return blocks[block ^ flip, var, start : start + size, half * 128 : half * 128 + 128]

    return cells


def parts_of(tile, shifts):
    return jnp.concatenate([rolled(tile, shift) for shift in shifts], axis=0)


def advance_cube(source, flip, columns, fluxes, passed, own_pack, ghost_pack, emit):
    lanes = lanes_of((16, 128))
    cells = cells_in(source, flip)
    ghost = [[ghost_pack[side * VARS + var] for var in range(VARS)] for side in range(6)]
    for block in range(8):
        row = 8 + (block & 1) * 16
        for half in range(2):
            for var in range(VARS):
                columns[column(block, half), var, row : row + 16, :] = cells(block, half, var, 0, 16)
    lows = []
    for axis_id in range(3):
        for var in range(VARS):
            pack_side(cells, own_pack, axis_id * VARS + var, var, axis_id, 0, 0)
        inner = [own_pack[axis_id * VARS + var] for var in range(VARS)]
        outer = ghost[2 * axis_id]
        lows.append(face_flux(outer, flux_of(outer, primitives(outer), axis_id), inner, axis_id))
    for number in range(8):
        for var in range(VARS):
            columns[number, var, 40:41, :] = ghost[1][var][number : number + 1, :]
            fluxes[number, var, 7:8, :] = lows[0][var][number : number + 1, :]

    def tiles(block, half):
        row = 8 + (block & 1) * 16
        return [columns[column(block, half), var, row : row + 16, :] for var in range(VARS)]

    def places_of(t, half):
        return [t * 4 + part * 2 + half for part in range(2)]

    chains = [(x_bit, z_bit) for z_bit in range(2) for x_bit in range(2)]
    for x_bit, z_bit in chains:
        t = x_bit + 2 * z_bit
        line = [(x_bit | y_bit << 1 | z_bit << 2, half) for y_bit in range(2) for half in range(2)]
        for var in range(VARS):
            turned = [rolled(tiles(*spot)[var], -16) for spot in line]
            turned.append(parts_of(ghost[3][var], [112 - (t * 2 + part) * 16 for part in range(2)]))
            for number, (block, half) in enumerate(line):
                above = jnp.where(lanes >= 112, turned[number + 1], turned[number])
                passed[block * 2 + half, var] = above
                if z_bit:
                    places = places_of(block & 3, half)
                    beyond = parts_of(ghost[5][var], [15 - place for place in places])
                else:
                    beyond = rolled(tiles(block | 4, half)[var], 15)
                own_turned = rolled(tiles(block, half)[var], -1)
                passed[16 + block * 2 + half, var] = jnp.where(lanes & 15 == 15, beyond, own_turned)

    for block in range(8):
        row = 8 + (block & 1) * 16
        for half in range(2):
            here = tiles(block, half)
            prims = primitives(here)
            spot, number = column(block, half), block * 2 + half
            above = [
                [columns[spot, var, row + 1 : row + 17, :] for var in range(VARS)],
                [passed[number, var] for var in range(VARS)],
                [passed[16 + number, var] for var in range(VARS)],
            ]
            faces = [face_flux(here, flux_of(here, prims, k), above[k], k) for k in range(3)]
            for var in range(VARS):
                fluxes[spot, var, row : row + 16, :] = faces[0][var]
                passed[number, var] = faces[1][var]
                passed[16 + number, var] = faces[2][var]

    for x_bit, z_bit in chains:
        t = x_bit + 2 * z_bit
        row = 8 + x_bit * 16
        before = [parts_of(lows[1][var], [-(t * 2 + part) * 16 for part in range(2)]) for var in range(VARS)]
        for y_bit in range(2):
            block = x_bit | y_bit << 1 | z_bit << 2
            for half in range(2):
                spot, number = column(block, half), block * 2 + half
                places = places_of(block & 3, half)
                here = tiles(block, half)
                result = []
                for var in range(VARS):
                    faces = [fluxes[spot, var, row : row + 16, :], passed[number, var], passed[16 + number, var]]
                    change = faces[0] - fluxes[spot, var, row - 1 : row + 15, :]
                    after = rolled(faces[1], 16)
                    change += faces[1] - jnp.where(lanes < 16, before[var], after)
                    before[var] = after
                    if z_bit:
                        behind = rolled(passed[16 + number - 8, var], -15)
                    else:
                        behind = parts_of(lows[2][var], [-place for place in places])
                    change += faces[2] - jnp.where(lanes & 15 == 0, behind, rolled(faces[2], 1))
                    result.append(here[var] - LAMBDA_STEP * change)
                emit(block, half, result)


def pack_all(cells, pack, base, inner, depth=0):
    def one(var, carry):
        for facing in range(6):
            high = facing % 2
            pack_side(cells, pack, base + facing * VARS + var, var, facing // 2, high, high ^ inner, depth)
        return carry

    lax.fori_loop(0, VARS, one, 0, unroll=True)


def spread_packs(pack, base, out, stride, kind):
    def one(number, carry):
        for pair in range(4):
            out[(number * 4 + pair) * stride + kind] = pack[base + number, pair * 2 : pair * 2 + 2, :]
        return carry

    lax.fori_loop(0, 30, one, 0, unroll=True)


def collect_packs(incoming, stride, kind, pack, turned=1):
    def one(var, carry):
        for facing in range(6):
            for pair in range(4):
                chunk = ((facing ^ turned) * SLOTS + var * 4 + pair) * stride + kind
                pack[facing * VARS + var, pair * 2 : pair * 2 + 2, :] = incoming[chunk]
        return carry

    lax.fori_loop(0, VARS, one, 0)


def flip_of(device_id):
    flip = 0
    for level in range(7):
        flip = flip ^ ((device_id >> level & 1) << level % 3)
    return flip


def first_kernel(scalars, coarse_hbm, fine_hbm, out, pack, coarse, fine, arrived):
    flip = flip_of(scalars[0])
    copies = [
        pltpu.make_async_copy(fine_hbm, fine, arrived.at[0]),
        pltpu.make_async_copy(coarse_hbm, coarse, arrived.at[1]),
    ]
    for copy in copies:
        copy.start()
    copies[0].wait()
    for depth in range(2):
        pack_all(cells_in(fine, 0), pack, depth * 30, 0, depth)
        spread_packs(pack, depth * 30, out, 6, depth)
    copies[1].wait()
    for inner in range(2):
        for depth in range(2):
            kind = 2 + 2 * inner + depth
            pack_all(cells_in(coarse, flip), pack, kind * 30, inner, depth)
            spread_packs(pack, kind * 30, out, 6, kind)


def select_kernel(index, incoming, masks, out):
    up = [masks[lateral] > 0 for lateral in range(2)]

    def one(step, carry):
        results = []
        for lane in range(8):
            number = step * 8 + lane
            rows = [incoming[index[number * 9 + column]] for column in range(9)]
            strips = [jnp.where(up[j], rows[4 + 2 * j], rows[3 + 2 * j]) for j in range(2)]
            results.append(rows[:3] + strips + rows[7:])
        for lane in range(8):
            for kind in range(CHUNKS):
                out[(step * 8 + lane) * CHUNKS + kind] = results[lane][kind]
        return carry

    lax.fori_loop(0, out.shape[0] // (8 * CHUNKS), one, 0)


def place_kernel(target, incoming, out):
    def one(step, carry):
        for lane in range(8):
            number = step * 8 + lane
            out[target[number]] = incoming[number]
        return carry

    lax.fori_loop(0, target.shape[0] // 8, one, 0)


def coarse_kernel(scalars, coarse, incoming, coarse_new, columns, fluxes, passed, ghost, own):
    flip = scalars[0]

    def emit(block, half, values):
        for var in range(VARS):
            coarse_new[block ^ flip, var, :, half * 128 : half * 128 + 128] = values[var]

    collect_packs(incoming, CHUNKS, 5, ghost)
    advance_cube(coarse, flip, columns, fluxes, passed, own, ghost, emit)


def sheet_step(facing, here, below, deeper, laterals):
    axis_id = facing // 2
    prims = primitives(here)
    change = [None] * VARS
    pairs = {axis_id: (below, deeper) if facing % 2 else (deeper, below)}
    for lateral, other in enumerate(others(axis_id)):
        pairs[other] = laterals[lateral]
    for along in range(3):
        down, up = pairs[along]
        upper = face_flux(here, flux_of(here, prims, along), up, along)
        lower = face_flux(down, flux_of(down, primitives(down), along), here, along)
        for var in range(VARS):
            term = upper[var] - lower[var]
            change[var] = term if along == 0 else change[var] + term
    return [here[var] - LAMBDA_STEP * change[var] for var in range(VARS)]


def family_ghosts(scalars, fine, tables, packs, old, mid, own):
    coarse_layer, other_layer, second_layer, strip_a, strip_b, parent_layer = packs
    strips = (strip_a, strip_b)
    for facing in range(6):
        axis_id, high = facing // 2, facing % 2
        rows = [facing * VARS + var for var in range(VARS)]
        turn = scalars[7 + facing]

        def moved_sheet(tile, strip, lateral, up):
            tile = jnp.where(tables[axis_id, lateral, up, 2] > 0, strip, tile)
            tile = take(tile, tables[axis_id, lateral, up, 0], 1)
            return take(tile, tables[axis_id, lateral, up, 1], 0)

        @pl.when(scalars[1 + facing] > 0)
        def _():
            for var in range(VARS):
                pack_side(cells_in(fine, 0), own, var, var, axis_id, high, high)
            here = [other_layer[row] for row in rows]
            laterals = []
            for lateral in range(2):
                pair = []
                for up in range(2):
                    known = scalars[14 + facing * 4 + lateral * 2 + up] > 0
                    edge = (tables[axis_id, lateral, 1 - up, 2] > 0) & jnp.logical_not(known)
                    values = []
                    for row in rows:
                        strip = strips[lateral][row]
                        coarse = moved_sheet(coarse_layer[row], strip, lateral, up)
                        fine_value = moved_sheet(other_layer[row], strip, lateral, up)
                        values.append(jnp.where(edge, inject(coarse, axis_id, turn), fine_value))
                    pair.append(values)
                laterals.append(pair)
            deeper = [second_layer[row] for row in rows]
            below = [own[var] for var in range(VARS)]
            result = sheet_step(facing, here, below, deeper, laterals)
            for var in range(VARS):
                old[rows[var]] = here[var]
                mid[rows[var]] = result[var]

        @pl.when(scalars[1 + facing] == 0)
        def _():
            here = [coarse_layer[row] for row in rows]
            laterals = [
                [[moved_sheet(coarse_layer[row], strips[lateral][row], lateral, up) for row in rows] for up in range(2)]
                for lateral in range(2)
            ]
            deeper = [other_layer[row] for row in rows]
            below = [parent_layer[row] for row in rows]
            result = sheet_step(facing, here, below, deeper, laterals)
            for var in range(VARS):
                old[rows[var]] = inject(here[var], axis_id, turn)
                mid[rows[var]] = inject(0.5 * (here[var] + result[var]), axis_id, turn)


def fine_kernel(
    scalars, fine, incoming, tables, fine_next, out, columns, fluxes, passed, new, middle, packs, old, mid, pack, own
):
    lanes = lanes_of()
    for number, kind in enumerate((0, 1, 2, 3, 4, 6)):
        collect_packs(incoming, CHUNKS, kind, packs.at[number], 0 if kind == 6 else 1)
    family_ghosts(scalars, fine, tables, [packs.at[number] for number in range(6)], old, mid, own)
    live = scalars[13] > 0

    def emit_middle(block, half, values):
        for var in range(VARS):
            middle[block, var, :, half * 128 : half * 128 + 128] = values[var]

    def emit(block, half, values):
        for var in range(VARS):
            new[block * 2 + half, var] = values[var]
            fine_next[block, var, :, half * 128 : half * 128 + 128] = jnp.where(live, values[var], 0.0)

    advance_cube(fine, 0, columns, fluxes, passed, own, old, emit_middle)
    advance_cube(middle, 0, columns, fluxes, passed, own, mid, emit)

    source = (lanes >> 4 & 3) * 32 + (lanes & 7) * 2

    def means(var, carry):
        for part in range(2):
            for y_bit in range(2):
                total = jnp.zeros((8, 128), jnp.float32)
                for half in range(2):
                    for z_bit in range(2):
                        number = (part | y_bit << 1 | z_bit << 2) * 2 + half
                        tile = new[number, var, pl.ds(0, 8, 2), :] + new[number, var, pl.ds(1, 8, 2), :]
                        tile = tile + rolled(tile, -1)
                        tile = tile + rolled(tile, -16)
                        tile = take(tile, source, 1) * 0.125
                        wanted = (lanes >> 6 == half) & (lanes >> 3 & 1 == z_bit)
                        total = jnp.where(wanted, tile, total)
                pack[(var * 2 + part) * 2 + y_bit] = total
        return carry

    lax.fori_loop(0, VARS, means, 0)

    def one(number, carry):
        for pair in range(4):
            out[number * 4 + pair] = pack[number, pair * 2 : pair * 2 + 2, :]
        return carry

    lax.fori_loop(0, 20, one, 0)


def merge_kernel(home_rank, coarse_new, incoming, out, *, places):
    out[...] = coarse_new[...]
    for block in range(8):

        @pl.when(home_rank[block] >= 0)
        def _():
            def one(number, carry):
                for part in range(2):
                    for half in range(2):
                        for pair in range(4):
                            chunk = ((number * 2 + part) * 2 + half) * 4 + pair
                            row = part * 8 + pair * 2
                            out[block, number, row : row + 2, half * 128 : half * 128 + 128] = incoming[
                                chunk * places + home_rank[block]
                            ]
                return carry

            lax.fori_loop(0, VARS, one, 0)


def call(kernel, mebibytes, scalar_count, shapes, scratch, *operands, space=pltpu.VMEM, semaphores=0):
    vmem = pl.BlockSpec(memory_space=pltpu.VMEM)
    smem = pl.BlockSpec(memory_space=pltpu.SMEM)
    outs = [jax.ShapeDtypeStruct(shape, jnp.float32) for shape in shapes]
    result = pl.pallas_call(
        kernel,
        out_shape=outs,
        in_specs=[smem] * scalar_count + [pl.BlockSpec(memory_space=space)] * (len(operands) - scalar_count),
        out_specs=[vmem] * len(outs),
        scratch_shapes=[pltpu.VMEM(shape, jnp.float32) for shape in scratch]
        + ([pltpu.SemaphoreType.DMA((semaphores,))] if semaphores else []),
        compiler_params=pltpu.CompilerParams(vmem_limit_bytes=mebibytes * MIB),
    )(*operands)
    return result if len(outs) > 1 else result[0]


def decode(code, levels):
    coords = []
    for axis_id in range(3):
        gray = jnp.zeros_like(code)
        for level in range(axis_id, levels, 3):
            gray = gray | ((code >> level & 1) << level // 3)
        coord = gray
        for shift in range(1, levels):
            coord = coord ^ (gray >> shift)
        coords.append(coord)
    return coords


def encode(coords, levels):
    code = jnp.zeros_like(coords[0])
    for level in range(levels):
        coord = coords[level % 3]
        gray = coord ^ (coord >> 1)
        code = code | ((gray >> level // 3 & 1) << level)
    return code


def extents(levels):
    return [1 << len(range(axis_id, levels, 3)) for axis_id in range(3)]


def moved(coords, axis_id, step, levels):
    sizes = extents(levels)
    return [jnp.where(axis_id == k, (coords[k] + step) & (sizes[k] - 1), coords[k]) for k in range(3)]


def exchange(values):
    return lax.all_to_all(values, AXES, split_axis=0, concat_axis=0, tiled=True)


def shards(coarse_state, fine_state, fine_parent):
    devices = lax.axis_size(AXES)
    device_id = lax.axis_index(AXES).astype(jnp.int32)
    blocks_here = coarse_state.shape[0]
    levels = (blocks_here * devices).bit_length() - 1
    device_levels = levels - 3
    device_ids = jnp.arange(devices, dtype=jnp.int32)

    facing = jnp.minimum(device_id // SLOTS, 5)
    axis_id, high = facing // 2, facing % 2
    step = 1 - 2 * high
    parents = jnp.maximum(fine_parent, 0)
    parent_coords = decode(parents, levels)

    def family_at(blocks):
        match = fine_parent[None, :] == blocks.reshape(-1)[:, None]
        return jnp.max(jnp.where(match, device_ids[None, :], -1), axis=1).reshape(blocks.shape)

    def inner_of(coords):
        along = jnp.where(axis_id == 0, coords[0], jnp.where(axis_id == 1, coords[1], coords[2]))
        return jnp.where((along & 1) == high, 0, 1)

    beside = moved(parent_coords, axis_id, step, levels)
    beside_id = encode(beside, levels)
    near = family_at(beside_id)
    coarse_kind = 2 + 2 * inner_of(beside)
    coarse_index = (beside_id >> 3) * 6 + coarse_kind
    columns_of = [coarse_index, jnp.where(near >= 0, near * 6, coarse_index + 1), jnp.maximum(near, 0) * 6 + 1]
    for lateral in range(2):
        other = jnp.where(axis_id > lateral, lateral, lateral + 1)
        for direction in (-1, 1):
            third_id = encode(moved(beside, other, direction, levels), levels)
            third = family_at(third_id)
            columns_of.append(
                jnp.where((near >= 0) & (third >= 0), third * 6, (third_id >> 3) * 6 + coarse_kind)
            )
    across = encode(moved(decode(device_ids, device_levels), axis_id, step, device_levels), device_levels)
    columns_of += [across * 6 + 2, (parents >> 3) * 6 + 2 + 2 * inner_of(parent_coords)]
    first_index = jnp.stack(columns_of, axis=1).reshape(-1)
    tables = jnp.asarray(sheet_tables())
    pair = (device_id - facing * SLOTS) % 4
    edges = jnp.asarray(sheet_tables()[:, :, 1, 2].reshape(3, 2, 4, 2, 128))
    masks = lax.dynamic_slice(edges, (axis_id, 0, pair, 0, 0), (1, 2, 1, 2, 128)).reshape(2, 2, 128)

    own_parent = lax.dynamic_index_in_dim(fine_parent, device_id, keepdims=False)
    live = own_parent >= 0
    own_coords = decode(jnp.maximum(own_parent, 0), levels)
    sides = jnp.arange(6, dtype=jnp.int32)
    side_coords = moved([jnp.broadcast_to(c, (6,)) for c in own_coords], sides // 2, 2 * (sides % 2) - 1, levels)

    def has_family(coords):
        ids = encode(coords, levels)
        return jnp.any(fine_parent[None, :] == ids[:, None], axis=1).astype(jnp.int32)

    side_near = has_family(side_coords)
    spots = jnp.arange(24, dtype=jnp.int32)
    spot_axis, spot_lateral = spots // 8, spots // 2 % 2
    spot_coords = moved([jnp.broadcast_to(c, (24,)) for c in own_coords], spot_axis, 2 * (spots // 4 % 2) - 1, levels)
    spot_other = jnp.where(spot_axis > spot_lateral, spot_lateral, spot_lateral + 1)
    third_near = has_family(moved(spot_coords, spot_other, 2 * (spots % 2) - 1, levels))
    low_bits = [c & 1 for c in own_coords]
    turns = jnp.stack(
        [
            low_bits[others(side // 2)[0]] + 2 * low_bits[others(side // 2)[1]]
            for side in range(6)
        ]
    )
    flip = flip_of(device_id)
    scalars = jnp.concatenate(
        [flip[None], side_near, turns, live.astype(jnp.int32)[None], third_near]
    ).astype(jnp.int32)
    local_ids = device_id * blocks_here + jnp.arange(blocks_here, dtype=jnp.int32)
    home = family_at(local_ids)

    has_children = fine_parent >= 0
    owner = jnp.where(has_children, fine_parent >> 3, -1)
    earlier = device_ids[None, :] < device_ids[:, None]
    rank = jnp.sum(((owner[None, :] == owner[:, None]) & earlier).astype(jnp.int32), axis=1)
    fullest = jnp.max(jnp.where(has_children, rank, 0)) + 1
    empty = jnp.max(jnp.where(jnp.any(owner[None, :] == device_ids[:, None], axis=1), -1, device_ids))
    target_owner = jnp.where(has_children, owner, empty)
    target_rank = jnp.where(has_children, rank, 0)
    before_home = (owner[None, :] == device_id) & (device_ids[None, :] < home[:, None])
    home_rank = jnp.where(home >= 0, jnp.sum(before_home.astype(jnp.int32), axis=1), -1)

    block_shape = coarse_state.shape
    columns = (8, VARS, ROWS, 128)
    passed = (32, VARS, 16, 128)
    packs = (30, 8, 128)
    own = (3 * VARS, 8, 128)

    outgoing = call(
        first_kernel,
        56,
        1,
        [(devices * 6, 2, 128)],
        [(180, 8, 128), block_shape, block_shape],
        device_id[None],
        coarse_state,
        fine_state,
        space=pl.ANY,
        semaphores=2,
    )
    incoming = exchange(outgoing)
    selected = call(select_kernel, 6, 1, [(devices * CHUNKS, 2, 128)], [], first_index, incoming, masks)
    received = exchange(selected)
    fine_next, outgoing = call(
        fine_kernel,
        16,
        1,
        [block_shape, (devices, 2, 128)],
        [columns, columns, passed, (16, VARS, 16, 128), block_shape, (6, 30, 8, 128), packs, packs, packs, own],
        scalars,
        fine_state,
        received,
        tables,
    )
    coarse_new = call(
        coarse_kernel, 12, 1, [block_shape], [columns, columns, passed, packs, own], scalars, coarse_state, received
    )
    incoming = exchange(outgoing)

    def finish(places):
        def branch(incoming, coarse_new, targets, home_rank):
            placed = call(place_kernel, 4, 1, [(devices * places, 2, 128)], [], targets, incoming)
            received = exchange(placed)
            merge = functools.partial(merge_kernel, places=places)
            return call(merge, 6, 1, [block_shape], [], home_rank, coarse_new, received)

        return branch

    sizes = (3, 4, 5, 8)
    choice = sum((fullest > size).astype(jnp.int32) for size in sizes[:-1])
    places_now = sum(jnp.where(choice == number, size, 0) for number, size in enumerate(sizes))
    targets, home_rank = lax.optimization_barrier((target_owner * places_now + target_rank, home_rank))
    coarse_next = lax.switch(
        choice, [finish(size) for size in sizes], incoming, coarse_new, targets, home_rank
    )
    return coarse_next, fine_next


def solution(mesh):
    in_specs = (P(AXES, None, None, None), P(AXES, None, None, None), P())
    out_specs = (P(AXES, None, None, None), P(AXES, None, None, None))
    return jax.shard_map(shards, mesh=mesh, in_specs=in_specs, out_specs=out_specs, check_vma=False)
```

```python
import functools

import jax
import jax.numpy as jnp
import numpy as np
from jax import lax
from jax.experimental import pallas as pl
from jax.experimental.pallas import tpu as pltpu
from jax.sharding import PartitionSpec as P

GAMMA = 1.4
LAMBDA_STEP = 0.08
AXES = ("wide", "narrow")
VARS = 5
SLOTS = 20
CHUNKS = 7
MIB = 1024 * 1024


def lanes_of(shape=(8, 128)):
    return lax.broadcasted_iota(jnp.int32, shape, 1)


def rows_of(shape=(8, 128)):
    return lax.broadcasted_iota(jnp.int32, shape, 0)


def others(axis_id):
    return [other for other in range(3) if other != axis_id]


def cube_block(axis_id, bit, t):
    first, second = others(axis_id)
    return (bit << axis_id) | ((t & 1) << first) | ((t >> 1) << second)


def rolled(values, shift, axis=1):
    shift %= values.shape[axis]
    return pltpu.roll(values, shift, axis) if shift else values


def sheet_cells(axis_id):
    row, lane = np.meshgrid(np.arange(8), np.arange(128), indexing="ij")
    if axis_id == 0:
        t, half = row >> 1, row & 1
        return (t & 1) * 16 + half * 8 + (lane >> 4), (t >> 1) * 16 + (lane & 15)
    if axis_id == 1:
        t, part = lane >> 5, lane >> 4 & 1
        return (t & 1) * 16 + part * 8 + row, (t >> 1) * 16 + (lane & 15)
    t, part, half = lane >> 2 & 3, lane >> 1 & 1, lane & 1
    return (t & 1) * 16 + part * 8 + row, (t >> 1) * 16 + half * 8 + (lane >> 4)


def sheet_tables():
    tables = np.zeros((3, 2, 2, 3, 8, 128), np.int32)
    for axis_id in range(3):
        cells = sheet_cells(axis_id)
        place = np.zeros((32, 32, 2), np.int32)
        for row in range(8):
            for lane in range(128):
                place[cells[0][row, lane], cells[1][row, lane]] = (row, lane)
        for lateral in range(2):
            for up in range(2):
                wanted = list(cells)
                wanted[lateral] = (wanted[lateral] + (1 if up else -1)) % 32
                source = place[wanted[0], wanted[1]]
                rows, lanes = source[..., 0], source[..., 1]
                table = tables[axis_id, lateral, up]
                table[1] = rows
                for lane in range(128):
                    table[0][rows[:, lane], lane] = lanes[:, lane]
                table[2] = cells[lateral] == (0 if up else 31)
    return tables


def pack_side(cells, pack, pack_row, var, axis_id, high, bit, depth=0):
    lanes = lanes_of()
    if axis_id == 0:
        row = 15 - depth if high else depth
        for t in range(4):
            for half in range(2):
                tile = cells(cube_block(0, bit, t), half, var, row, 1)
                pack[pack_row, t * 2 + half : t * 2 + half + 1, :] = tile
        return
    total = jnp.zeros((8, 128), jnp.float32)
    if axis_id == 1:
        offset = 112 - 16 * depth if high else 16 * depth
        for t in range(4):
            for part in range(2):
                group = t * 2 + part
                tile = cells(cube_block(1, bit, t), high, var, part * 8, 8)
                total = jnp.where(lanes >> 4 == group, rolled(tile, group * 16 - offset), total)
    else:
        offset = 15 - depth if high else depth
        for t in range(4):
            for part in range(2):
                for half in range(2):
                    place = t * 4 + part * 2 + half
                    tile = cells(cube_block(2, bit, t), half, var, part * 8, 8)
                    total = jnp.where(lanes & 15 == place, rolled(tile, place - offset), total)
    pack[pack_row] = total


def take(tile, index, axis):
    return jnp.take_along_axis(tile, index, axis=axis, mode="promise_in_bounds")


def inject(tile, axis_id, t):
    lanes, rows = lanes_of(), rows_of()
    if axis_id == 0:
        row_index = 2 * t + (rows >> 1 & 1)
        lane_index = (4 * (rows & 1) + (lanes >> 5)) * 16 + 8 * (rows >> 2 & 1) + (lanes >> 1 & 7)
        return take(take(tile, row_index, 0), lane_index, 1)
    if axis_id == 1:
        part = lanes >> 4 & 1
        lane_index = (2 * t + (lanes >> 5 & 1)) * 16 + 8 * (lanes >> 6 & 1) + (lanes >> 1 & 7)
    else:
        part = lanes >> 1 & 1
        lane_index = (4 * (lanes & 1) + (lanes >> 5)) * 16 + 4 * t + 2 * (lanes >> 2 & 1) + (lanes >> 3 & 1)
    low = take(take(tile, rows >> 1, 0), lane_index, 1)
    high = take(take(tile, 4 + (rows >> 1), 0), lane_index, 1)
    return jnp.where(part == 1, high, low)


ROWS = 48


def primitives(values):
    inverse = 1.0 / values[0]
    squares = values[1] * values[1] + values[2] * values[2] + values[3] * values[3]
    pressure = (GAMMA - 1.0) * (values[4] - 0.5 * squares * inverse)
    return inverse, pressure


def flux_of(values, prims, axis_id):
    inverse, pressure = prims
    velocity = values[1 + axis_id] * inverse
    result = [values[1 + axis_id]]
    for component in range(3):
        term = values[1 + component] * velocity
        result.append(term + pressure if component == axis_id else term)
    result.append((values[4] + pressure) * velocity)
    return result


def face_flux(low, low_flux, high, axis_id):
    high_flux = flux_of(high, primitives(high), axis_id)
    middle = [
        0.5 * (low[v] + high[v]) - 0.5 * LAMBDA_STEP * (high_flux[v] - low_flux[v]) for v in range(VARS)
    ]
    return flux_of(middle, primitives(middle), axis_id)


def column(block, half):
    return (block >> 1) * 2 + half


def cells_of(columns):
    def cells(block, half, var, start, size):
        row = 8 + (block & 1) * 16 + start
        return columns[column(block, half), var, row : row + size, :]

    return cells


def cells_in(blocks, flip):
    def cells(block, half, var, start, size):
        return blocks[block ^ flip, var, start : start + size, half * 128 : half * 128 + 128]

    return cells


def parts_of(tile, shifts):
    return jnp.concatenate([rolled(tile, shift) for shift in shifts], axis=0)


def advance_cube(source, flip, columns, fluxes, passed, own_pack, ghost_pack, emit):
    lanes = lanes_of((16, 128))
    cells = cells_in(source, flip)
    ghost = [[ghost_pack[side * VARS + var] for var in range(VARS)] for side in range(6)]
    for block in range(8):
        row = 8 + (block & 1) * 16
        for half in range(2):
            for var in range(VARS):
                columns[column(block, half), var, row : row + 16, :] = cells(block, half, var, 0, 16)
    lows = []
    for axis_id in range(3):
        for var in range(VARS):
            pack_side(cells, own_pack, axis_id * VARS + var, var, axis_id, 0, 0)
        inner = [own_pack[axis_id * VARS + var] for var in range(VARS)]
        outer = ghost[2 * axis_id]
        lows.append(face_flux(outer, flux_of(outer, primitives(outer), axis_id), inner, axis_id))
    for number in range(8):
        for var in range(VARS):
            columns[number, var, 40:41, :] = ghost[1][var][number : number + 1, :]
            fluxes[number, var, 7:8, :] = lows[0][var][number : number + 1, :]

    def tiles(block, half):
        row = 8 + (block & 1) * 16
        return [columns[column(block, half), var, row : row + 16, :] for var in range(VARS)]

    def places_of(t, half):
        return [t * 4 + part * 2 + half for part in range(2)]

    chains = [(x_bit, z_bit) for z_bit in range(2) for x_bit in range(2)]
    for x_bit, z_bit in chains:
        t = x_bit + 2 * z_bit
        line = [(x_bit | y_bit << 1 | z_bit << 2, half) for y_bit in range(2) for half in range(2)]
        for var in range(VARS):
            turned = [rolled(tiles(*spot)[var], -16) for spot in line]
            turned.append(parts_of(ghost[3][var], [112 - (t * 2 + part) * 16 for part in range(2)]))
            for number, (block, half) in enumerate(line):
                above = jnp.where(lanes >= 112, turned[number + 1], turned[number])
                passed[block * 2 + half, var] = above
                if z_bit:
                    places = places_of(block & 3, half)
                    beyond = parts_of(ghost[5][var], [15 - place for place in places])
                else:
                    beyond = rolled(tiles(block | 4, half)[var], 15)
                own_turned = rolled(tiles(block, half)[var], -1)
                passed[16 + block * 2 + half, var] = jnp.where(lanes & 15 == 15, beyond, own_turned)

    for block in range(8):
        row = 8 + (block & 1) * 16
        for half in range(2):
            here = tiles(block, half)
            prims = primitives(here)
            spot, number = column(block, half), block * 2 + half
            above = [
                [columns[spot, var, row + 1 : row + 17, :] for var in range(VARS)],
                [passed[number, var] for var in range(VARS)],
                [passed[16 + number, var] for var in range(VARS)],
            ]
            faces = [face_flux(here, flux_of(here, prims, k), above[k], k) for k in range(3)]
            for var in range(VARS):
                fluxes[spot, var, row : row + 16, :] = faces[0][var]
                passed[number, var] = faces[1][var]
                passed[16 + number, var] = faces[2][var]

    for x_bit, z_bit in chains:
        t = x_bit + 2 * z_bit
        row = 8 + x_bit * 16
        before = [parts_of(lows[1][var], [-(t * 2 + part) * 16 for part in range(2)]) for var in range(VARS)]
        for y_bit in range(2):
            block = x_bit | y_bit << 1 | z_bit << 2
            for half in range(2):
                spot, number = column(block, half), block * 2 + half
                places = places_of(block & 3, half)
                here = tiles(block, half)
                result = []
                for var in range(VARS):
                    faces = [fluxes[spot, var, row : row + 16, :], passed[number, var], passed[16 + number, var]]
                    change = faces[0] - fluxes[spot, var, row - 1 : row + 15, :]
                    after = rolled(faces[1], 16)
                    change += faces[1] - jnp.where(lanes < 16, before[var], after)
                    before[var] = after
                    if z_bit:
                        behind = rolled(passed[16 + number - 8, var], -15)
                    else:
                        behind = parts_of(lows[2][var], [-place for place in places])
                    change += faces[2] - jnp.where(lanes & 15 == 0, behind, rolled(faces[2], 1))
                    result.append(here[var] - LAMBDA_STEP * change)
                emit(block, half, result)


def pack_all(cells, pack, base, inner, depth=0):
    def one(var, carry):
        for facing in range(6):
            high = facing % 2
            pack_side(cells, pack, base + facing * VARS + var, var, facing // 2, high, high ^ inner, depth)
        return carry

    lax.fori_loop(0, VARS, one, 0, unroll=True)


def spread_packs(pack, base, out, stride, kind):
    def one(number, carry):
        for pair in range(4):
            out[(number * 4 + pair) * stride + kind] = pack[base + number, pair * 2 : pair * 2 + 2, :]
        return carry

    lax.fori_loop(0, 30, one, 0, unroll=True)


def collect_packs(incoming, stride, kind, pack, turned=1):
    def one(var, carry):
        for facing in range(6):
            for pair in range(4):
                chunk = ((facing ^ turned) * SLOTS + var * 4 + pair) * stride + kind
                pack[facing * VARS + var, pair * 2 : pair * 2 + 2, :] = incoming[chunk]
        return carry

    lax.fori_loop(0, VARS, one, 0, unroll=True)


def flip_of(device_id):
    flip = 0
    for level in range(7):
        flip = flip ^ ((device_id >> level & 1) << level % 3)
    return flip


def first_kernel(scalars, coarse_hbm, fine_hbm, out, pack, coarse, fine, arrived):
    flip = flip_of(scalars[0])
    copies = [
        pltpu.make_async_copy(fine_hbm, fine, arrived.at[0]),
        pltpu.make_async_copy(coarse_hbm, coarse, arrived.at[1]),
    ]
    for copy in copies:
        copy.start()
    copies[0].wait()
    for depth in range(2):
        pack_all(cells_in(fine, 0), pack, depth * 30, 0, depth)
        spread_packs(pack, depth * 30, out, 6, depth)
    copies[1].wait()
    for inner in range(2):
        for depth in range(2):
            kind = 2 + 2 * inner + depth
            pack_all(cells_in(coarse, flip), pack, kind * 30, inner, depth)
            spread_packs(pack, kind * 30, out, 6, kind)


def select_kernel(index, incoming, masks, out):
    up = [masks[lateral] > 0 for lateral in range(2)]

    def one(step, carry):
        results = []
        for lane in range(8):
            number = step * 8 + lane
            rows = [incoming[index[number * 9 + column]] for column in range(9)]
            strips = [jnp.where(up[j], rows[4 + 2 * j], rows[3 + 2 * j]) for j in range(2)]
            results.append(rows[:3] + strips + rows[7:])
        for lane in range(8):
            for kind in range(CHUNKS):
                out[(step * 8 + lane) * CHUNKS + kind] = results[lane][kind]
        return carry

    lax.fori_loop(0, out.shape[0] // (8 * CHUNKS), one, 0, unroll=2)


def place_kernel(target, incoming, out):
    def one(step, carry):
        for lane in range(8):
            number = step * 8 + lane
            out[target[number]] = incoming[number]
        return carry

    lax.fori_loop(0, target.shape[0] // 8, one, 0)


def coarse_kernel(scalars, coarse, incoming, coarse_new, columns, fluxes, passed, ghost, own):
    flip = scalars[0]

    def emit(block, half, values):
        for var in range(VARS):
            coarse_new[block ^ flip, var, :, half * 128 : half * 128 + 128] = values[var]

    collect_packs(incoming, CHUNKS, 5, ghost)
    advance_cube(coarse, flip, columns, fluxes, passed, own, ghost, emit)


def sheet_step(facing, here, below, deeper, laterals):
    axis_id = facing // 2
    prims = primitives(here)
    change = [None] * VARS
    pairs = {axis_id: (below, deeper) if facing % 2 else (deeper, below)}
    for lateral, other in enumerate(others(axis_id)):
        pairs[other] = laterals[lateral]
    for along in range(3):
        down, up = pairs[along]
        upper = face_flux(here, flux_of(here, prims, along), up, along)
        lower = face_flux(down, flux_of(down, primitives(down), along), here, along)
        for var in range(VARS):
            term = upper[var] - lower[var]
            change[var] = term if along == 0 else change[var] + term
    return [here[var] - LAMBDA_STEP * change[var] for var in range(VARS)]


def family_ghosts(scalars, fine, tables, packs, old, mid, own):
    coarse_layer, other_layer, second_layer, strip_a, strip_b, parent_layer = packs
    strips = (strip_a, strip_b)
    for facing in range(6):
        axis_id, high = facing // 2, facing % 2
        rows = [facing * VARS + var for var in range(VARS)]
        turn = scalars[7 + facing]

        def moved_sheet(tile, strip, lateral, up):
            tile = jnp.where(tables[axis_id, lateral, up, 2] > 0, strip, tile)
            tile = take(tile, tables[axis_id, lateral, up, 0], 1)
            return take(tile, tables[axis_id, lateral, up, 1], 0)

        @pl.when(scalars[1 + facing] > 0)
        def _():
            for var in range(VARS):
                pack_side(cells_in(fine, 0), own, var, var, axis_id, high, high)
            here = [other_layer[row] for row in rows]
            laterals = []
            for lateral in range(2):
                pair = []
                for up in range(2):
                    known = scalars[14 + facing * 4 + lateral * 2 + up] > 0
                    edge = (tables[axis_id, lateral, 1 - up, 2] > 0) & jnp.logical_not(known)
                    values = []
                    for row in rows:
                        strip = strips[lateral][row]
                        coarse = moved_sheet(coarse_layer[row], strip, lateral, up)
                        fine_value = moved_sheet(other_layer[row], strip, lateral, up)
                        values.append(jnp.where(edge, inject(coarse, axis_id, turn), fine_value))
                    pair.append(values)
                laterals.append(pair)
            deeper = [second_layer[row] for row in rows]
            below = [own[var] for var in range(VARS)]
            result = sheet_step(facing, here, below, deeper, laterals)
            for var in range(VARS):
                old[rows[var]] = here[var]
                mid[rows[var]] = result[var]

        @pl.when(scalars[1 + facing] == 0)
        def _():
            here = [coarse_layer[row] for row in rows]
            laterals = [
                [[moved_sheet(coarse_layer[row], strips[lateral][row], lateral, up) for row in rows] for up in range(2)]
                for lateral in range(2)
            ]
            deeper = [other_layer[row] for row in rows]
            below = [parent_layer[row] for row in rows]
            result = sheet_step(facing, here, below, deeper, laterals)
            for var in range(VARS):
                old[rows[var]] = inject(here[var], axis_id, turn)
                mid[rows[var]] = inject(0.5 * (here[var] + result[var]), axis_id, turn)


def fine_kernel(
    scalars, fine, incoming, tables, fine_next, out, columns, fluxes, passed, new, middle, packs, old, mid, pack, own
):
    lanes = lanes_of()
    for number, kind in enumerate((0, 1, 2, 3, 4, 6)):
        collect_packs(incoming, CHUNKS, kind, packs.at[number], 0 if kind == 6 else 1)
    family_ghosts(scalars, fine, tables, [packs.at[number] for number in range(6)], old, mid, own)
    live = scalars[13] > 0

    def emit_middle(block, half, values):
        for var in range(VARS):
            middle[block, var, :, half * 128 : half * 128 + 128] = values[var]

    def emit(block, half, values):
        for var in range(VARS):
            new[block * 2 + half, var] = values[var]
            fine_next[block, var, :, half * 128 : half * 128 + 128] = jnp.where(live, values[var], 0.0)

    advance_cube(fine, 0, columns, fluxes, passed, own, old, emit_middle)
    advance_cube(middle, 0, columns, fluxes, passed, own, mid, emit)

    source = (lanes >> 4 & 3) * 32 + (lanes & 7) * 2

    def means(var, carry):
        for part in range(2):
            for y_bit in range(2):
                total = jnp.zeros((8, 128), jnp.float32)
                for half in range(2):
                    for z_bit in range(2):
                        number = (part | y_bit << 1 | z_bit << 2) * 2 + half
                        tile = new[number, var, pl.ds(0, 8, 2), :] + new[number, var, pl.ds(1, 8, 2), :]
                        tile = tile + rolled(tile, -1)
                        tile = tile + rolled(tile, -16)
                        tile = take(tile, source, 1) * 0.125
                        wanted = (lanes >> 6 == half) & (lanes >> 3 & 1 == z_bit)
                        total = jnp.where(wanted, tile, total)
                pack[(var * 2 + part) * 2 + y_bit] = total
        return carry

    lax.fori_loop(0, VARS, means, 0)

    def one(number, carry):
        for pair in range(4):
            out[number * 4 + pair] = pack[number, pair * 2 : pair * 2 + 2, :]
        return carry

    lax.fori_loop(0, 20, one, 0)


def merge_kernel(home_rank, coarse_new, incoming, out, *, places):
    out[...] = coarse_new[...]
    for block in range(8):

        @pl.when(home_rank[block] >= 0)
        def _():
            def one(number, carry):
                for part in range(2):
                    for half in range(2):
                        for pair in range(4):
                            chunk = ((number * 2 + part) * 2 + half) * 4 + pair
                            row = part * 8 + pair * 2
                            out[block, number, row : row + 2, half * 128 : half * 128 + 128] = incoming[
                                chunk * places + home_rank[block]
                            ]
                return carry

            lax.fori_loop(0, VARS, one, 0)


def call(kernel, mebibytes, scalar_count, shapes, scratch, *operands, space=pltpu.VMEM, semaphores=0):
    vmem = pl.BlockSpec(memory_space=pltpu.VMEM)
    smem = pl.BlockSpec(memory_space=pltpu.SMEM)
    outs = [jax.ShapeDtypeStruct(shape, jnp.float32) for shape in shapes]
    result = pl.pallas_call(
        kernel,
        out_shape=outs,
        in_specs=[smem] * scalar_count + [pl.BlockSpec(memory_space=space)] * (len(operands) - scalar_count),
        out_specs=[vmem] * len(outs),
        scratch_shapes=[pltpu.VMEM(shape, jnp.float32) for shape in scratch]
        + ([pltpu.SemaphoreType.DMA((semaphores,))] if semaphores else []),
        compiler_params=pltpu.CompilerParams(vmem_limit_bytes=mebibytes * MIB),
    )(*operands)
    return result if len(outs) > 1 else result[0]


def decode(code, levels):
    coords = []
    for axis_id in range(3):
        gray = jnp.zeros_like(code)
        for level in range(axis_id, levels, 3):
            gray = gray | ((code >> level & 1) << level // 3)
        coord = gray
        for shift in range(1, levels):
            coord = coord ^ (gray >> shift)
        coords.append(coord)
    return coords


def encode(coords, levels):
    code = jnp.zeros_like(coords[0])
    for level in range(levels):
        coord = coords[level % 3]
        gray = coord ^ (coord >> 1)
        code = code | ((gray >> level // 3 & 1) << level)
    return code


def extents(levels):
    return [1 << len(range(axis_id, levels, 3)) for axis_id in range(3)]


def moved(coords, axis_id, step, levels):
    sizes = extents(levels)
    return [jnp.where(axis_id == k, (coords[k] + step) & (sizes[k] - 1), coords[k]) for k in range(3)]


def exchange(values):
    return lax.all_to_all(values, AXES, split_axis=0, concat_axis=0, tiled=True)


def shards(coarse_state, fine_state, fine_parent):
    devices = lax.axis_size(AXES)
    device_id = lax.axis_index(AXES).astype(jnp.int32)
    blocks_here = coarse_state.shape[0]
    levels = (blocks_here * devices).bit_length() - 1
    device_levels = levels - 3
    device_ids = jnp.arange(devices, dtype=jnp.int32)

    facing = jnp.minimum(device_id // SLOTS, 5)
    axis_id, high = facing // 2, facing % 2
    step = 1 - 2 * high
    parents = jnp.maximum(fine_parent, 0)
    parent_coords = decode(parents, levels)

    def family_at(blocks):
        match = fine_parent[None, :] == blocks.reshape(-1)[:, None]
        return jnp.max(jnp.where(match, device_ids[None, :], -1), axis=1).reshape(blocks.shape)

    def inner_of(coords):
        along = jnp.where(axis_id == 0, coords[0], jnp.where(axis_id == 1, coords[1], coords[2]))
        return jnp.where((along & 1) == high, 0, 1)

    beside = moved(parent_coords, axis_id, step, levels)
    beside_id = encode(beside, levels)
    near = family_at(beside_id)
    coarse_kind = 2 + 2 * inner_of(beside)
    coarse_index = (beside_id >> 3) * 6 + coarse_kind
    columns_of = [coarse_index, jnp.where(near >= 0, near * 6, coarse_index + 1), jnp.maximum(near, 0) * 6 + 1]
    for lateral in range(2):
        other = jnp.where(axis_id > lateral, lateral, lateral + 1)
        for direction in (-1, 1):
            third_id = encode(moved(beside, other, direction, levels), levels)
            third = family_at(third_id)
            columns_of.append(
                jnp.where((near >= 0) & (third >= 0), third * 6, (third_id >> 3) * 6 + coarse_kind)
            )
    across = encode(moved(decode(device_ids, device_levels), axis_id, step, device_levels), device_levels)
    columns_of += [across * 6 + 2, (parents >> 3) * 6 + 2 + 2 * inner_of(parent_coords)]
    first_index = jnp.stack(columns_of, axis=1).reshape(-1)
    tables = jnp.asarray(sheet_tables())
    pair = (device_id - facing * SLOTS) % 4
    edges = jnp.asarray(sheet_tables()[:, :, 1, 2].reshape(3, 2, 4, 2, 128))
    masks = lax.dynamic_slice(edges, (axis_id, 0, pair, 0, 0), (1, 2, 1, 2, 128)).reshape(2, 2, 128)

    own_parent = lax.dynamic_index_in_dim(fine_parent, device_id, keepdims=False)
    live = own_parent >= 0
    own_coords = decode(jnp.maximum(own_parent, 0), levels)
    sides = jnp.arange(6, dtype=jnp.int32)
    side_coords = moved([jnp.broadcast_to(c, (6,)) for c in own_coords], sides // 2, 2 * (sides % 2) - 1, levels)

    def has_family(coords):
        ids = encode(coords, levels)
        return jnp.any(fine_parent[None, :] == ids[:, None], axis=1).astype(jnp.int32)

    side_near = has_family(side_coords)
    spots = jnp.arange(24, dtype=jnp.int32)
    spot_axis, spot_lateral = spots // 8, spots // 2 % 2
    spot_coords = moved([jnp.broadcast_to(c, (24,)) for c in own_coords], spot_axis, 2 * (spots // 4 % 2) - 1, levels)
    spot_other = jnp.where(spot_axis > spot_lateral, spot_lateral, spot_lateral + 1)
    third_near = has_family(moved(spot_coords, spot_other, 2 * (spots % 2) - 1, levels))
    low_bits = [c & 1 for c in own_coords]
    turns = jnp.stack(
        [
            low_bits[others(side // 2)[0]] + 2 * low_bits[others(side // 2)[1]]
            for side in range(6)
        ]
    )
    flip = flip_of(device_id)
    scalars = jnp.concatenate(
        [flip[None], side_near, turns, live.astype(jnp.int32)[None], third_near]
    ).astype(jnp.int32)
    local_ids = device_id * blocks_here + jnp.arange(blocks_here, dtype=jnp.int32)
    home = family_at(local_ids)

    has_children = fine_parent >= 0
    owner = jnp.where(has_children, fine_parent >> 3, -1)
    earlier = device_ids[None, :] < device_ids[:, None]
    rank = jnp.sum(((owner[None, :] == owner[:, None]) & earlier).astype(jnp.int32), axis=1)
    fullest = jnp.max(jnp.where(has_children, rank, 0)) + 1
    empty = jnp.max(jnp.where(jnp.any(owner[None, :] == device_ids[:, None], axis=1), -1, device_ids))
    target_owner = jnp.where(has_children, owner, empty)
    target_rank = jnp.where(has_children, rank, 0)
    before_home = (owner[None, :] == device_id) & (device_ids[None, :] < home[:, None])
    home_rank = jnp.where(home >= 0, jnp.sum(before_home.astype(jnp.int32), axis=1), -1)

    block_shape = coarse_state.shape
    columns = (8, VARS, ROWS, 128)
    passed = (32, VARS, 16, 128)
    packs = (30, 8, 128)
    own = (3 * VARS, 8, 128)

    outgoing = call(
        first_kernel,
        56,
        1,
        [(devices * 6, 2, 128)],
        [(180, 8, 128), block_shape, block_shape],
        device_id[None],
        coarse_state,
        fine_state,
        space=pl.ANY,
        semaphores=2,
    )
    incoming = exchange(outgoing)
    selected = call(select_kernel, 6, 1, [(devices * CHUNKS, 2, 128)], [], first_index, incoming, masks)
    received = exchange(selected)
    fine_next, outgoing = call(
        fine_kernel,
        16,
        1,
        [block_shape, (devices, 2, 128)],
        [columns, columns, passed, (16, VARS, 16, 128), block_shape, (6, 30, 8, 128), packs, packs, packs, own],
        scalars,
        fine_state,
        received,
        tables,
    )
    coarse_new = call(
        coarse_kernel, 12, 1, [block_shape], [columns, columns, passed, packs, own], scalars, coarse_state, received
    )
    incoming = exchange(outgoing)

    def finish(places):
        def branch(incoming, coarse_new, targets, home_rank):
            placed = call(place_kernel, 4, 1, [(devices * places, 2, 128)], [], targets, incoming)
            received = exchange(placed)
            merge = functools.partial(merge_kernel, places=places)
            return call(merge, 6, 1, [block_shape], [], home_rank, coarse_new, received)

        return branch

    sizes = (3, 4, 5, 8)
    choice = sum((fullest > size).astype(jnp.int32) for size in sizes[:-1])
    places_now = sum(jnp.where(choice == number, size, 0) for number, size in enumerate(sizes))
    targets, home_rank = lax.optimization_barrier((target_owner * places_now + target_rank, home_rank))
    coarse_next = lax.switch(
        choice, [finish(size) for size in sizes], incoming, coarse_new, targets, home_rank
    )
    return coarse_next, fine_next


def solution(mesh):
    in_specs = (P(AXES, None, None, None), P(AXES, None, None, None), P())
    out_specs = (P(AXES, None, None, None), P(AXES, None, None, None))
    return jax.shard_map(shards, mesh=mesh, in_specs=in_specs, out_specs=out_specs, check_vma=False)
```
